512 devices in a mesh: space: 128 (over z, y, core), lead: 4 (over x).
Axes of the slice: x: 4, y: 4, z: 16, core: 2. Of those that a mesh axis runs over, the one named last changes fastest.
Arguments:
- tiles: bfloat16 [128, 16, 32, 256], P('space'), may hold values from -6 to 6
- station_obs: bfloat16 [32768, 128], P('space'), may hold values from -6 to 6
- station_tile: int32 [32768, 1], P('space'), may hold values from 0 to 127; in each aligned block of 256 rows (0 to 255, 256 to 511, ...) at most 4 rows name the same one
- station_pixel: int32 [32768], P('space'), may hold values from 0 to 511
- station_embed: bfloat16 [128, 256], replicated, may hold values from -0.5 to 0.5
- conv_fine: bfloat16 [3, 3, 256, 256], replicated, may hold values from -0.125 to 0.125
- conv_mid: bfloat16 [3, 3, 256, 256], replicated, may hold values from -0.125 to 0.125
- conv_coarse: bfloat16 [3, 3, 256, 256], replicated, may hold values from -0.125 to 0.125
- norm_gains: bfloat16 [4, 256], replicated, may hold values from 0.099609375 to 1.8984375
- film_table: bfloat16 [720, 512], P('lead'), may hold values from -3 to 3
- horizon_step_list: int32 [4], replicated, may hold values from 0 to 719
- out_proj: bfloat16 [256, 256], replicated, may hold values from -0.375 to 0.375
- gauge_bin_projector: bfloat16 [256, 256], replicated, may hold values from -0.375 to 0.375
Outputs:
- horizon_feature_maps: bfloat16 [4, 128, 16, 32, 256], P('lead', 'space')
- gauge_horizon_scores: bfloat16 [4, 32768, 256], P('lead', 'space')
The draws below stay inside these ranges and needn't reach their ends.
Inputs may be any that keep to these rules, and one draw needn't show every extreme that they name: `station_tile`: among the 256 stations of one index of space no tile is named more than 4 times, a bound that some block reaches; every tile is named by some station.
All inputs are finite; a program needn't handle non-finite values.
Results may differ from the reference program's by a relative error of at most 0.015.
Values may be sent and summed in bfloat16 or wider, within the bound.
No kernel may reach another device: no remote copies, remote signals or barrier semaphores. Data moves between devices by JAX's collectives and lax.ppermute only.
A program may use at most 64 MiB of HBM per device.

```python
import math
import jax
import jax.numpy as jnp
import numpy as np
from jax import lax

FEATURE_DEPTH = 256
STF = 128
OUTCOME_BINS = 256
HORIZON_EMBEDDED = 720
TILE_COLS = 8
PATCH_HEIGHT = 16
PATCH_WIDTH = 32
STA_DEV = 256
PATCH_TOTAL = 128
GAUGE_SITES = 32768
HORIZON_STEPS = 4
CAP = 4
N_SPACE = 128


def place_ends(values, stream_key, smallest, largest):
    dims = values.shape
    index_at = [jax.random.randint(jax.random.fold_in(stream_key, axis), (), 0, dims[axis]) for axis in range(len(dims))]
    values = values.at[tuple(index_at)].set(smallest)
    longest = dims.index(max(dims))
    index_at[longest] = (index_at[longest] + 1) % dims[longest]
    return values.at[tuple(index_at)].set(largest)


def levels(key, shape, cuts, low, top_value):
    level, own = 1.0, jax.random.fold_in(key, 6)
    for position, blocks in cuts:
        draws = jnp.exp(jax.random.uniform(jax.random.fold_in(own, position), (blocks,), jnp.float32, low / len(cuts), top_value / len(cuts)))
        level = level * jnp.repeat(draws, shape[position] // blocks).reshape([-1 if axis == position else 1 for axis in range(len(shape))])
    return level


def shared_out(key, own, number, rows, number_of, top, most, skew):
    ranking = jax.random.permutation(key, number_of)
    packed, common = portions_of(number_of, rows * top, most, skew, True), portions_of(number_of, rows * top, most, skew, False)
    places = jnp.arange(number_of)

    def named(sizes, turn):
        used = int((sizes > 0).sum())
        fixed = max(1, used // 4)
        passed = fixed + (places - fixed + turn * (used - fixed)) % max(1, number_of - fixed)
        return jnp.zeros((number_of,), jnp.int32).at[ranking[jnp.where(places < fixed, places, passed)]].set(jnp.asarray(sizes, jnp.int32))

    sizes = jnp.where(number % 4 == 0, named(packed, number // 4), named(common, number - number // 4 - 1))
    mixed = jax.random.permutation(jax.random.fold_in(own, 3), number_of)
    donor, sink = mixed[0:number_of // 2 * 2:2], mixed[1:number_of // 2 * 2:2]
    room = jnp.minimum(sizes[donor] - 1, most - sizes[sink]) // 2
    room = jnp.where((donor == ranking[0]) | (sink == ranking[0]) | (sizes[sink] == 0), 0, jnp.maximum(room, 0))
    passed = jax.random.randint(jax.random.fold_in(own, 4), (number_of // 2,), 0, 1 << 20) % (room + 1)
    sizes = sizes.at[donor].add(-passed).at[sink].add(passed)
    members = jnp.searchsorted(jnp.cumsum(sizes), jnp.arange(rows * top), side="right").astype(jnp.int32)
    table = members.reshape(top, rows).T
    table = table[jax.random.permutation(jax.random.fold_in(own, 1), rows)]
    turn = jax.random.randint(jax.random.fold_in(own, 2), (rows, 1), 0, top)
    return jnp.take_along_axis(table, (jnp.arange(top)[None, :] + turn) % top, axis=1)


def portions_of(amount, total, limit, skew, full):
    weights = [(1 << 20) // math.isqrt(rank ** skew) + 1 for rank in range(1, amount + 1)]
    largest = limit if full else min(limit, max(-(-total // amount), total * weights[0] // sum(weights)))
    least = 1 if total - largest >= amount - 1 else 0
    given, rest = [largest] + [least] * (amount - 1), total - largest - least * (amount - 1)
    while rest > 0:
        movable = [i for i in range(1, amount) if given[i] < largest] or [i for i in range(1, amount) if given[i] < limit]
        whole, budget = sum([weights[i] for i in movable]), rest
        for i in movable:
            addition = min(limit - given[i], max(1, budget * weights[i] // whole), rest)
            given[i] = given[i] + addition
            rest = rest - addition
    return np.array(given)


def normal_values(stream_key, shape, spread, most, shards=(), held_as=jnp.bfloat16):
    values = jax.random.normal(stream_key, shape, jnp.float32) * spread
    if len(shards) > 0:
        values = levels(stream_key, shape, shards, -0.22, 0.18) * values
    return jnp.clip(values, min=-most, max=most).astype(held_as)


def setup_inputs(seed: int = 0) -> dict:
    streams_of = jax.random.split(jax.random.key(seed), 14)
    tiles = normal_values(streams_of[0], (PATCH_TOTAL, PATCH_HEIGHT, PATCH_WIDTH, FEATURE_DEPTH), 1.0, 6.0, ((0, 128),))
    station_obs = normal_values(streams_of[1], (GAUGE_SITES, STF), 1.0, 6.0, ((0, 128),))
    station_tile_keys = jax.random.split(jax.random.fold_in(streams_of[2], 1), GAUGE_SITES // STA_DEV)
    station_tile_turns = jax.random.permutation(jax.random.fold_in(streams_of[2], 3), GAUGE_SITES // STA_DEV)
    station_tile = jax.vmap(lambda own, number: shared_out(jax.random.fold_in(streams_of[2], 2), own, number, STA_DEV, N_SPACE, 1, CAP, 2))(station_tile_keys, station_tile_turns).reshape((GAUGE_SITES, 1))
    station_pixel = place_ends(jax.random.randint(streams_of[3], (GAUGE_SITES,), 0, PATCH_HEIGHT * PATCH_WIDTH), jax.random.fold_in(streams_of[3], 1), 0, (PATCH_HEIGHT * PATCH_WIDTH) - 1).astype(jnp.int32)
    station_embed = normal_values(streams_of[4], (STF, FEATURE_DEPTH), STF ** -0.5, 0.5)
    conv_fine = normal_values(streams_of[5], (3, 3, FEATURE_DEPTH, FEATURE_DEPTH), (9 * FEATURE_DEPTH) ** -0.5, 0.125)
    conv_mid = normal_values(streams_of[6], (3, 3, FEATURE_DEPTH, FEATURE_DEPTH), (9 * FEATURE_DEPTH) ** -0.5, 0.125)
    conv_coarse = normal_values(streams_of[7], (3, 3, FEATURE_DEPTH, FEATURE_DEPTH), (9 * FEATURE_DEPTH) ** -0.5, 0.125)
    norm_gains = jnp.clip(1.0 + 0.18 * jax.random.normal(streams_of[8], (4, FEATURE_DEPTH), jnp.float32), 0.099609375, 1.8984375).astype(jnp.bfloat16)
    film_table = normal_values(streams_of[9], (HORIZON_EMBEDDED, 2 * FEATURE_DEPTH), 0.5, 3.0, ((0, 4),))
    horizon_step_list = place_ends(jax.random.randint(streams_of[10], (HORIZON_STEPS,), 0, HORIZON_EMBEDDED), jax.random.fold_in(streams_of[10], 1), 0, HORIZON_EMBEDDED - 1).astype(jnp.int32)
    out_proj = normal_values(streams_of[11], (FEATURE_DEPTH, FEATURE_DEPTH), FEATURE_DEPTH ** -0.5, 0.375)
    gauge_bin_projector = normal_values(streams_of[12], (FEATURE_DEPTH, OUTCOME_BINS), FEATURE_DEPTH ** -0.5, 0.375)
    return dict(tiles=tiles, station_obs=station_obs, station_tile=station_tile, station_pixel=station_pixel, station_embed=station_embed, conv_fine=conv_fine, conv_mid=conv_mid, conv_coarse=conv_coarse, norm_gains=norm_gains, film_table=film_table, horizon_step_list=horizon_step_list, out_proj=out_proj, gauge_bin_projector=gauge_bin_projector)


EPS = 1e-06

def rms_scale(values, gain):
    mean_sq = lax.optimization_barrier(jnp.mean(values * values, axis=-1, keepdims=True))
    return values * lax.rsqrt(mean_sq + EPS) * gain.astype(jnp.float32)

def conv_same(picture, weight):
    result = lax.conv_general_dilated(picture.astype(jnp.float32)[None], weight.astype(jnp.float32), (1, 1), 'SAME', dimension_numbers=('NHWC', 'HWIO', 'NHWC'), precision=lax.Precision.HIGHEST)
    return result[0]

def pool_four(picture):
    height, width, feature_depth = picture.shape
    return lax.optimization_barrier(jnp.mean(picture.reshape(height // 4, 4, width // 4, 4, feature_depth), axis=(1, 3)))

def spread_four(picture):
    return jnp.repeat(jnp.repeat(picture, 4, axis=0), 4, axis=1)

def to_image(tile_stack):
    tile_rows = PATCH_TOTAL // TILE_COLS
    grid = tile_stack.reshape(tile_rows, TILE_COLS, PATCH_HEIGHT, PATCH_WIDTH, FEATURE_DEPTH)
    return grid.transpose(0, 2, 1, 3, 4).reshape(tile_rows * PATCH_HEIGHT, TILE_COLS * PATCH_WIDTH, FEATURE_DEPTH)

def to_tiles(picture):
    tile_rows = PATCH_TOTAL // TILE_COLS
    grid = picture.reshape(tile_rows, PATCH_HEIGHT, TILE_COLS, PATCH_WIDTH, FEATURE_DEPTH)
    return grid.transpose(0, 2, 1, 3, 4).reshape(PATCH_TOTAL, PATCH_HEIGHT, PATCH_WIDTH, FEATURE_DEPTH)

def reference(tiles, station_obs, station_tile, station_pixel, station_embed, conv_fine, conv_mid, conv_coarse, norm_gains, film_table, horizon_step_list, out_proj, gauge_bin_projector):
    embedded = jnp.dot(station_obs, station_embed, preferred_element_type=jnp.float32).astype(jnp.bfloat16)
    linear_cell_index = (station_tile[:, 0] * (PATCH_HEIGHT * PATCH_WIDTH) + station_pixel).astype(jnp.int32)
    inject = jnp.zeros((PATCH_TOTAL * PATCH_HEIGHT * PATCH_WIDTH, FEATURE_DEPTH), jnp.float32).at[linear_cell_index].add(embedded.astype(jnp.float32))
    tiled_input = tiles.astype(jnp.float32) + inject.reshape(PATCH_TOTAL, PATCH_HEIGHT, PATCH_WIDTH, FEATURE_DEPTH)
    fine_in = to_image(tiled_input)
    normed = rms_scale(fine_in, norm_gains[0]).astype(jnp.bfloat16)
    enc_fine = (fine_in + jax.nn.silu(conv_same(normed, conv_fine))).astype(jnp.bfloat16)
    mid_in = pool_four(enc_fine.astype(jnp.float32))
    mid_normed = rms_scale(mid_in, norm_gains[1]).astype(jnp.bfloat16)
    enc_mid = mid_in + jax.nn.silu(conv_same(mid_normed, conv_mid))
    coarse_in = pool_four(enc_mid)
    coarse_normed = rms_scale(coarse_in, norm_gains[2]).astype(jnp.bfloat16)
    context = coarse_in + jax.nn.silu(conv_same(coarse_normed, conv_coarse))
    merged = enc_fine.astype(jnp.float32) + spread_four(enc_mid + spread_four(context))
    affine_shift_entries = film_table[horizon_step_list].astype(jnp.float32)
    normed_out = rms_scale(merged, norm_gains[3])

    def unet_upsampling_path(lead_film):
        decoded = jax.nn.silu(normed_out * (1.0 + lead_film[:FEATURE_DEPTH]) + lead_film[FEATURE_DEPTH:]).astype(jnp.bfloat16)
        mixed = jnp.dot(decoded.reshape(-1, FEATURE_DEPTH), out_proj, preferred_element_type=jnp.float32)
        result = (merged + mixed.reshape(merged.shape)).astype(jnp.bfloat16)
        return to_tiles(result)
    horizon_feature_maps = lax.map(unet_upsampling_path, affine_shift_entries)
    gathered_entries = horizon_feature_maps.reshape(HORIZON_STEPS, PATCH_TOTAL * PATCH_HEIGHT * PATCH_WIDTH, FEATURE_DEPTH)[:, linear_cell_index]
    unnormalised_scores = jnp.dot(gathered_entries.reshape(HORIZON_STEPS * GAUGE_SITES, FEATURE_DEPTH), gauge_bin_projector, preferred_element_type=jnp.float32)
    gauge_horizon_scores = unnormalised_scores.astype(jnp.bfloat16).reshape(HORIZON_STEPS, GAUGE_SITES, OUTCOME_BINS)
    return (horizon_feature_maps, gauge_horizon_scores)
```

```python
import jax
import jax.numpy as jnp
from jax import lax
from jax.sharding import PartitionSpec as P

TILE_COLS = 8
EPS = 1e-06
HALO = 5
F32 = jnp.float32
BF16 = jnp.bfloat16


def rms_scale(values, gain):
    mean_sq = jnp.mean(values * values, axis=-1, keepdims=True)
    return values * lax.rsqrt(mean_sq + EPS) * gain


def conv3(picture, weight, padding):
    return lax.conv_general_dilated(
        picture[None],
        weight,
        (1, 1),
        padding,
        dimension_numbers=("NHWC", "HWIO", "NHWC"),
        preferred_element_type=F32,
    )[0]


def pool_four(picture):
    height, width, depth = picture.shape
    return jnp.mean(picture.reshape(height // 4, 4, width // 4, 4, depth), axis=(1, 3))


def spread(picture, times):
    return jnp.repeat(jnp.repeat(picture, times, axis=0), times, axis=1)


def shifted(value, row_step, col_step):
    count = lax.axis_size("space")
    pairs = []
    for source in range(count):
        row, col = source // TILE_COLS + row_step, source % TILE_COLS + col_step
        if 0 <= row < count // TILE_COLS and 0 <= col < TILE_COLS:
            pairs.append((source, row * TILE_COLS + col))
    return lax.ppermute(value, "space", pairs)


def body(
    tiles,
    station_obs,
    station_tile,
    station_pixel,
    station_embed,
    conv_fine,
    conv_mid,
    conv_coarse,
    norm_gains,
    film_table,
    horizon_step_list,
    out_proj,
    gauge_bin_projector,
):
    space_count = lax.axis_size("space")
    tile_rows, tile_cols, depth = tiles.shape[1:]
    cells = tile_rows * tile_cols
    count, readings = station_obs.shape
    gains = norm_gains.astype(F32)
    space_at = lax.axis_index("space")
    row_at, col_at = space_at // TILE_COLS, space_at % TILE_COLS

    table_rows = film_table.shape[0]
    own_rows = lax.axis_index("lead") * table_rows + jnp.arange(table_rows, dtype=jnp.int32)
    lead_hot = (horizon_step_list[:, None] == own_rows[None, :]).astype(BF16)
    film_part = jnp.dot(lead_hot, film_table, preferred_element_type=F32).astype(BF16)
    film_parts = lax.all_gather(film_part, "lead")

    dest = station_tile[:, 0]
    dest_hot = (dest[None, :] == jnp.arange(space_count, dtype=jnp.int32)[:, None]).astype(BF16)
    order = jnp.arange(count, dtype=jnp.int32)
    earlier = (order[:, None] < order[None, :]).astype(BF16)
    prior = jnp.dot(dest_hot, earlier, preferred_element_type=F32)
    position = jnp.sum(prior * dest_hot.astype(F32), axis=0).astype(jnp.int32)
    key = dest * 2 + position % 2 + 2 * space_count * (position // 2)
    slot_rows = jnp.arange(2 * space_count, dtype=jnp.int32)
    first = key[None, :] == slot_rows[:, None]
    second = key[None, :] == slot_rows[:, None] + 2 * space_count
    match = jnp.concatenate([first, second], axis=1).astype(BF16)
    high = (station_pixel // 16).astype(BF16)[:, None]
    low = (station_pixel % 16).astype(BF16)[:, None]
    blank = jnp.zeros((count, readings), BF16)
    zero_two = jnp.zeros((count, 2), BF16)
    tail = jnp.zeros((count, readings - 4), BF16)
    records = jnp.concatenate(
        [
            jnp.concatenate([station_obs, blank, high, low, zero_two, tail], axis=1),
            jnp.concatenate([blank, station_obs, zero_two, high, low, tail], axis=1),
        ],
        axis=0,
    )
    payload = jnp.dot(match, records, preferred_element_type=F32).astype(BF16)
    arrived = lax.all_to_all(
        payload.reshape(space_count, 2, 3 * readings), "space", 0, 0, tiled=True
    ).reshape(2 * space_count, 3 * readings)
    embedded = jnp.dot(
        jnp.concatenate([arrived[:, :readings], arrived[:, readings : 2 * readings]], axis=0),
        station_embed,
        preferred_element_type=F32,
    ).astype(BF16)
    places = arrived[:, 2 * readings : 2 * readings + 4].astype(F32)
    pixel = jnp.concatenate(
        [places[:, 0] * 16 + places[:, 1], places[:, 2] * 16 + places[:, 3]], axis=0
    ).astype(jnp.int32)
    pixel_hot = (pixel[:, None] == jnp.arange(cells, dtype=jnp.int32)[None, :]).astype(BF16)
    inject = jnp.einsum("kp,kc->pc", pixel_hot, embedded, preferred_element_type=F32)
    fine_own = tiles[0].astype(F32) + inject.reshape(tile_rows, tile_cols, depth)

    rim = fine_own.astype(BF16)
    west = shifted(rim[:, -HALO:], 0, 1)
    east = shifted(rim[:, :HALO], 0, -1)
    wide = jnp.concatenate([west, rim, east], axis=1)
    north = shifted(wide[-HALO:], 1, 0)
    south = shifted(wide[:HALO], -1, 0)
    middle = jnp.concatenate([west.astype(F32), fine_own, east.astype(F32)], axis=1)
    fine_in = jnp.concatenate([north.astype(F32), middle, south.astype(F32)], axis=0)

    normed = rms_scale(fine_in, gains[0]).astype(BF16)
    enc_fine = (
        fine_in[1:-1, 1:-1] + jax.nn.silu(conv3(normed, conv_fine, "VALID"))
    ).astype(BF16)
    mid_in = pool_four(enc_fine.astype(F32))
    mid_rows = row_at * (tile_rows // 4) - 1 + jnp.arange(mid_in.shape[0], dtype=jnp.int32)
    mid_cols = col_at * (tile_cols // 4) - 1 + jnp.arange(mid_in.shape[1], dtype=jnp.int32)
    last_row = space_count // TILE_COLS * (tile_rows // 4)
    last_col = TILE_COLS * (tile_cols // 4)
    inside = ((mid_rows >= 0) & (mid_rows < last_row))[:, None, None] & (
        (mid_cols >= 0) & (mid_cols < last_col)
    )[None, :, None]
    mid_normed = jnp.where(inside, rms_scale(mid_in, gains[1]), 0.0).astype(BF16)
    enc_mid = mid_in[1:-1, 1:-1] + jax.nn.silu(conv3(mid_normed, conv_mid, "VALID"))
    coarse_own = pool_four(enc_mid)
    partial = enc_fine[4:-4, 4:-4].astype(F32) + spread(enc_mid, 4)

    found = jnp.dot(
        pixel_hot, partial.astype(BF16).reshape(cells, depth), preferred_element_type=F32
    ).astype(BF16)
    found = jnp.concatenate(
        [
            found[: 2 * space_count].reshape(space_count, 2, depth),
            found[2 * space_count :].reshape(space_count, 2, depth),
        ],
        axis=1,
    )
    coarse_rows = coarse_own.astype(BF16).reshape(1, 4, depth // 2)
    parcel = jnp.concatenate(
        [found, jnp.broadcast_to(coarse_rows, (space_count, 4, depth // 2))], axis=2
    )
    returned = lax.all_to_all(parcel, "space", 0, 0, tiled=True)

    grid_rows, grid_cols = space_count // TILE_COLS, TILE_COLS * 2
    coarse_in = returned[:, :, depth:].reshape(grid_rows, grid_cols, depth).astype(F32)
    coarse_normed = rms_scale(coarse_in, gains[2]).astype(BF16)
    context = coarse_in + jax.nn.silu(conv3(coarse_normed, conv_coarse, "SAME"))
    context_own = lax.dynamic_slice(context, (row_at, col_at * 2, 0), (1, 2, depth))
    merged = partial + spread(context_own, 16)

    film = jnp.sum(film_parts.astype(F32), axis=0)
    film = lax.dynamic_slice_in_dim(film, lax.axis_index("lead"), 1, 0)
    scale_row, shift_row = film[0, :depth], film[0, depth:]

    def decode(values):
        hidden = rms_scale(values, gains[3]) * (1.0 + scale_row) + shift_row
        mixed = jnp.dot(
            jax.nn.silu(hidden).astype(BF16), out_proj, preferred_element_type=F32
        )
        return (values + mixed).astype(BF16)

    maps = decode(merged.reshape(cells, depth))

    slot = dest * 4 + position
    coarse_at = (dest // TILE_COLS) * grid_cols + (dest % TILE_COLS) * 2 + (station_pixel % 32) // 16
    slot_hot = slot[:, None] == jnp.arange(4 * space_count, dtype=jnp.int32)[None, :]
    coarse_hot = coarse_at[:, None] == jnp.arange(grid_rows * grid_cols, dtype=jnp.int32)[None, :]
    pick = jnp.concatenate([slot_hot, coarse_hot], axis=1).astype(BF16)
    sources = jnp.concatenate(
        [
            returned[:, :, :depth].reshape(4 * space_count, depth),
            context.astype(BF16).reshape(grid_rows * grid_cols, depth),
        ],
        axis=0,
    )
    at_stations = decode(jnp.dot(pick, sources, preferred_element_type=F32))
    scores = jnp.dot(at_stations, gauge_bin_projector, preferred_element_type=F32).astype(BF16)
    return (
        maps.reshape(1, 1, tile_rows, tile_cols, depth),
        scores.reshape(1, count, -1),
    )


def solution(mesh):
    in_specs = (
        P("space", None, None, None),
        P("space", None),
        P("space", None),
        P("space"),
        P(),
        P(),
        P(),
        P(),
        P(),
        P("lead", None),
        P(),
        P(),
        P(),
    )
    out_specs = (P("lead", "space", None, None, None), P("lead", "space", None))
    return jax.shard_map(body, mesh=mesh, in_specs=in_specs, out_specs=out_specs, check_vma=False)
```

```python
import jax
import jax.numpy as jnp
import numpy as np
from jax import lax
from jax.experimental import pallas as pl
from jax.experimental.pallas import tpu as pltpu
from jax.sharding import PartitionSpec as P

TILE_COLS = 8
TILE_H, TILE_W, DEPTH = 16, 32, 256
CELLS = TILE_H * TILE_W
EPS = 1e-06
HALO = 5
SIDE = 8
FRAME_H, FRAME_W = TILE_H + 2 * HALO, TILE_W + 2 * SIDE
ENC_H = FRAME_H - 2
BAND = 8
MID_W = 16
F32 = jnp.float32
BF16 = jnp.bfloat16


def dot(a, b):
    return jnp.dot(a, b, preferred_element_type=F32)


def dot_wide(a, b):
    high = b.astype(BF16)
    return dot(a, high) + dot(a, (b - high.astype(F32)).astype(BF16))


def silu(v):
    return v / (1.0 + jnp.exp(-v))


def rms_scale(values, gain):
    mean_sq = jnp.mean(values * values, axis=-1, keepdims=True)
    return values * lax.rsqrt(mean_sq + EPS) * gain


def pool_fine_matrix():
    q = np.arange(BAND * FRAME_W)
    y, x = q // FRAME_W, q % FRAME_W
    rows = np.arange(BAND // 4 * MID_W)
    hit = (y // 4 == rows[:, None] // MID_W) & (x // 4 - 1 == rows[:, None] % MID_W)
    return jnp.asarray(hit & (rows[:, None] % MID_W < 10), BF16) / 16


def spread_mid_matrix():
    q = np.arange(CELLS)
    at = q // TILE_W // 4 * MID_W + q % TILE_W // 4 + 1
    return jnp.asarray(at[:, None] == np.arange(4 * MID_W)[None, :], BF16)


def pool_mid_matrix():
    x = np.arange(4 * MID_W) % MID_W - 1
    rows = np.arange(16)
    return jnp.asarray((x >= 0) & (x < 8) & (x // 4 == rows[:, None]), BF16) / 16


def trunk_kernel(
    place, north, south, west, east, own, conv_fine, conv_mid, gains,
    pool_fine, spread_mid, pool_mid, pixel_hot,
    partial_ref, found_ref, coarse_ref,
    frame, taps, enc, mid_in, mid_taps,
):
    frame[:HALO] = north[...].astype(F32)
    frame[HALO + TILE_H :] = south[...].astype(F32)
    frame[HALO : HALO + TILE_H, :SIDE] = west[...].astype(F32)
    frame[HALO : HALO + TILE_H, SIDE : SIDE + TILE_W] = own[...]
    frame[HALO : HALO + TILE_H, SIDE + TILE_W :] = east[...].astype(F32)
    gain = gains[0:1].astype(F32)
    for y in range(FRAME_H):
        normed = rms_scale(frame[y], gain)
        rows = slice(y * FRAME_W, (y + 1) * FRAME_W)
        taps[rows, :DEPTH] = pltpu.roll(normed, 1, 0).astype(BF16)
        taps[rows, DEPTH : 2 * DEPTH] = normed.astype(BF16)
        taps[rows, 2 * DEPTH :] = pltpu.roll(normed, FRAME_W - 1, 0).astype(BF16)
    size = BAND * FRAME_W
    mid_size = BAND // 4 * MID_W
    for band in range(ENC_H // BAND):
        first = band * BAND
        conv = 0.0
        for dy in range(3):
            start = (first + dy) * FRAME_W
            conv += dot(taps[start : start + size], conv_fine[dy])
        rows = frame[first + 1 : first + 1 + BAND].reshape(size, DEPTH)
        done = (rows + silu(conv)).astype(BF16)
        enc[first : first + BAND] = done.astype(F32).reshape(BAND, FRAME_W, DEPTH)
        mid_in[band * mid_size : (band + 1) * mid_size] = dot(pool_fine[...], done)

    mid = mid_in[...]
    normed = rms_scale(mid, gains[1:2].astype(F32))
    at = lax.broadcasted_iota(jnp.int32, mid.shape, 0)
    row = place[0] * (TILE_H // 4) - 1 + at // MID_W
    col = place[1] * (TILE_W // 4) - 1 + at % MID_W
    inside = (row >= 0) & (row < place[2] * (TILE_H // 4))
    inside = inside & (col >= 0) & (col < TILE_COLS * (TILE_W // 4))
    normed = jnp.where(inside, normed, 0.0)
    mid_taps[:, :DEPTH] = pltpu.roll(normed, 1, 0).astype(BF16)
    mid_taps[:, DEPTH : 2 * DEPTH] = normed.astype(BF16)
    mid_taps[:, 2 * DEPTH :] = pltpu.roll(normed, mid.shape[0] - 1, 0).astype(BF16)
    conv = 0.0
    for dy in range(3):
        conv += dot(mid_taps[dy * MID_W : (dy + 4) * MID_W], conv_mid[dy])
    enc_mid = mid[MID_W : 5 * MID_W] + silu(conv)
    coarse_ref[...] = dot_wide(pool_mid[...], enc_mid).astype(BF16)
    centre = enc[HALO - 1 : HALO - 1 + TILE_H, SIDE : SIDE + TILE_W]
    partial = centre.reshape(CELLS, DEPTH) + dot_wide(spread_mid[...], enc_mid)
    partial_ref[...] = partial
    found_ref[...] = dot(pixel_hot[...], partial.astype(BF16)).astype(BF16)


def tail_kernel(
    place, slots, coarse_in, conv_coarse, gains, partial, film, pick, out_proj, projector,
    maps_ref, scores_ref,
    taps,
):
    cells, wide = coarse_in.shape[0], TILE_COLS * 2
    coarse = coarse_in[...].astype(F32)
    normed = rms_scale(coarse, gains[2:3].astype(F32))
    col = lax.broadcasted_iota(jnp.int32, coarse.shape, 0) % wide
    taps[:wide] = jnp.zeros((wide, 3 * DEPTH), BF16)
    taps[wide + cells :] = jnp.zeros((wide, 3 * DEPTH), BF16)
    inner = slice(wide, wide + cells)
    left, right = pltpu.roll(normed, 1, 0), pltpu.roll(normed, cells - 1, 0)
    taps[inner, :DEPTH] = jnp.where(col == 0, 0.0, left).astype(BF16)
    taps[inner, DEPTH : 2 * DEPTH] = normed.astype(BF16)
    taps[inner, 2 * DEPTH :] = jnp.where(col == wide - 1, 0.0, right).astype(BF16)
    conv = 0.0
    for dy in range(3):
        conv += dot(taps[dy * wide : dy * wide + cells], conv_coarse[dy])
    context = coarse + silu(conv)
    high = context.astype(BF16)
    low = (context - high.astype(F32)).astype(BF16)

    gain = gains[3:4].astype(F32)
    scale, shift = 1.0 + film[0:1], film[1:2]

    def decode(values):
        hidden = rms_scale(values, gain) * scale + shift
        return (values + dot(silu(hidden).astype(BF16), out_proj[...])).astype(BF16)

    at = lax.broadcasted_iota(jnp.int32, (CELLS, cells), 0)
    here = place[0] * wide + place[1] * 2 + (at % TILE_W) // (TILE_W // 2)
    mine = (lax.broadcasted_iota(jnp.int32, (CELLS, cells), 1) == here).astype(F32).astype(BF16)
    maps_ref[...] = decode(partial[...] + (dot(mine, high) + dot(mine, low)))

    count = slots.shape[0]
    at_stations = dot(pick[:, :count], slots[...])
    at_stations += dot(pick[:, count:], high) + dot(pick[:, count:], low)
    scores_ref[...] = dot(decode(at_stations), projector[...]).astype(BF16)


def call(kernel, outs, scratch, operands):
    vmem = pl.BlockSpec(memory_space=pltpu.VMEM)
    smem = pl.BlockSpec(memory_space=pltpu.SMEM)
    return pl.pallas_call(
        kernel,
        out_shape=outs,
        in_specs=[smem] + [vmem] * (len(operands) - 1),
        out_specs=[vmem] * len(outs),
        scratch_shapes=[pltpu.VMEM(shape, dtype) for shape, dtype in scratch],
        compiler_params=pltpu.CompilerParams(vmem_limit_bytes=32 * 2**20),
    )(*operands)


def trunk(place, north, south, west, east, own, conv_fine, conv_mid, gains, pixel_hot):
    slot_count = pixel_hot.shape[0]
    return call(
        trunk_kernel,
        [
            jax.ShapeDtypeStruct((CELLS, DEPTH), F32),
            jax.ShapeDtypeStruct((slot_count, DEPTH), BF16),
            jax.ShapeDtypeStruct((16, DEPTH), BF16),
        ],
        [
            ((FRAME_H, FRAME_W, DEPTH), F32),
            ((FRAME_H * FRAME_W, 3 * DEPTH), BF16),
            ((ENC_H, FRAME_W, DEPTH), F32),
            ((ENC_H // 4 * MID_W, DEPTH), F32),
            ((ENC_H // 4 * MID_W, 3 * DEPTH), BF16),
        ],
        [
            place, north, south, west, east, own,
            conv_fine.reshape(3, 3 * DEPTH, DEPTH),
            conv_mid.reshape(3, 3 * DEPTH, DEPTH),
            gains, pool_fine_matrix(), spread_mid_matrix(), pool_mid_matrix(), pixel_hot,
        ],
    )


def tail(place, slots, coarse_in, conv_coarse, gains, partial, film, pick, out_proj, projector):
    cells = coarse_in.shape[0]
    return call(
        tail_kernel,
        [
            jax.ShapeDtypeStruct((CELLS, DEPTH), BF16),
            jax.ShapeDtypeStruct((pick.shape[0], projector.shape[1]), BF16),
        ],
        [((cells + 4 * TILE_COLS, 3 * DEPTH), BF16)],
        [
            place, slots, coarse_in, conv_coarse.reshape(3, 3 * DEPTH, DEPTH), gains,
            partial, film, pick, out_proj, projector,
        ],
    )


def shifted(value, row_step, col_step):
    count = lax.axis_size("space")
    pairs = []
    for source in range(count):
        row, col = source // TILE_COLS + row_step, source % TILE_COLS + col_step
        if 0 <= row < count // TILE_COLS and 0 <= col < TILE_COLS:
            pairs.append((source, row * TILE_COLS + col))
    return lax.ppermute(value, "space", pairs)


def body(
    tiles,
    station_obs,
    station_tile,
    station_pixel,
    station_embed,
    conv_fine,
    conv_mid,
    conv_coarse,
    norm_gains,
    film_table,
    horizon_step_list,
    out_proj,
    gauge_bin_projector,
):
    space_count = lax.axis_size("space")
    count, readings = station_obs.shape
    space_at = lax.axis_index("space")
    place = jnp.stack(
        [space_at // TILE_COLS, space_at % TILE_COLS, jnp.int32(space_count // TILE_COLS)]
    ).astype(jnp.int32)

    table_rows = film_table.shape[0]
    own_rows = lax.axis_index("lead") * table_rows + jnp.arange(table_rows, dtype=jnp.int32)
    lead_hot = (horizon_step_list[:, None] == own_rows[None, :]).astype(BF16)
    film_parts = lax.all_gather(dot(lead_hot, film_table).astype(BF16), "lead")
    film = jnp.sum(film_parts.astype(F32), axis=0)
    film = lax.dynamic_slice_in_dim(film, lax.axis_index("lead"), 1, 0).reshape(2, DEPTH)

    dest = station_tile[:, 0]
    dest_hot = (dest[None, :] == jnp.arange(space_count, dtype=jnp.int32)[:, None]).astype(BF16)
    order = jnp.arange(count, dtype=jnp.int32)
    earlier = (order[:, None] < order[None, :]).astype(BF16)
    prior = dot(dest_hot, earlier)
    position = jnp.sum(prior * dest_hot.astype(F32), axis=0).astype(jnp.int32)
    half, pair = position % 2, position // 2
    key = dest * 2 + half + 2 * space_count * pair
    slot_rows = jnp.arange(2 * space_count, dtype=jnp.int32)
    first = key[None, :] == slot_rows[:, None]
    second = key[None, :] == slot_rows[:, None] + 2 * space_count
    match = jnp.concatenate([first, second], axis=1).astype(BF16)
    high = (station_pixel // 16).astype(BF16)[:, None]
    low = (station_pixel % 16).astype(BF16)[:, None]
    blank = jnp.zeros((count, readings), BF16)
    zero_two = jnp.zeros((count, 2), BF16)
    rest = jnp.zeros((count, readings - 4), BF16)
    records = jnp.concatenate(
        [
            jnp.concatenate([station_obs, blank, high, low, zero_two, rest], axis=1),
            jnp.concatenate([blank, station_obs, zero_two, high, low, rest], axis=1),
        ],
        axis=0,
    )
    payload = dot(match, records).astype(BF16)
    arrived = lax.all_to_all(
        payload.reshape(space_count, 2, 3 * readings), "space", 0, 0, tiled=True
    ).reshape(2 * space_count, 3 * readings)
    embedded = dot(
        jnp.concatenate([arrived[:, :readings], arrived[:, readings : 2 * readings]], axis=0),
        station_embed,
    ).astype(BF16)
    places = arrived[:, 2 * readings : 2 * readings + 4].astype(F32)
    pixel = jnp.stack(
        [places[:, 0] * 16 + places[:, 1], places[:, 2] * 16 + places[:, 3]], axis=0
    ).astype(jnp.int32)
    cell = jnp.arange(CELLS, dtype=jnp.int32)
    pixel_hot = (pixel.reshape(-1)[:, None] == cell[None, :]).astype(BF16)
    inject = jnp.einsum("kp,kc->pc", pixel_hot, embedded, preferred_element_type=F32)
    fine_own = tiles[0].astype(F32) + inject.reshape(TILE_H, TILE_W, DEPTH)

    rim = fine_own.astype(BF16)
    west = shifted(rim[:, -SIDE:], 0, 1)
    east = shifted(rim[:, :SIDE], 0, -1)
    wide = jnp.concatenate([west, rim, east], axis=1)
    north = shifted(wide[-HALO:], 1, 0)
    south = shifted(wide[:HALO], -1, 0)

    back_hot = (pixel.T.reshape(-1)[:, None] == cell[None, :]).astype(BF16)
    partial, found, coarse_own = trunk(
        place, north, south, west, east, fine_own, conv_fine, conv_mid, norm_gains, back_hot
    )
    coarse_rows = coarse_own[:2].reshape(1, 4, DEPTH // 2)
    parcel = jnp.concatenate(
        [
            found.reshape(space_count, 4, DEPTH),
            jnp.broadcast_to(coarse_rows, (space_count, 4, DEPTH // 2)),
        ],
        axis=2,
    )
    returned = lax.all_to_all(parcel, "space", 0, 0, tiled=True)

    grid = 2 * space_count
    coarse_in = returned[:, :, DEPTH:].reshape(grid, DEPTH)
    slots = returned[:, :, :DEPTH].reshape(4 * space_count, DEPTH)
    slot = dest * 4 + half * 2 + pair
    coarse_at = (dest // TILE_COLS) * (TILE_COLS * 2) + (dest % TILE_COLS) * 2
    coarse_at = coarse_at + (station_pixel % TILE_W) // (TILE_W // 2)
    slot_hot = slot[:, None] == jnp.arange(4 * space_count, dtype=jnp.int32)[None, :]
    coarse_hot = coarse_at[:, None] == jnp.arange(grid, dtype=jnp.int32)[None, :]
    pick = jnp.concatenate([slot_hot, coarse_hot], axis=1).astype(BF16)
    maps, scores = tail(
        place, slots, coarse_in, conv_coarse, norm_gains, partial, film, pick,
        out_proj, gauge_bin_projector,
    )
    return maps.reshape(1, 1, TILE_H, TILE_W, DEPTH), scores.reshape(1, count, -1)


def solution(mesh):
    in_specs = (
        P("space", None, None, None),
        P("space", None),
        P("space", None),
        P("space"),
        P(),
        P(),
        P(),
        P(),
        P(),
        P("lead", None),
        P(),
        P(),
        P(),
    )
    out_specs = (P("lead", "space", None, None, None), P("lead", "space", None))
    return jax.shard_map(body, mesh=mesh, in_specs=in_specs, out_specs=out_specs, check_vma=False)
```

```python
import jax
import jax.numpy as jnp
import numpy as np
from jax import lax
from jax.experimental import pallas as pl
from jax.experimental.pallas import tpu as pltpu
from jax.sharding import PartitionSpec as P

TILE_COLS = 8
TILE_H, TILE_W, DEPTH = 16, 32, 256
CELLS = TILE_H * TILE_W
EPS = 1e-06
HALO = 5
SIDE = 8
FRAME_H, FRAME_W = TILE_H + 2 * HALO, TILE_W + 2 * SIDE
ENC_H = FRAME_H - 2
BAND = 24
MID_W = 16
F32 = jnp.float32
BF16 = jnp.bfloat16


def dot(a, b):
    return jnp.dot(a, b, preferred_element_type=F32)


def silu(v):
    return v / (1.0 + jnp.exp(-v))


def rms_scale(values, gain):
    mean_sq = jnp.mean(values * values, axis=-1, keepdims=True)
    return values * lax.rsqrt(mean_sq + EPS) * gain


def column(shape):
    return lax.broadcasted_iota(jnp.int32, shape, 1)


def line(shape):
    return lax.broadcasted_iota(jnp.int32, shape, 0)


def ones_where(condition):
    return condition.astype(F32).astype(BF16)


def pool_fine_matrix():
    q = np.arange(BAND * FRAME_W)
    y, x = q // FRAME_W, q % FRAME_W
    rows = np.arange(BAND // 4 * MID_W)[:, None]
    hit = (y // 4 == rows // MID_W) & (x // 4 - 1 == rows % MID_W) & (rows % MID_W < 10)
    return jnp.asarray(hit, BF16) / 16


def pack_kernel(dest_ref, pixel_ref, obs, payload, key_ref):
    count, readings = obs.shape
    pairs = payload.shape[0]
    dest = dest_ref[...]
    hot = (line((pairs // 2, count)) == dest).astype(F32)
    earlier = ones_where(line((count, count)) < column((count, count)))
    prior = dot(hot.astype(BF16), earlier)
    position = jnp.sum(prior * hot, axis=0, keepdims=True).astype(jnp.int32)
    key = dest * 2 + (position & 1) + pairs * (position >> 1)
    key_ref[...] = key
    pixel = pixel_ref[...]
    lane = column((pairs, readings))
    places = jnp.zeros((pairs, readings), jnp.int32)
    for half in range(2):
        match = line((pairs, count)) + half * pairs == key
        sent = dot(ones_where(match), obs[...])
        payload[:, half * readings : (half + 1) * readings] = sent.astype(BF16)
        at = jnp.sum(jnp.where(match, pixel, 0), axis=1, keepdims=True)
        places = jnp.where(lane == 2 * half, at >> 4, places)
        places = jnp.where(lane == 2 * half + 1, at & 15, places)
    payload[:, 2 * readings :] = places.astype(F32).astype(BF16)


def inject_kernel(arrived, embed, tiles, own, first_cols, last_cols, first_rows, last_rows):
    pairs = arrived.shape[0]
    readings = embed.shape[0]
    sort, lane = line((8, readings)), column((8, readings))
    weights = jnp.where(lane == 2 * sort, 16.0, jnp.where(lane == 2 * sort + 1, 1.0, 0.0))
    weights = jnp.where(sort < 2, weights, 0.0).astype(BF16)
    pixels = lax.dot_general(
        weights,
        arrived[:, 2 * readings :],
        (((1,), (1,)), ((), ())),
        preferred_element_type=F32,
    ).astype(jnp.int32)
    fine = tiles[...].astype(F32)
    for half in range(2):
        embedded = dot(arrived[:, half * readings : (half + 1) * readings], embed[...])
        hot = ones_where(line((CELLS, pairs)) == pixels[half : half + 1])
        fine += dot(hot, embedded.astype(BF16))
    fine = fine.reshape(TILE_H, TILE_W, DEPTH)
    own[...] = fine
    first_cols[...] = fine[:, :SIDE].astype(BF16)
    last_cols[...] = fine[:, -SIDE:].astype(BF16)
    first_rows[...] = fine[:HALO].astype(BF16)
    last_rows[...] = fine[-HALO:].astype(BF16)


def trunk_kernel(
    place, north, south, west, east, own, conv_fine, conv_mid, gains, pool_fine, arrived,
    partial_ref, parcel,
    frame, taps, enc, mid_in, mid_taps, held, sent,
):
    frame[:HALO] = north[...].astype(F32)
    frame[HALO + TILE_H :] = south[...].astype(F32)
    frame[HALO : HALO + TILE_H, :SIDE] = west[...].astype(F32)
    frame[HALO : HALO + TILE_H, SIDE : SIDE + TILE_W] = own[...]
    frame[HALO : HALO + TILE_H, SIDE + TILE_W :] = east[...].astype(F32)
    gain = gains[0:1].astype(F32)
    for y in range(FRAME_H):
        normed = rms_scale(frame[y], gain)
        rows = slice(y * FRAME_W, (y + 1) * FRAME_W)
        taps[rows, :DEPTH] = pltpu.roll(normed, 1, 0).astype(BF16)
        taps[rows, DEPTH : 2 * DEPTH] = normed.astype(BF16)
        taps[rows, 2 * DEPTH :] = pltpu.roll(normed, FRAME_W - 1, 0).astype(BF16)
    size = BAND * FRAME_W
    mid_size = BAND // 4 * MID_W
    for band in range(ENC_H // BAND):
        first = band * BAND
        conv = 0.0
        for dy in range(3):
            start = (first + dy) * FRAME_W
            conv += dot(taps[start : start + size], conv_fine[dy])
        rows = frame[first + 1 : first + 1 + BAND].reshape(size, DEPTH)
        done = (rows + silu(conv)).astype(BF16)
        enc[first : first + BAND] = done.astype(F32).reshape(BAND, FRAME_W, DEPTH)
        mid_in[band * mid_size : (band + 1) * mid_size] = dot(pool_fine[...], done)

    mid = mid_in[...]
    normed = rms_scale(mid, gains[1:2].astype(F32))
    at = line(mid.shape)
    row = place[0] * (TILE_H // 4) - 1 + at // MID_W
    col = place[1] * (TILE_W // 4) - 1 + at % MID_W
    inside = (row >= 0) & (row < place[2] * (TILE_H // 4))
    inside = inside & (col >= 0) & (col < TILE_COLS * (TILE_W // 4))
    normed = jnp.where(inside, normed, 0.0)
    mid_taps[:, :DEPTH] = pltpu.roll(normed, 1, 0).astype(BF16)
    mid_taps[:, DEPTH : 2 * DEPTH] = normed.astype(BF16)
    mid_taps[:, 2 * DEPTH :] = pltpu.roll(normed, mid.shape[0] - 1, 0).astype(BF16)
    conv = 0.0
    for dy in range(3):
        conv += dot(mid_taps[dy * MID_W : (dy + 4) * MID_W], conv_mid[dy])
    enc_mid = mid[MID_W : 5 * MID_W] + silu(conv)
    high = enc_mid.astype(BF16)
    low = (enc_mid - high.astype(F32)).astype(BF16)

    shape = (CELLS, 4 * MID_W)
    cell = line(shape)
    spread = (cell >> 7) * MID_W + ((cell & (TILE_W - 1)) >> 2) + 1
    spread = ones_where(column(shape) == spread)
    centre = enc[HALO - 1 : HALO - 1 + TILE_H, SIDE : SIDE + TILE_W]
    partial = centre.reshape(CELLS, DEPTH) + (dot(spread, high) + dot(spread, low))
    held[...] = partial
    copy = pltpu.make_async_copy(held, partial_ref, sent)
    copy.start()

    x = column((16, 4 * MID_W)) % MID_W - 1
    pool = (x >= 0) & (x < 8) & ((x >> 2) == line((16, 4 * MID_W)))
    pool = jnp.where(pool, 1.0 / 16, 0.0).astype(BF16)
    coarse = dot(pool, high) + dot(pool, low)
    pairs, readings = arrived.shape[0], arrived.shape[1] // 3
    partial = partial.astype(BF16)
    for half in range(2):
        at = 2 * readings + 2 * half
        pixel = arrived[:, at : at + 1].astype(F32) * 16 + arrived[:, at + 1 : at + 2].astype(F32)
        hot = ones_where(column((pairs, CELLS)) == pixel.astype(jnp.int32))
        parcel[:, half * DEPTH : (half + 1) * DEPTH] = dot(hot, partial).astype(BF16)
    even = line((pairs, DEPTH)) % 2 == 0
    parcel[:, 2 * DEPTH :] = jnp.where(even, coarse[0:1], coarse[1:2]).astype(BF16)
    copy.wait()


def tail_kernel(
    place, returned, conv_coarse, gains, partial_ref, film, pick, out_proj, projector,
    maps_ref, scores_ref,
    taps, partial, maps, scores, sems,
):
    fetch = pltpu.make_async_copy(partial_ref, partial, sems.at[0])
    fetch.start()
    cells, wide = returned.shape[0], TILE_COLS * 2
    coarse = returned[:, 2 * DEPTH :].astype(F32)
    normed = rms_scale(coarse, gains[2:3].astype(F32))
    col = line(coarse.shape) % wide
    taps[:wide] = jnp.zeros((wide, 3 * DEPTH), BF16)
    taps[wide + cells :] = jnp.zeros((wide, 3 * DEPTH), BF16)
    inner = slice(wide, wide + cells)
    left, right = pltpu.roll(normed, 1, 0), pltpu.roll(normed, cells - 1, 0)
    taps[inner, :DEPTH] = jnp.where(col == 0, 0.0, left).astype(BF16)
    taps[inner, DEPTH : 2 * DEPTH] = normed.astype(BF16)
    taps[inner, 2 * DEPTH :] = jnp.where(col == wide - 1, 0.0, right).astype(BF16)
    conv = 0.0
    for dy in range(3):
        conv += dot(taps[dy * wide : dy * wide + cells], conv_coarse[dy])
    context = coarse + silu(conv)
    high = context.astype(BF16)
    low = (context - high.astype(F32)).astype(BF16)

    gain = gains[3:4].astype(F32)
    scale, shift = 1.0 + film[0:1], film[1:2]

    def decode(values):
        hidden = rms_scale(values, gain) * scale + shift
        return (values + dot(silu(hidden).astype(BF16), out_proj[...])).astype(BF16)

    here = place[0] * wide + place[1] * 2 + ((line((CELLS, cells)) & (TILE_W - 1)) >> 4)
    mine = ones_where(column((CELLS, cells)) == here)
    spread = dot(mine, high) + dot(mine, low)
    fetch.wait()
    maps[...] = decode(partial[...] + spread)
    put_maps = pltpu.make_async_copy(maps, maps_ref, sems.at[1])
    put_maps.start()

    at_stations = dot(pick[:, 2 * cells :], high) + dot(pick[:, 2 * cells :], low)
    for half in range(2):
        found = returned[:, half * DEPTH : (half + 1) * DEPTH]
        at_stations += dot(pick[:, half * cells : (half + 1) * cells], found)
    scores[...] = dot(decode(at_stations), projector[...]).astype(BF16)
    put_scores = pltpu.make_async_copy(scores, scores_ref, sems.at[2])
    put_scores.start()
    put_maps.wait()
    put_scores.wait()


def call(kernel, outs, scratch, operands, anywhere=(), scalars=0):
    vmem = pl.BlockSpec(memory_space=pltpu.VMEM)
    smem = pl.BlockSpec(memory_space=pltpu.SMEM)
    hbm = pl.BlockSpec(memory_space=pl.ANY)
    ins = [smem if i < scalars else vmem for i in range(len(operands))]
    return pl.pallas_call(
        kernel,
        out_shape=[jax.ShapeDtypeStruct(shape, dtype) for shape, dtype in outs],
        in_specs=[hbm if ("in", i) in anywhere else spec for i, spec in enumerate(ins)],
        out_specs=[hbm if ("out", i) in anywhere else vmem for i in range(len(outs))],
        scratch_shapes=scratch,
        compiler_params=pltpu.CompilerParams(vmem_limit_bytes=32 * 2**20),
    )(*operands)


def pack(dest, pixel, obs, space_count):
    count, readings = obs.shape
    return call(
        pack_kernel,
        [((2 * space_count, 3 * readings), BF16), ((1, count), jnp.int32)],
        [],
        [dest, pixel, obs],
    )


def inject(arrived, embed, tiles):
    return call(
        inject_kernel,
        [
            ((TILE_H, TILE_W, DEPTH), F32),
            ((TILE_H, SIDE, DEPTH), BF16),
            ((TILE_H, SIDE, DEPTH), BF16),
            ((HALO, TILE_W, DEPTH), BF16),
            ((HALO, TILE_W, DEPTH), BF16),
        ],
        [],
        [arrived, embed, tiles],
    )


def trunk(place, north, south, west, east, own, conv_fine, conv_mid, gains, arrived):
    return call(
        trunk_kernel,
        [((CELLS, DEPTH), F32), ((arrived.shape[0], 3 * DEPTH), BF16)],
        [
            pltpu.VMEM((FRAME_H, FRAME_W, DEPTH), F32),
            pltpu.VMEM((FRAME_H * FRAME_W, 3 * DEPTH), BF16),
            pltpu.VMEM((ENC_H, FRAME_W, DEPTH), F32),
            pltpu.VMEM((ENC_H // 4 * MID_W, DEPTH), F32),
            pltpu.VMEM((ENC_H // 4 * MID_W, 3 * DEPTH), BF16),
            pltpu.VMEM((CELLS, DEPTH), F32),
            pltpu.SemaphoreType.DMA,
        ],
        [
            place, north, south, west, east, own,
            conv_fine.reshape(3, 3 * DEPTH, DEPTH),
            conv_mid.reshape(3, 3 * DEPTH, DEPTH),
            gains, pool_fine_matrix(), arrived,
        ],
        anywhere=[("out", 0)],
        scalars=1,
    )


def tail(place, returned, conv_coarse, gains, partial, film, pick, out_proj, projector):
    cells = returned.shape[0]
    outs = [((CELLS, DEPTH), BF16), ((pick.shape[0], projector.shape[1]), BF16)]
    return call(
        tail_kernel,
        outs,
        [
            pltpu.VMEM((cells + 4 * TILE_COLS, 3 * DEPTH), BF16),
            pltpu.VMEM((CELLS, DEPTH), F32),
            *[pltpu.VMEM(shape, dtype) for shape, dtype in outs],
            pltpu.SemaphoreType.DMA((3,)),
        ],
        [
            place, returned, conv_coarse.reshape(3, 3 * DEPTH, DEPTH), gains,
            partial, film, pick, out_proj, projector,
        ],
        anywhere=[("in", 4), ("out", 0), ("out", 1)],
        scalars=1,
    )


def shifted(value, row_step, col_step):
    count = lax.axis_size("space")
    pairs = []
    for source in range(count):
        row, col = source // TILE_COLS + row_step, source % TILE_COLS + col_step
        if 0 <= row < count // TILE_COLS and 0 <= col < TILE_COLS:
            pairs.append((source, row * TILE_COLS + col))
    return lax.ppermute(value, "space", pairs)


def body(
    tiles,
    station_obs,
    station_tile,
    station_pixel,
    station_embed,
    conv_fine,
    conv_mid,
    conv_coarse,
    norm_gains,
    film_table,
    horizon_step_list,
    out_proj,
    gauge_bin_projector,
):
    space_count = lax.axis_size("space")
    count, readings = station_obs.shape
    space_at = lax.axis_index("space")
    place = jnp.stack(
        [space_at // TILE_COLS, space_at % TILE_COLS, jnp.int32(space_count // TILE_COLS)]
    ).astype(jnp.int32)

    table_rows = film_table.shape[0]
    own_rows = lax.axis_index("lead") * table_rows + jnp.arange(table_rows, dtype=jnp.int32)
    lead_hot = (horizon_step_list[:, None] == own_rows[None, :]).astype(BF16)
    film_parts = lax.all_gather(dot(lead_hot, film_table).astype(BF16), "lead")
    film = jnp.sum(film_parts.astype(F32), axis=0)
    film = lax.dynamic_slice_in_dim(film, lax.axis_index("lead"), 1, 0).reshape(2, DEPTH)

    dest = station_tile.reshape(1, count)
    pixel = station_pixel.reshape(1, count)
    payload, key = pack(dest, pixel, station_obs, space_count)
    arrived = lax.all_to_all(
        payload.reshape(space_count, 2, 3 * readings), "space", 0, 0, tiled=True
    ).reshape(2 * space_count, 3 * readings)
    own, first_cols, last_cols, first_rows, last_rows = inject(
        arrived, station_embed, tiles.reshape(CELLS, DEPTH)
    )

    west = shifted(last_cols, 0, 1)
    east = shifted(first_cols, 0, -1)

    def widened(rows, side):
        return jnp.concatenate([west[side], rows, east[side]], axis=1)

    north = shifted(widened(last_rows, slice(-HALO, None)), 1, 0)
    south = shifted(widened(first_rows, slice(0, HALO)), -1, 0)

    partial, parcel = trunk(
        place, north, south, west, east, own, conv_fine, conv_mid, norm_gains, arrived
    )
    returned = lax.all_to_all(
        parcel.reshape(space_count, 2, 3 * DEPTH), "space", 0, 0, tiled=True
    ).reshape(2 * space_count, 3 * DEPTH)

    coarse_at = (dest // TILE_COLS) * (TILE_COLS * 2) + (dest % TILE_COLS) * 2
    coarse_at = coarse_at + (pixel % TILE_W) // (TILE_W // 2) + 4 * space_count
    rows = jnp.arange(6 * space_count, dtype=jnp.int32)[None, :]
    pick = ((key.reshape(count, 1) == rows) | (coarse_at.reshape(count, 1) == rows)).astype(BF16)
    maps, scores = tail(
        place, returned, conv_coarse, norm_gains, partial, film, pick,
        out_proj, gauge_bin_projector,
    )
    return maps.reshape(1, 1, TILE_H, TILE_W, DEPTH), scores.reshape(1, count, -1)


def solution(mesh):
    in_specs = (
        P("space", None, None, None),
        P("space", None),
        P("space", None),
        P("space"),
        P(),
        P(),
        P(),
        P(),
        P(),
        P("lead", None),
        P(),
        P(),
        P(),
    )
    out_specs = (P("lead", "space", None, None, None), P("lead", "space", None))
    return jax.shard_map(body, mesh=mesh, in_specs=in_specs, out_specs=out_specs, check_vma=False)
```

```python
import functools

import jax
import jax.numpy as jnp
from jax import lax
from jax.experimental import pallas as pl
from jax.experimental.pallas import tpu as pltpu
from jax.sharding import PartitionSpec as P

TILE_COLS = 8
TILE_H, TILE_W, DEPTH = 16, 32, 256
CELLS = TILE_H * TILE_W
EPS = 1e-06
HALO = 5
SIDE = 8
FRAME_H, FRAME_W = TILE_H + 2 * HALO, TILE_W + 2 * SIDE
ENC_H = FRAME_H - 2
MID_W = 16
F32 = jnp.float32
BF16 = jnp.bfloat16


def dot(a, b):
    return jnp.dot(a, b, preferred_element_type=F32)


def silu(v):
    return v / (1.0 + jnp.exp(-v))


def rms_scale(values, gain):
    mean_sq = jnp.mean(values * values, axis=-1, keepdims=True)
    return values * lax.rsqrt(mean_sq + EPS) * gain


def column(shape):
    return lax.broadcasted_iota(jnp.int32, shape, 1)


def line(shape):
    return lax.broadcasted_iota(jnp.int32, shape, 0)


def ones_where(condition):
    return condition.astype(F32).astype(BF16)


def grid_place():
    at = lax.axis_index("space")
    return lax.div(at, TILE_COLS), lax.rem(at, TILE_COLS)


def pack_kernel(ids, obs, payload, lookup):
    count, readings = obs.shape
    pairs = payload.shape[0]
    earlier = ones_where(line((count, count)) < column((count, count)))
    lane = column((pairs, readings))
    dest, pixel = ids[...] // CELLS, ids[...] % CELLS
    hot = (line((pairs // 2, count)) == dest).astype(F32)
    prior = dot(hot.astype(BF16), earlier)
    position = jnp.sum(prior * hot, axis=0, keepdims=True).astype(jnp.int32)
    key = dest * 2 + (position & 1) + pairs * (position >> 1)
    coarse = dest * 2 + ((pixel & (TILE_W - 1)) >> 4)
    sort = line((16, count))
    found = jnp.where(sort == 0, key >> 4, jnp.where(sort == 1, key & 15, 0))
    found = jnp.where(sort == 2, coarse >> 4, jnp.where(sort == 3, coarse & 15, found))
    lookup[...] = found.astype(F32).astype(BF16)
    places = jnp.zeros((pairs, readings), jnp.int32)
    for half in range(2):
        match = line((pairs, count)) + half * pairs == key
        sent = dot(ones_where(match), obs[...])
        payload[:, half * readings : (half + 1) * readings] = sent.astype(BF16)
        at = jnp.sum(jnp.where(match, pixel, 0), axis=1, keepdims=True)
        places = jnp.where(lane == 2 * half, at >> 4, places)
        places = jnp.where(lane == 2 * half + 1, at & 15, places)
    payload[:, 2 * readings :] = places.astype(F32).astype(BF16)


def inject_kernel(
    arrived, embed, tiles, own, first_cols, last_cols, first_rows, last_rows
):
    pairs = arrived.shape[0]
    readings = embed.shape[0]
    weight = embed[...].astype(BF16)
    sort, lane = line((8, readings)), column((8, readings))
    weights = jnp.where(lane == 2 * sort, 16.0, jnp.where(lane == 2 * sort + 1, 1.0, 0.0))
    weights = jnp.where(sort < 2, weights, 0.0).astype(BF16)
    pixels = lax.dot_general(
        weights,
        arrived[:, 2 * readings :],
        (((1,), (1,)), ((), ())),
        preferred_element_type=F32,
    ).astype(jnp.int32)
    fine = 0.0
    for half in range(2):
        embedded = dot(arrived[:, half * readings : (half + 1) * readings], weight)
        hot = ones_where(line((CELLS, pairs)) == pixels[half : half + 1])
        fine += dot(hot, embedded.astype(BF16))
    fine = (fine + tiles[...]).reshape(TILE_H, TILE_W, DEPTH)
    own[...] = fine
    first_cols[...] = fine[:, :SIDE].astype(BF16)
    last_cols[...] = fine[:, -SIDE:].astype(BF16)
    first_rows[...] = fine[:HALO].astype(BF16)
    last_rows[...] = fine[-HALO:].astype(BF16)


def widen_kernel(west, east, first_rows, last_rows, top, bottom):
    for rows, target, side in (
        (first_rows, top, slice(0, HALO)),
        (last_rows, bottom, slice(TILE_H - HALO, TILE_H)),
    ):
        parts = [west[side], rows[...], east[side]]
        whole = jnp.concatenate([part.astype(F32) for part in parts], axis=1)
        target[...] = whole.astype(BF16)


def trunk_kernel(
    image_rows,
    north, south, west, east, own, conv_fine, conv_mid, gains, arrived,
    partial_ref, parcel,
    frame, taps, enc, mid_in, mid_taps,
):
    frame[:HALO] = north[...].astype(F32)
    frame[HALO + TILE_H :] = south[...].astype(F32)
    frame[HALO : HALO + TILE_H, :SIDE] = west[...].astype(F32)
    frame[HALO : HALO + TILE_H, SIDE : SIDE + TILE_W] = own[...]
    frame[HALO : HALO + TILE_H, SIDE + TILE_W :] = east[...].astype(F32)
    gain = gains[0:1].astype(F32)
    for y in range(FRAME_H):
        normed = rms_scale(frame[y], gain)
        rows = slice(y * FRAME_W, (y + 1) * FRAME_W)
        taps[rows, :DEPTH] = pltpu.roll(normed, 1, 0).astype(BF16)
        taps[rows, DEPTH : 2 * DEPTH] = normed.astype(BF16)
        taps[rows, 2 * DEPTH :] = pltpu.roll(normed, FRAME_W - 1, 0).astype(BF16)
    size = ENC_H * FRAME_W
    conv = 0.0
    for dy in range(3):
        conv += dot(taps[dy * FRAME_W : dy * FRAME_W + size], conv_fine[dy])
    done = (frame[1 : 1 + ENC_H].reshape(size, DEPTH) + silu(conv)).astype(BF16)
    enc[...] = done.astype(F32).reshape(ENC_H, FRAME_W, DEPTH)
    group = 4 * FRAME_W
    at = column((MID_W, group))
    x = at - FRAME_W * sum((at >= FRAME_W * i).astype(jnp.int32) for i in range(1, 4))
    pool = ((x >> 2) - 1 == line((MID_W, group))) & (line((MID_W, group)) < 10)
    pool = jnp.where(pool, 1.0 / 16, 0.0).astype(BF16)
    for i in range(ENC_H // 4):
        mid_in[i * MID_W : (i + 1) * MID_W] = dot(pool, done[i * group : (i + 1) * group])

    mid = mid_in[...]
    normed = rms_scale(mid, gains[1:2].astype(F32))
    at = line(mid.shape)
    row_at, col_at = grid_place()
    row = row_at * (TILE_H // 4) - 1 + at // MID_W
    col = col_at * (TILE_W // 4) - 1 + at % MID_W
    inside = (row >= 0) & (row < image_rows * (TILE_H // 4))
    inside = inside & (col >= 0) & (col < TILE_COLS * (TILE_W // 4))
    normed = jnp.where(inside, normed, 0.0)
    mid_taps[:, :DEPTH] = pltpu.roll(normed, 1, 0).astype(BF16)
    mid_taps[:, DEPTH : 2 * DEPTH] = normed.astype(BF16)
    mid_taps[:, 2 * DEPTH :] = pltpu.roll(normed, mid.shape[0] - 1, 0).astype(BF16)
    conv = 0.0
    for dy in range(3):
        conv += dot(mid_taps[dy * MID_W : (dy + 4) * MID_W], conv_mid[dy])
    enc_mid = mid[MID_W : 5 * MID_W] + silu(conv)
    high = enc_mid.astype(BF16)
    low = (enc_mid - high.astype(F32)).astype(BF16)

    shape = (CELLS, 4 * MID_W)
    cell = line(shape)
    spread = (cell >> 7) * MID_W + ((cell & (TILE_W - 1)) >> 2) + 1
    spread = ones_where(column(shape) == spread)
    centre = enc[HALO - 1 : HALO - 1 + TILE_H, SIDE : SIDE + TILE_W]
    partial = centre.reshape(CELLS, DEPTH) + (dot(spread, high) + dot(spread, low))
    partial_ref[...] = partial

    x = column((16, 4 * MID_W)) % MID_W - 1
    pool = (x >= 0) & (x < 8) & ((x >> 2) == line((16, 4 * MID_W)))
    pool = jnp.where(pool, 1.0 / 16, 0.0).astype(BF16)
    coarse = dot(pool, high) + dot(pool, low)
    pairs, readings = arrived.shape[0], arrived.shape[1] // 3
    partial = partial.astype(BF16)
    for half in range(2):
        at = 2 * readings + 2 * half
        pixel = arrived[:, at : at + 1].astype(F32) * 16 + arrived[:, at + 1 : at + 2].astype(F32)
        hot = ones_where(column((pairs, CELLS)) == pixel.astype(jnp.int32))
        parcel[:, half * DEPTH : (half + 1) * DEPTH] = dot(hot, partial).astype(BF16)
    even = line((pairs, DEPTH)) % 2 == 0
    parcel[:, 2 * DEPTH :] = jnp.where(even, coarse[0:1], coarse[1:2]).astype(BF16)


def tail_kernel(
    returned, conv_coarse, gains, partial, film, lookup, out_proj, projector,
    maps_ref, scores_ref,
    taps, maps, scores, sems,
):
    cells, wide = returned.shape[0], TILE_COLS * 2
    coarse = returned[:, 2 * DEPTH :].astype(F32)
    normed = rms_scale(coarse, gains[2:3].astype(F32))
    col = line(coarse.shape) % wide
    taps[:wide] = jnp.zeros((wide, 3 * DEPTH), BF16)
    taps[wide + cells :] = jnp.zeros((wide, 3 * DEPTH), BF16)
    inner = slice(wide, wide + cells)
    left, right = pltpu.roll(normed, 1, 0), pltpu.roll(normed, cells - 1, 0)
    taps[inner, :DEPTH] = jnp.where(col == 0, 0.0, left).astype(BF16)
    taps[inner, DEPTH : 2 * DEPTH] = normed.astype(BF16)
    taps[inner, 2 * DEPTH :] = jnp.where(col == wide - 1, 0.0, right).astype(BF16)
    conv = 0.0
    for dy in range(3):
        conv += dot(taps[dy * wide : dy * wide + cells], conv_coarse[dy])
    context = coarse + silu(conv)
    high = context.astype(BF16)
    low = (context - high.astype(F32)).astype(BF16)

    gain = gains[3:4].astype(F32)
    scale, shift = 1.0 + film[0:1], film[1:2]

    def decode(values):
        hidden = rms_scale(values, gain) * scale + shift
        return (values + dot(silu(hidden).astype(BF16), out_proj[...])).astype(BF16)

    row_at, col_at = grid_place()
    here = row_at * wide + col_at * 2 + ((line((CELLS, cells)) & (TILE_W - 1)) >> 4)
    mine = ones_where(column((CELLS, cells)) == here)
    spread = dot(mine, high) + dot(mine, low)
    maps[...] = decode(partial[...] + spread)
    put_maps = pltpu.make_async_copy(maps, maps_ref, sems.at[0])
    put_maps.start()

    count = lookup.shape[1]
    same = ones_where(line((count, count)) == column((count, count)))
    where = lax.dot_general(
        same, lookup[...], (((1,), (1,)), ((), ())), preferred_element_type=F32
    )
    key = (where[:, 0:1] * 16 + where[:, 1:2]).astype(jnp.int32)
    area = (where[:, 2:3] * 16 + where[:, 3:4]).astype(jnp.int32)
    slot = column((count, cells))
    pick = ones_where(slot == area)
    at_stations = dot(pick, high) + dot(pick, low)
    for half in range(2):
        found = returned[:, half * DEPTH : (half + 1) * DEPTH]
        at_stations += dot(ones_where(slot + half * cells == key), found)
    scores[...] = dot(decode(at_stations), projector[...]).astype(BF16)
    put_scores = pltpu.make_async_copy(scores, scores_ref, sems.at[1])
    put_scores.start()
    put_maps.wait()
    put_scores.wait()


def call(kernel, outs, scratch, operands, hbm_outs=(), megabytes=4):
    vmem = pl.BlockSpec(memory_space=pltpu.VMEM)
    hbm = pl.BlockSpec(memory_space=pltpu.HBM)
    return pl.pallas_call(
        kernel,
        out_shape=[jax.ShapeDtypeStruct(shape, dtype) for shape, dtype in outs],
        in_specs=[vmem] * len(operands),
        out_specs=[hbm if i in hbm_outs else vmem for i in range(len(outs))],
        scratch_shapes=scratch,
        compiler_params=pltpu.CompilerParams(vmem_limit_bytes=megabytes * 2**20),
    )(*operands)


def pack(ids, obs, space_count):
    count, readings = obs.shape
    outs = [((2 * space_count, 3 * readings), BF16), ((16, count), BF16)]
    return call(pack_kernel, outs, [], [ids, obs], megabytes=8)


def inject(arrived, embed, tiles):
    return call(
        inject_kernel,
        [
            ((TILE_H, TILE_W, DEPTH), F32),
            ((TILE_H, SIDE, DEPTH), BF16),
            ((TILE_H, SIDE, DEPTH), BF16),
            ((HALO, TILE_W, DEPTH), BF16),
            ((HALO, TILE_W, DEPTH), BF16),
        ],
        [],
        [arrived, embed, tiles],
        megabytes=8,
    )


def widen(west, east, first_rows, last_rows):
    shape = (HALO, FRAME_W, DEPTH)
    return call(
        widen_kernel, [(shape, BF16), (shape, BF16)], [], [west, east, first_rows, last_rows]
    )


def trunk(image_rows, north, south, west, east, own, conv_fine, conv_mid, gains, arrived):
    return call(
        functools.partial(trunk_kernel, image_rows),
        [((CELLS, DEPTH), F32), ((arrived.shape[0], 3 * DEPTH), BF16)],
        [
            pltpu.VMEM((FRAME_H, FRAME_W, DEPTH), F32),
            pltpu.VMEM((FRAME_H * FRAME_W, 3 * DEPTH), BF16),
            pltpu.VMEM((ENC_H, FRAME_W, DEPTH), F32),
            pltpu.VMEM((ENC_H // 4 * MID_W, DEPTH), F32),
            pltpu.VMEM((ENC_H // 4 * MID_W, 3 * DEPTH), BF16),
        ],
        [
            north, south, west, east, own,
            conv_fine.reshape(3, 3 * DEPTH, DEPTH),
            conv_mid.reshape(3, 3 * DEPTH, DEPTH),
            gains, arrived,
        ],
        megabytes=16,
    )


def tail(returned, conv_coarse, gains, partial, film, lookup, out_proj, projector):
    cells = returned.shape[0]
    outs = [((CELLS, DEPTH), BF16), ((lookup.shape[1], projector.shape[1]), BF16)]
    return call(
        tail_kernel,
        outs,
        [
            pltpu.VMEM((cells + 4 * TILE_COLS, 3 * DEPTH), BF16),
            *[pltpu.VMEM(shape, dtype) for shape, dtype in outs],
            pltpu.SemaphoreType.DMA((2,)),
        ],
        [
            returned, conv_coarse.reshape(3, 3 * DEPTH, DEPTH), gains,
            partial, film, lookup, out_proj, projector,
        ],
        hbm_outs=(0, 1),
        megabytes=16,
    )


def shifted(value, row_step, col_step):
    count = lax.axis_size("space")
    pairs = []
    for source in range(count):
        row, col = source // TILE_COLS + row_step, source % TILE_COLS + col_step
        if 0 <= row < count // TILE_COLS and 0 <= col < TILE_COLS:
            pairs.append((source, row * TILE_COLS + col))
    return lax.ppermute(value, "space", pairs)


def body(
    tiles,
    station_obs,
    station_tile,
    station_pixel,
    station_embed,
    conv_fine,
    conv_mid,
    conv_coarse,
    norm_gains,
    film_table,
    horizon_step_list,
    out_proj,
    gauge_bin_projector,
):
    space_count = lax.axis_size("space")
    count, readings = station_obs.shape
    table_rows = film_table.shape[0]
    own_rows = lax.axis_index("lead") * table_rows + jnp.arange(table_rows, dtype=jnp.int32)
    lead_hot = (horizon_step_list[:, None] == own_rows[None, :]).astype(BF16)
    film_parts = lax.all_gather(dot(lead_hot, film_table).astype(BF16), "lead")
    film = jnp.sum(film_parts.astype(F32), axis=0)
    film = lax.dynamic_slice_in_dim(film, lax.axis_index("lead"), 1, 0).reshape(2, DEPTH)

    ids = (station_tile[:, 0] * CELLS + station_pixel).reshape(1, count)
    payload, lookup = pack(ids, station_obs, space_count)
    arrived = lax.all_to_all(
        payload.reshape(space_count, 2, 3 * readings), "space", 0, 0, tiled=True
    ).reshape(2 * space_count, 3 * readings)
    arrived, film, embed, fine = lax.optimization_barrier(
        (arrived, film, station_embed.astype(F32), tiles.reshape(CELLS, DEPTH).astype(F32))
    )
    own, first_cols, last_cols, first_rows, last_rows = inject(arrived, embed, fine)

    west = shifted(last_cols, 0, 1)
    east = shifted(first_cols, 0, -1)

    top, bottom = widen(west, east, first_rows, last_rows)
    north = shifted(bottom, 1, 0)
    south = shifted(top, -1, 0)

    partial, parcel = trunk(
        space_count // TILE_COLS,
        north, south, west, east, own, conv_fine, conv_mid, norm_gains, arrived,
    )
    returned = lax.all_to_all(
        parcel.reshape(space_count, 2, 3 * DEPTH), "space", 0, 0, tiled=True
    ).reshape(2 * space_count, 3 * DEPTH)

    maps, scores = tail(
        returned, conv_coarse, norm_gains, partial, film, lookup, out_proj, gauge_bin_projector
    )
    return maps.reshape(1, 1, TILE_H, TILE_W, DEPTH), scores.reshape(1, count, -1)


def solution(mesh):
    in_specs = (
        P("space", None, None, None),
        P("space", None),
        P("space", None),
        P("space"),
        P(),
        P(),
        P(),
        P(),
        P(),
        P("lead", None),
        P(),
        P(),
        P(),
    )
    out_specs = (P("lead", "space", None, None, None), P("lead", "space", None))
    return jax.shard_map(body, mesh=mesh, in_specs=in_specs, out_specs=out_specs, check_vma=False)
```

```python
import functools

import jax
import jax.numpy as jnp
from jax import lax
from jax.experimental import pallas as pl
from jax.experimental.pallas import tpu as pltpu
from jax.sharding import PartitionSpec as P

TILE_COLS = 8
TILE_H, TILE_W, DEPTH = 16, 32, 256
CELLS = TILE_H * TILE_W
EPS = 1e-06
HALO = 5
SIDE = 8
FRAME_H, FRAME_W = TILE_H + 2 * HALO, TILE_W + 2 * SIDE
ENC_H = FRAME_H - 2
MID_W = 16
F32 = jnp.float32
BF16 = jnp.bfloat16


def dot(a, b):
    return jnp.dot(a, b, preferred_element_type=F32)


def dot_rows(a, b):
    return lax.dot_general(a, b, (((1,), (1,)), ((), ())), preferred_element_type=F32)


def silu(v):
    return v / (1.0 + jnp.exp(-v))


def rms_scale(values, gain):
    mean_sq = jnp.mean(values * values, axis=-1, keepdims=True)
    return values * lax.rsqrt(mean_sq + EPS) * gain


def column(shape):
    return lax.broadcasted_iota(jnp.int32, shape, 1)


def line(shape):
    return lax.broadcasted_iota(jnp.int32, shape, 0)


def ones_where(condition):
    return condition.astype(F32).astype(BF16)


def grid_place():
    at = lax.axis_index("space")
    return lax.div(at, TILE_COLS), lax.rem(at, TILE_COLS)


def pack_kernel(records, payload, lookup):
    count, readings = records.shape[0], records.shape[1] // 2
    pairs = payload.shape[0]
    obs = records[:, :readings]
    earlier = ones_where(line((count, count)) < column((count, count)))
    sort, lane = line((16, readings)), column((16, readings))
    weights = jnp.where((sort == 1) & (lane == 1), 16.0, 0.0)
    weights = jnp.where((sort == 0) & (lane == 0) | (sort == 1) & (lane == 2), 1.0, weights)
    ids = dot_rows(weights.astype(BF16), records[:, readings:]).astype(jnp.int32)
    dest, pixel = ids[0:1], ids[1:2]
    lane = column((pairs, readings))
    hot = (line((pairs // 2, count)) == dest).astype(F32)
    prior = dot(hot.astype(BF16), earlier)
    position = jnp.sum(prior * hot, axis=0, keepdims=True).astype(jnp.int32)
    key = dest * 2 + (position & 1) + pairs * (position >> 1)
    coarse = dest * 2 + ((pixel & (TILE_W - 1)) >> 4)
    sort = line((16, count))
    found = jnp.where(sort == 0, key >> 4, jnp.where(sort == 1, key & 15, 0))
    found = jnp.where(sort == 2, coarse >> 4, jnp.where(sort == 3, coarse & 15, found))
    lookup[...] = found.astype(F32).astype(BF16)
    places = jnp.zeros((pairs, readings), jnp.int32)
    for half in range(2):
        match = line((pairs, count)) + half * pairs == key
        sent = dot(ones_where(match), obs)
        payload[:, half * readings : (half + 1) * readings] = sent.astype(BF16)
        at = jnp.sum(jnp.where(match, pixel, 0), axis=1, keepdims=True)
        places = jnp.where(lane == 2 * half, at >> 4, places)
        places = jnp.where(lane == 2 * half + 1, at & 15, places)
    payload[:, 2 * readings :] = places.astype(F32).astype(BF16)


def inject_kernel(
    steps, arrived, embed, tiles, film_table,
    own, first_cols, last_cols, first_rows, last_rows, film,
):
    pairs = arrived.shape[0]
    readings = embed.shape[0]
    weight = embed[...]
    sort, lane = line((8, readings)), column((8, readings))
    weights = jnp.where(lane == 2 * sort, 16.0, jnp.where(lane == 2 * sort + 1, 1.0, 0.0))
    weights = jnp.where(sort < 2, weights, 0.0).astype(BF16)
    pixels = dot_rows(weights, arrived[:, 2 * readings :]).astype(jnp.int32)
    fine = 0.0
    for half in range(2):
        embedded = dot(arrived[:, half * readings : (half + 1) * readings], weight)
        hot = ones_where(line((CELLS, pairs)) == pixels[half : half + 1])
        fine += dot(hot, embedded.astype(BF16))
    fine = (fine + tiles[...].astype(F32)).reshape(TILE_H, TILE_W, DEPTH)
    own[...] = fine
    table_rows = film_table.shape[0]
    offset = lax.axis_index("lead") * table_rows
    sort = line((8, table_rows))
    at = jnp.full((8, table_rows), -1, jnp.int32)
    for i in range(4):
        at = jnp.where((sort & 3) == i, steps[i] - offset, at)
    hot = ones_where(column((8, table_rows)) == at)
    both = dot(hot, film_table[...])
    rows = jnp.where(line((8, DEPTH)) < 4, both[:, :DEPTH], both[:, DEPTH:])
    film[...] = rows
    at = line((SIDE, DEPTH))
    for y in range(TILE_H):
        first, last = fine[y, :SIDE], fine[y, -SIDE:]
        if y < 8:
            first = jnp.where(at == SIDE - 1, rows[y : y + 1], first)
            last = jnp.where(at == 0, rows[y : y + 1], last)
        first_cols[y] = first.astype(BF16)
        last_cols[y] = last.astype(BF16)
    first_rows[...] = fine[:HALO].astype(BF16)
    last_rows[...] = fine[-HALO:].astype(BF16)


def widen_kernel(west, east, first_rows, last_rows, top, bottom):
    _, col_at = grid_place()
    at = line((FRAME_W, DEPTH))
    for rows, target, offset in ((first_rows, top, 0), (last_rows, bottom, TILE_H - HALO)):
        for y in range(HALO):
            left = jnp.where(col_at > 0, west[offset + y].astype(F32), 0.0)
            right = jnp.where(col_at < TILE_COLS - 1, east[offset + y].astype(F32), 0.0)
            whole = jnp.concatenate([left, rows[y].astype(F32), right], axis=0)
            if offset:
                whole = jnp.where(at == 0, west[y, 0:1].astype(F32), whole)
                if y + HALO < 8:
                    whole = jnp.where(at == 1, west[y + HALO, 0:1].astype(F32), whole)
            target[y] = whole.astype(BF16)


def trunk_kernel(
    image_rows,
    north, south, west, east, own, film, conv_fine, conv_mid, gains, arrived,
    partial_ref, parcel, film_ref,
    frame, taps, enc, mid_in, mid_taps,
):
    row_at, col_at = grid_place()
    left = west[...].astype(F32)
    right = east[...].astype(F32)
    above = north[...].astype(F32)
    at = line((8, DEPTH))
    rows = film[...]
    for y in range(8):
        extra = above[y, 0:1] if y < HALO else above[y - HALO, 1:2]
        rows += jnp.where(at == y, left[y, 0:1] + right[y, SIDE - 1 : SIDE] + extra, 0.0)
    film_ref[...] = rows
    frame[:HALO] = jnp.where(row_at > 0, above, 0.0)
    frame[HALO + TILE_H :] = jnp.where(row_at < image_rows - 1, south[...].astype(F32), 0.0)
    frame[HALO : HALO + TILE_H, :SIDE] = jnp.where(col_at > 0, left, 0.0)
    frame[HALO : HALO + TILE_H, SIDE : SIDE + TILE_W] = own[...]
    frame[HALO : HALO + TILE_H, SIDE + TILE_W :] = jnp.where(col_at < TILE_COLS - 1, right, 0.0)
    gain = gains[0:1].astype(F32)
    for y in range(FRAME_H):
        normed = rms_scale(frame[y], gain)
        rows = slice(y * FRAME_W, (y + 1) * FRAME_W)
        taps[rows, :DEPTH] = pltpu.roll(normed, 1, 0).astype(BF16)
        taps[rows, DEPTH : 2 * DEPTH] = normed.astype(BF16)
        taps[rows, 2 * DEPTH :] = pltpu.roll(normed, FRAME_W - 1, 0).astype(BF16)
    size = ENC_H * FRAME_W
    conv = 0.0
    for dy in range(3):
        conv += dot(taps[dy * FRAME_W : dy * FRAME_W + size], conv_fine[dy])
    done = (frame[1 : 1 + ENC_H].reshape(size, DEPTH) + silu(conv)).astype(BF16)
    enc[...] = done.astype(F32).reshape(ENC_H, FRAME_W, DEPTH)
    group = 4 * FRAME_W
    at = column((MID_W, group))
    x = at - FRAME_W * sum((at >= FRAME_W * i).astype(jnp.int32) for i in range(1, 4))
    pool = ((x >> 2) - 1 == line((MID_W, group))) & (line((MID_W, group)) < 10)
    pool = jnp.where(pool, 1.0 / 16, 0.0).astype(BF16)
    for i in range(ENC_H // 4):
        mid_in[i * MID_W : (i + 1) * MID_W] = dot(pool, done[i * group : (i + 1) * group])

    mid = mid_in[...]
    normed = rms_scale(mid, gains[1:2].astype(F32))
    at = line(mid.shape)
    row = row_at * (TILE_H // 4) - 1 + at // MID_W
    col = col_at * (TILE_W // 4) - 1 + at % MID_W
    inside = (row >= 0) & (row < image_rows * (TILE_H // 4))
    inside = inside & (col >= 0) & (col < TILE_COLS * (TILE_W // 4))
    normed = jnp.where(inside, normed, 0.0)
    mid_taps[:, :DEPTH] = pltpu.roll(normed, 1, 0).astype(BF16)
    mid_taps[:, DEPTH : 2 * DEPTH] = normed.astype(BF16)
    mid_taps[:, 2 * DEPTH :] = pltpu.roll(normed, mid.shape[0] - 1, 0).astype(BF16)
    conv = 0.0
    for dy in range(3):
        conv += dot(mid_taps[dy * MID_W : (dy + 4) * MID_W], conv_mid[dy])
    enc_mid = mid[MID_W : 5 * MID_W] + silu(conv)
    high = enc_mid.astype(BF16)
    low = (enc_mid - high.astype(F32)).astype(BF16)

    shape = (CELLS, 4 * MID_W)
    cell = line(shape)
    spread = (cell >> 7) * MID_W + ((cell & (TILE_W - 1)) >> 2) + 1
    spread = ones_where(column(shape) == spread)
    centre = enc[HALO - 1 : HALO - 1 + TILE_H, SIDE : SIDE + TILE_W]
    partial = centre.reshape(CELLS, DEPTH) + (dot(spread, high) + dot(spread, low))
    partial_ref[...] = partial

    x = column((16, 4 * MID_W)) % MID_W - 1
    pool = (x >= 0) & (x < 8) & ((x >> 2) == line((16, 4 * MID_W)))
    pool = jnp.where(pool, 1.0 / 16, 0.0).astype(BF16)
    coarse = dot(pool, high) + dot(pool, low)
    pairs, readings = arrived.shape[0], arrived.shape[1] // 3
    partial = partial.astype(BF16)
    for half in range(2):
        at = 2 * readings + 2 * half
        pixel = arrived[:, at : at + 1].astype(F32) * 16 + arrived[:, at + 1 : at + 2].astype(F32)
        hot = ones_where(column((pairs, CELLS)) == pixel.astype(jnp.int32))
        parcel[:, half * DEPTH : (half + 1) * DEPTH] = dot(hot, partial).astype(BF16)
    even = line((pairs, DEPTH)) % 2 == 0
    parcel[:, 2 * DEPTH :] = jnp.where(even, coarse[0:1], coarse[1:2]).astype(BF16)


def tail_kernel(
    returned, conv_coarse, gains, partial, film, lookup, out_proj, projector,
    maps_ref, scores_ref,
    taps, maps, scores, sems,
):
    cells, wide = returned.shape[0], TILE_COLS * 2
    coarse = returned[:, 2 * DEPTH :].astype(F32)
    normed = rms_scale(coarse, gains[2:3].astype(F32))
    col = line(coarse.shape) % wide
    taps[:wide] = jnp.zeros((wide, 3 * DEPTH), BF16)
    taps[wide + cells :] = jnp.zeros((wide, 3 * DEPTH), BF16)
    inner = slice(wide, wide + cells)
    left, right = pltpu.roll(normed, 1, 0), pltpu.roll(normed, cells - 1, 0)
    taps[inner, :DEPTH] = jnp.where(col == 0, 0.0, left).astype(BF16)
    taps[inner, DEPTH : 2 * DEPTH] = normed.astype(BF16)
    taps[inner, 2 * DEPTH :] = jnp.where(col == wide - 1, 0.0, right).astype(BF16)
    conv = 0.0
    for dy in range(3):
        conv += dot(taps[dy * wide : dy * wide + cells], conv_coarse[dy])
    context = coarse + silu(conv)
    high = context.astype(BF16)
    low = (context - high.astype(F32)).astype(BF16)

    gain = gains[3:4].astype(F32)
    lead, at = lax.axis_index("lead"), line((8, DEPTH))
    scale = 1.0 + jnp.sum(jnp.where(at == lead, film[...], 0.0), axis=0, keepdims=True)
    shift = jnp.sum(jnp.where(at == lead + 4, film[...], 0.0), axis=0, keepdims=True)

    def decode(values):
        hidden = rms_scale(values, gain) * scale + shift
        return (values + dot(silu(hidden).astype(BF16), out_proj[...])).astype(BF16)

    row_at, col_at = grid_place()
    here = row_at * wide + col_at * 2 + ((line((CELLS, cells)) & (TILE_W - 1)) >> 4)
    mine = ones_where(column((CELLS, cells)) == here)
    spread = dot(mine, high) + dot(mine, low)
    maps[...] = decode(partial[...] + spread)
    put_maps = pltpu.make_async_copy(maps, maps_ref, sems.at[0])
    put_maps.start()

    count = lookup.shape[1]
    same = ones_where(line((count, count)) == column((count, count)))
    where = dot_rows(same, lookup[...])
    key = (where[:, 0:1] * 16 + where[:, 1:2]).astype(jnp.int32)
    area = (where[:, 2:3] * 16 + where[:, 3:4]).astype(jnp.int32)
    slot = column((count, cells))
    pick = ones_where(slot == area)
    at_stations = dot(pick, high) + dot(pick, low)
    for half in range(2):
        found = returned[:, half * DEPTH : (half + 1) * DEPTH]
        at_stations += dot(ones_where(slot + half * cells == key), found)
    scores[...] = dot(decode(at_stations), projector[...]).astype(BF16)
    put_scores = pltpu.make_async_copy(scores, scores_ref, sems.at[1])
    put_scores.start()
    put_maps.wait()
    put_scores.wait()


def call(kernel, outs, scratch, operands, hbm_outs=(), scalars=0, megabytes=4):
    vmem = pl.BlockSpec(memory_space=pltpu.VMEM)
    hbm = pl.BlockSpec(memory_space=pltpu.HBM)
    smem = pl.BlockSpec(memory_space=pltpu.SMEM)
    return pl.pallas_call(
        kernel,
        out_shape=[jax.ShapeDtypeStruct(shape, dtype) for shape, dtype in outs],
        in_specs=[smem] * scalars + [vmem] * (len(operands) - scalars),
        out_specs=[hbm if i in hbm_outs else vmem for i in range(len(outs))],
        scratch_shapes=scratch,
        compiler_params=pltpu.CompilerParams(vmem_limit_bytes=megabytes * 2**20),
    )(*operands)


def pack(records, space_count):
    count, width = records.shape
    outs = [((2 * space_count, width // 2 * 3), BF16), ((16, count), BF16)]
    return call(pack_kernel, outs, [], [records], megabytes=8)


def inject(steps, arrived, embed, tiles, film_table):
    return call(
        inject_kernel,
        [
            ((TILE_H, TILE_W, DEPTH), F32),
            ((TILE_H, SIDE, DEPTH), BF16),
            ((TILE_H, SIDE, DEPTH), BF16),
            ((HALO, TILE_W, DEPTH), BF16),
            ((HALO, TILE_W, DEPTH), BF16),
            ((8, DEPTH), F32),
        ],
        [],
        [steps, arrived, embed, tiles, film_table],
        scalars=1,
        megabytes=8,
    )


def widen(west, east, first_rows, last_rows):
    shape = (HALO, FRAME_W, DEPTH)
    return call(
        widen_kernel, [(shape, BF16), (shape, BF16)], [], [west, east, first_rows, last_rows]
    )


def trunk(image_rows, north, south, west, east, own, film, conv_fine, conv_mid, gains, arrived):
    return call(
        functools.partial(trunk_kernel, image_rows),
        [((CELLS, DEPTH), F32), ((arrived.shape[0], 3 * DEPTH), BF16), ((8, DEPTH), F32)],
        [
            pltpu.VMEM((FRAME_H, FRAME_W, DEPTH), F32),
            pltpu.VMEM((FRAME_H * FRAME_W, 3 * DEPTH), BF16),
            pltpu.VMEM((ENC_H, FRAME_W, DEPTH), F32),
            pltpu.VMEM((ENC_H // 4 * MID_W, DEPTH), F32),
            pltpu.VMEM((ENC_H // 4 * MID_W, 3 * DEPTH), BF16),
        ],
        [
            north, south, west, east, own, film,
            conv_fine.reshape(3, 3 * DEPTH, DEPTH),
            conv_mid.reshape(3, 3 * DEPTH, DEPTH),
            gains, arrived,
        ],
        megabytes=16,
    )


def tail(returned, conv_coarse, gains, partial, film, lookup, out_proj, projector):
    cells = returned.shape[0]
    outs = [((CELLS, DEPTH), BF16), ((lookup.shape[1], projector.shape[1]), BF16)]
    return call(
        tail_kernel,
        outs,
        [
            pltpu.VMEM((cells + 4 * TILE_COLS, 3 * DEPTH), BF16),
            *[pltpu.VMEM(shape, dtype) for shape, dtype in outs],
            pltpu.SemaphoreType.DMA((2,)),
        ],
        [
            returned, conv_coarse.reshape(3, 3 * DEPTH, DEPTH), gains,
            partial, film, lookup, out_proj, projector,
        ],
        hbm_outs=(0, 1),
        megabytes=16,
    )


def shifted(value, row_step, col_step, lead_step):
    rows, leads = lax.axis_size("space") // TILE_COLS, lax.axis_size("lead")
    pairs = []
    for row in range(rows):
        for col in range(TILE_COLS):
            for lead in range(leads):
                source = (row * TILE_COLS + col) * leads + lead
                there = (row + row_step) % rows * TILE_COLS + (col + col_step) % TILE_COLS
                pairs.append((source, there * leads + (lead - lead_step) % leads))
    return lax.ppermute(value, ("space", "lead"), pairs)


def body(
    tiles,
    station_obs,
    station_tile,
    station_pixel,
    station_embed,
    conv_fine,
    conv_mid,
    conv_coarse,
    norm_gains,
    film_table,
    horizon_step_list,
    out_proj,
    gauge_bin_projector,
):
    space_count = lax.axis_size("space")
    count, readings = station_obs.shape
    records = jnp.concatenate(
        [
            station_obs,
            station_tile.astype(BF16),
            (station_pixel // 16).astype(BF16)[:, None],
            (station_pixel % 16).astype(BF16)[:, None],
            jnp.zeros((count, readings - 3), BF16),
        ],
        axis=1,
    )
    payload, lookup = pack(records, space_count)
    arrived = lax.all_to_all(
        payload.reshape(space_count, 2, 3 * readings), "space", 0, 0, tiled=True
    ).reshape(2 * space_count, 3 * readings)
    own, first_cols, last_cols, first_rows, last_rows, film = inject(
        horizon_step_list, arrived, station_embed, tiles.reshape(CELLS, DEPTH), film_table
    )

    west = shifted(last_cols, 0, 1, 1)
    east = shifted(first_cols, 0, -1, -1)
    top, bottom = widen(west, east, first_rows, last_rows)
    north = shifted(bottom, 1, 0, 1)
    south = shifted(top, -1, 0, 0)

    partial, parcel, film = trunk(
        space_count // TILE_COLS,
        north, south, west, east, own, film, conv_fine, conv_mid, norm_gains, arrived,
    )
    returned = lax.all_to_all(
        parcel.reshape(space_count, 2, 3 * DEPTH), "space", 0, 0, tiled=True
    ).reshape(2 * space_count, 3 * DEPTH)

    maps, scores = tail(
        returned, conv_coarse, norm_gains, partial, film, lookup, out_proj, gauge_bin_projector
    )
    return maps.reshape(1, 1, TILE_H, TILE_W, DEPTH), scores.reshape(1, count, -1)


def solution(mesh):
    in_specs = (
        P("space", None, None, None),
        P("space", None),
        P("space", None),
        P("space"),
        P(),
        P(),
        P(),
        P(),
        P(),
        P("lead", None),
        P(),
        P(),
        P(),
    )
    out_specs = (P("lead", "space", None, None, None), P("lead", "space", None))
    return jax.shard_map(body, mesh=mesh, in_specs=in_specs, out_specs=out_specs, check_vma=False)
```

```python
import functools

import jax
import jax.numpy as jnp
from jax import lax
from jax.experimental import pallas as pl
from jax.experimental.pallas import tpu as pltpu
from jax.sharding import PartitionSpec as P

TILE_COLS = 8
TILE_H, TILE_W, DEPTH = 16, 32, 256
CELLS = TILE_H * TILE_W
EPS = 1e-06
HALO = 5
SIDE = 8
FRAME_H, FRAME_W = TILE_H + 2 * HALO, TILE_W + 2 * SIDE
ENC_H = FRAME_H - 2
MID_W = 16
F32 = jnp.float32
BF16 = jnp.bfloat16


def dot(a, b):
    return jnp.dot(a, b, preferred_element_type=F32)


def dot_rows(a, b):
    return lax.dot_general(a, b, (((1,), (1,)), ((), ())), preferred_element_type=F32)


def silu(v):
    return v / (1.0 + jnp.exp(-v))


def rms_scale(values, gain):
    mean_sq = jnp.mean(values * values, axis=-1, keepdims=True)
    return values * lax.rsqrt(mean_sq + EPS) * gain


def column(shape):
    return lax.broadcasted_iota(jnp.int32, shape, 1)


def line(shape):
    return lax.broadcasted_iota(jnp.int32, shape, 0)


def ones_where(condition):
    return condition.astype(F32).astype(BF16)


def grid_place():
    at = lax.axis_index("space")
    return lax.div(at, TILE_COLS), lax.rem(at, TILE_COLS)


def pack_kernel(records, payload, lookup):
    count, readings = records.shape[0], records.shape[1] // 2
    pairs = payload.shape[0]
    obs = records[:, :readings]
    earlier = ones_where(line((count, count)) < column((count, count)))
    sort, lane = line((16, readings)), column((16, readings))
    weights = jnp.where((sort == 1) & (lane == 1), 16.0, 0.0)
    weights = jnp.where((sort == 0) & (lane == 0) | (sort == 1) & (lane == 2), 1.0, weights)
    ids = dot_rows(weights.astype(BF16), records[:, readings:]).astype(jnp.int32)
    dest, pixel = ids[0:1], ids[1:2]
    lane = column((pairs, readings))
    hot = (line((pairs // 2, count)) == dest).astype(F32)
    prior = dot(hot.astype(BF16), earlier)
    position = jnp.sum(prior * hot, axis=0, keepdims=True).astype(jnp.int32)
    key = dest * 2 + (position & 1) + pairs * (position >> 1)
    coarse = dest * 2 + ((pixel & (TILE_W - 1)) >> 4)
    sort = line((16, count))
    found = jnp.where(sort == 0, key >> 4, jnp.where(sort == 1, key & 15, 0))
    found = jnp.where(sort == 2, coarse >> 4, jnp.where(sort == 3, coarse & 15, found))
    lookup[...] = found.astype(F32).astype(BF16)
    places = jnp.zeros((pairs, readings), jnp.int32)
    for half in range(2):
        match = line((pairs, count)) + half * pairs == key
        sent = dot(ones_where(match), obs)
        payload[:, half * readings : (half + 1) * readings] = sent.astype(BF16)
        at = jnp.sum(jnp.where(match, pixel, 0), axis=1, keepdims=True)
        places = jnp.where(lane == 2 * half, at >> 4, places)
        places = jnp.where(lane == 2 * half + 1, at & 15, places)
    payload[:, 2 * readings :] = places.astype(F32).astype(BF16)


def inject_kernel(
    steps, arrived, embed, tiles, film_table,
    own, first_rows, last_rows, film,
):
    pairs = arrived.shape[0]
    readings = embed.shape[0]
    weight = embed[...]
    sort, lane = line((8, readings)), column((8, readings))
    weights = jnp.where(lane == 2 * sort, 16.0, jnp.where(lane == 2 * sort + 1, 1.0, 0.0))
    weights = jnp.where(sort < 2, weights, 0.0).astype(BF16)
    pixels = dot_rows(weights, arrived[:, 2 * readings :]).astype(jnp.int32)
    fine = 0.0
    for half in range(2):
        embedded = dot(arrived[:, half * readings : (half + 1) * readings], weight)
        hot = ones_where(line((CELLS, pairs)) == pixels[half : half + 1])
        fine += dot(hot, embedded.astype(BF16))
    fine = (fine + tiles[...].astype(F32)).reshape(TILE_H, TILE_W, DEPTH)
    own[...] = fine
    table_rows = film_table.shape[0]
    offset = lax.axis_index("lead") * table_rows
    sort = line((8, table_rows))
    at = jnp.full((8, table_rows), -1, jnp.int32)
    for i in range(4):
        at = jnp.where((sort & 3) == i, steps[i] - offset, at)
    hot = ones_where(column((8, table_rows)) == at)
    both = dot(hot, film_table[...])
    rows = jnp.where(line((8, DEPTH)) < 4, both[:, :DEPTH], both[:, DEPTH:])
    film[...] = rows
    extra = jnp.concatenate([rows, jnp.zeros((TILE_W - 8, DEPTH), F32)], axis=0).astype(BF16)
    for target, start in ((first_rows, 0), (last_rows, TILE_H - HALO)):
        target[:HALO] = fine[start : start + HALO].astype(BF16)
        target[HALO] = extra


def brought_film(north, south, col_at):
    rows = north[HALO, :8].astype(F32)
    return rows + jnp.where(lax.rem(col_at, 2) == 0, south[HALO, :8].astype(F32), 0.0)


def widen_kernel(image_rows, north, south, own, first_cols, last_cols):
    row_at, col_at = grid_place()
    film = brought_film(north, south, col_at)
    at = line((SIDE, DEPTH))
    for y in range(FRAME_H):
        for target, cols in (
            (first_cols, slice(0, SIDE)),
            (last_cols, slice(TILE_W - SIDE, TILE_W)),
        ):
            if y < HALO:
                rows = jnp.where(row_at > 0, north[y, cols].astype(F32), 0.0)
            elif y < HALO + TILE_H:
                rows = own[y - HALO, cols]
            else:
                rows = south[y - HALO - TILE_H, cols].astype(F32)
                rows = jnp.where(row_at < image_rows - 1, rows, 0.0)
            if y < 8 and target is last_cols:
                rows = jnp.where(at == 0, film[y : y + 1], rows)
            target[y] = rows.astype(BF16)


def trunk_kernel(
    image_rows,
    north, south, west, east, own, film, conv_fine, conv_mid, gains, arrived,
    partial_ref, parcel, film_ref,
    frame, taps, enc, mid_in, mid_taps,
):
    row_at, col_at = grid_place()
    left = west[...].astype(F32)
    at = line((8, DEPTH))
    rows = film[...] + brought_film(north, south, col_at)
    for y in range(8):
        rows += jnp.where(at == y, left[y, 0:1], 0.0)
    film_ref[...] = rows
    above, below = north[:HALO].astype(F32), south[:HALO].astype(F32)
    inner = slice(SIDE, SIDE + TILE_W)
    frame[:HALO, inner] = jnp.where(row_at > 0, above, 0.0)
    frame[HALO : HALO + TILE_H, inner] = own[...]
    frame[HALO + TILE_H :, inner] = jnp.where(row_at < image_rows - 1, below, 0.0)
    frame[:, :SIDE] = jnp.where(col_at > 0, left, 0.0)
    frame[:, SIDE + TILE_W :] = jnp.where(col_at < TILE_COLS - 1, east[...].astype(F32), 0.0)
    gain = gains[0:1].astype(F32)
    for y in range(FRAME_H):
        normed = rms_scale(frame[y], gain)
        rows = slice(y * FRAME_W, (y + 1) * FRAME_W)
        taps[rows, :DEPTH] = pltpu.roll(normed, 1, 0).astype(BF16)
        taps[rows, DEPTH : 2 * DEPTH] = normed.astype(BF16)
        taps[rows, 2 * DEPTH :] = pltpu.roll(normed, FRAME_W - 1, 0).astype(BF16)
    size = ENC_H * FRAME_W
    conv = 0.0
    for dy in range(3):
        conv += dot(taps[dy * FRAME_W : dy * FRAME_W + size], conv_fine[dy])
    done = (frame[1 : 1 + ENC_H].reshape(size, DEPTH) + silu(conv)).astype(BF16)
    enc[...] = done.astype(F32).reshape(ENC_H, FRAME_W, DEPTH)
    group = 4 * FRAME_W
    at = column((MID_W, group))
    x = at - FRAME_W * sum((at >= FRAME_W * i).astype(jnp.int32) for i in range(1, 4))
    pool = ((x >> 2) - 1 == line((MID_W, group))) & (line((MID_W, group)) < 10)
    pool = jnp.where(pool, 1.0 / 16, 0.0).astype(BF16)
    for i in range(ENC_H // 4):
        mid_in[i * MID_W : (i + 1) * MID_W] = dot(pool, done[i * group : (i + 1) * group])

    mid = mid_in[...]
    normed = rms_scale(mid, gains[1:2].astype(F32))
    at = line(mid.shape)
    row = row_at * (TILE_H // 4) - 1 + at // MID_W
    col = col_at * (TILE_W // 4) - 1 + at % MID_W
    inside = (row >= 0) & (row < image_rows * (TILE_H // 4))
    inside = inside & (col >= 0) & (col < TILE_COLS * (TILE_W // 4))
    normed = jnp.where(inside, normed, 0.0)
    mid_taps[:, :DEPTH] = pltpu.roll(normed, 1, 0).astype(BF16)
    mid_taps[:, DEPTH : 2 * DEPTH] = normed.astype(BF16)
    mid_taps[:, 2 * DEPTH :] = pltpu.roll(normed, mid.shape[0] - 1, 0).astype(BF16)
    conv = 0.0
    for dy in range(3):
        conv += dot(mid_taps[dy * MID_W : (dy + 4) * MID_W], conv_mid[dy])
    enc_mid = mid[MID_W : 5 * MID_W] + silu(conv)
    high = enc_mid.astype(BF16)
    low = (enc_mid - high.astype(F32)).astype(BF16)

    shape = (CELLS, 4 * MID_W)
    cell = line(shape)
    spread = (cell >> 7) * MID_W + ((cell & (TILE_W - 1)) >> 2) + 1
    spread = ones_where(column(shape) == spread)
    centre = enc[HALO - 1 : HALO - 1 + TILE_H, SIDE : SIDE + TILE_W]
    partial = centre.reshape(CELLS, DEPTH) + (dot(spread, high) + dot(spread, low))
    partial_ref[...] = partial

    x = column((16, 4 * MID_W)) % MID_W - 1
    pool = (x >= 0) & (x < 8) & ((x >> 2) == line((16, 4 * MID_W)))
    pool = jnp.where(pool, 1.0 / 16, 0.0).astype(BF16)
    coarse = dot(pool, high) + dot(pool, low)
    pairs, readings = arrived.shape[0], arrived.shape[1] // 3
    partial = partial.astype(BF16)
    for half in range(2):
        at = 2 * readings + 2 * half
        pixel = arrived[:, at : at + 1].astype(F32) * 16 + arrived[:, at + 1 : at + 2].astype(F32)
        hot = ones_where(column((pairs, CELLS)) == pixel.astype(jnp.int32))
        parcel[:, half * DEPTH : (half + 1) * DEPTH] = dot(hot, partial).astype(BF16)
    even = line((pairs, DEPTH)) % 2 == 0
    parcel[:, 2 * DEPTH :] = jnp.where(even, coarse[0:1], coarse[1:2]).astype(BF16)


def tail_kernel(
    returned, conv_coarse, gains, partial, film, lookup, out_proj, projector,
    maps_ref, scores_ref,
    taps, maps, scores, sems,
):
    cells, wide = returned.shape[0], TILE_COLS * 2
    coarse = returned[:, 2 * DEPTH :].astype(F32)
    normed = rms_scale(coarse, gains[2:3].astype(F32))
    col = line(coarse.shape) % wide
    taps[:wide] = jnp.zeros((wide, 3 * DEPTH), BF16)
    taps[wide + cells :] = jnp.zeros((wide, 3 * DEPTH), BF16)
    inner = slice(wide, wide + cells)
    left, right = pltpu.roll(normed, 1, 0), pltpu.roll(normed, cells - 1, 0)
    taps[inner, :DEPTH] = jnp.where(col == 0, 0.0, left).astype(BF16)
    taps[inner, DEPTH : 2 * DEPTH] = normed.astype(BF16)
    taps[inner, 2 * DEPTH :] = jnp.where(col == wide - 1, 0.0, right).astype(BF16)
    conv = 0.0
    for dy in range(3):
        conv += dot(taps[dy * wide : dy * wide + cells], conv_coarse[dy])
    context = coarse + silu(conv)
    high = context.astype(BF16)
    low = (context - high.astype(F32)).astype(BF16)

    gain = gains[3:4].astype(F32)
    lead, at = lax.axis_index("lead"), line((8, DEPTH))
    scale = 1.0 + jnp.sum(jnp.where(at == lead, film[...], 0.0), axis=0, keepdims=True)
    shift = jnp.sum(jnp.where(at == lead + 4, film[...], 0.0), axis=0, keepdims=True)

    def decode(values):
        hidden = rms_scale(values, gain) * scale + shift
        return (values + dot(silu(hidden).astype(BF16), out_proj[...])).astype(BF16)

    row_at, col_at = grid_place()
    here = row_at * wide + col_at * 2 + ((line((CELLS, cells)) & (TILE_W - 1)) >> 4)
    mine = ones_where(column((CELLS, cells)) == here)
    spread = dot(mine, high) + dot(mine, low)
    maps[...] = decode(partial[...] + spread)
    put_maps = pltpu.make_async_copy(maps, maps_ref, sems.at[0])
    put_maps.start()

    count = lookup.shape[1]
    same = ones_where(line((count, count)) == column((count, count)))
    where = dot_rows(same, lookup[...])
    key = (where[:, 0:1] * 16 + where[:, 1:2]).astype(jnp.int32)
    area = (where[:, 2:3] * 16 + where[:, 3:4]).astype(jnp.int32)
    slot = column((count, cells))
    pick = ones_where(slot == area)
    at_stations = dot(pick, high) + dot(pick, low)
    for half in range(2):
        found = returned[:, half * DEPTH : (half + 1) * DEPTH]
        at_stations += dot(ones_where(slot + half * cells == key), found)
    scores[...] = dot(decode(at_stations), projector[...]).astype(BF16)
    put_scores = pltpu.make_async_copy(scores, scores_ref, sems.at[1])
    put_scores.start()
    put_maps.wait()
    put_scores.wait()


def call(kernel, outs, scratch, operands, hbm_outs=(), scalars=0, megabytes=4):
    vmem = pl.BlockSpec(memory_space=pltpu.VMEM)
    hbm = pl.BlockSpec(memory_space=pltpu.HBM)
    smem = pl.BlockSpec(memory_space=pltpu.SMEM)
    return pl.pallas_call(
        kernel,
        out_shape=[jax.ShapeDtypeStruct(shape, dtype) for shape, dtype in outs],
        in_specs=[smem] * scalars + [vmem] * (len(operands) - scalars),
        out_specs=[hbm if i in hbm_outs else vmem for i in range(len(outs))],
        scratch_shapes=scratch,
        compiler_params=pltpu.CompilerParams(vmem_limit_bytes=megabytes * 2**20),
    )(*operands)


def pack(records, space_count):
    count, width = records.shape
    outs = [((2 * space_count, width // 2 * 3), BF16), ((16, count), BF16)]
    return call(pack_kernel, outs, [], [records], megabytes=8)


def inject(steps, arrived, embed, tiles, film_table):
    return call(
        inject_kernel,
        [
            ((TILE_H, TILE_W, DEPTH), F32),
            ((HALO + 1, TILE_W, DEPTH), BF16),
            ((HALO + 1, TILE_W, DEPTH), BF16),
            ((8, DEPTH), F32),
        ],
        [],
        [steps, arrived, embed, tiles, film_table],
        scalars=1,
        megabytes=8,
    )


def widen(image_rows, north, south, own):
    shape = (FRAME_H, SIDE, DEPTH)
    return call(
        functools.partial(widen_kernel, image_rows),
        [(shape, BF16), (shape, BF16)],
        [],
        [north, south, own],
    )


def trunk(image_rows, north, south, west, east, own, film, conv_fine, conv_mid, gains, arrived):
    return call(
        functools.partial(trunk_kernel, image_rows),
        [((CELLS, DEPTH), F32), ((arrived.shape[0], 3 * DEPTH), BF16), ((8, DEPTH), F32)],
        [
            pltpu.VMEM((FRAME_H, FRAME_W, DEPTH), F32),
            pltpu.VMEM((FRAME_H * FRAME_W, 3 * DEPTH), BF16),
            pltpu.VMEM((ENC_H, FRAME_W, DEPTH), F32),
            pltpu.VMEM((ENC_H // 4 * MID_W, DEPTH), F32),
            pltpu.VMEM((ENC_H // 4 * MID_W, 3 * DEPTH), BF16),
        ],
        [
            north, south, west, east, own, film,
            conv_fine.reshape(3, 3 * DEPTH, DEPTH),
            conv_mid.reshape(3, 3 * DEPTH, DEPTH),
            gains, arrived,
        ],
        megabytes=16,
    )


def tail(returned, conv_coarse, gains, partial, film, lookup, out_proj, projector):
    cells = returned.shape[0]
    outs = [((CELLS, DEPTH), BF16), ((lookup.shape[1], projector.shape[1]), BF16)]
    return call(
        tail_kernel,
        outs,
        [
            pltpu.VMEM((cells + 4 * TILE_COLS, 3 * DEPTH), BF16),
            *[pltpu.VMEM(shape, dtype) for shape, dtype in outs],
            pltpu.SemaphoreType.DMA((2,)),
        ],
        [
            returned, conv_coarse.reshape(3, 3 * DEPTH, DEPTH), gains,
            partial, film, lookup, out_proj, projector,
        ],
        hbm_outs=(0, 1),
        megabytes=16,
    )


def shifted(value, row_step, col_step, lead_steps=(0, 0)):
    rows, leads = lax.axis_size("space") // TILE_COLS, lax.axis_size("lead")
    pairs = []
    for row in range(rows):
        for col in range(TILE_COLS):
            for lead in range(leads):
                source = (row * TILE_COLS + col) * leads + lead
                there = (row + row_step) % rows * TILE_COLS + (col + col_step) % TILE_COLS
                pairs.append((source, there * leads + (lead - lead_steps[col % 2]) % leads))
    return lax.ppermute(value, ("space", "lead"), pairs)


def body(
    tiles,
    station_obs,
    station_tile,
    station_pixel,
    station_embed,
    conv_fine,
    conv_mid,
    conv_coarse,
    norm_gains,
    film_table,
    horizon_step_list,
    out_proj,
    gauge_bin_projector,
):
    space_count = lax.axis_size("space")
    count, readings = station_obs.shape
    records = jnp.concatenate(
        [
            station_obs,
            station_tile.astype(BF16),
            (station_pixel // 16).astype(BF16)[:, None],
            (station_pixel % 16).astype(BF16)[:, None],
            jnp.zeros((count, readings - 3), BF16),
        ],
        axis=1,
    )
    payload, lookup = pack(records, space_count)
    arrived = lax.all_to_all(
        payload.reshape(space_count, 2, 3 * readings), "space", 0, 0, tiled=True
    ).reshape(2 * space_count, 3 * readings)
    own, first_rows, last_rows, film = inject(
        horizon_step_list, arrived, station_embed, tiles.reshape(CELLS, DEPTH), film_table
    )

    image_rows = space_count // TILE_COLS
    north = shifted(last_rows, 1, 0, (1, 2))
    south = shifted(first_rows, -1, 0, (-1, 0))
    first_cols, last_cols = widen(image_rows, north, south, own)
    west = shifted(last_cols, 0, 1)
    east = shifted(first_cols, 0, -1)

    partial, parcel, film = trunk(
        image_rows,
        north, south, west, east, own, film, conv_fine, conv_mid, norm_gains, arrived,
    )
    returned = lax.all_to_all(
        parcel.reshape(space_count, 2, 3 * DEPTH), "space", 0, 0, tiled=True
    ).reshape(2 * space_count, 3 * DEPTH)

    maps, scores = tail(
        returned, conv_coarse, norm_gains, partial, film, lookup, out_proj, gauge_bin_projector
    )
    return maps.reshape(1, 1, TILE_H, TILE_W, DEPTH), scores.reshape(1, count, -1)


def solution(mesh):
    in_specs = (
        P("space", None, None, None),
        P("space", None),
        P("space", None),
        P("space"),
        P(),
        P(),
        P(),
        P(),
        P(),
        P("lead", None),
        P(),
        P(),
        P(),
    )
    out_specs = (P("lead", "space", None, None, None), P("lead", "space", None))
    return jax.shard_map(body, mesh=mesh, in_specs=in_specs, out_specs=out_specs, check_vma=False)
```

```python
import functools

import jax
import jax.numpy as jnp
from jax import lax
from jax.experimental import pallas as pl
from jax.experimental.pallas import tpu as pltpu
from jax.sharding import PartitionSpec as P

TILE_COLS = 8
TILE_H, TILE_W, DEPTH = 16, 32, 256
CELLS = TILE_H * TILE_W
EPS = 1e-06
HALO = 5
SIDE = 8
FRAME_H, FRAME_W = TILE_H + 2 * HALO, TILE_W + 2 * SIDE
ENC_H = FRAME_H - 2
MID_W = 16
F32 = jnp.float32
BF16 = jnp.bfloat16


def dot(a, b):
    return jnp.dot(a, b, preferred_element_type=F32)


def dot_rows(a, b):
    return lax.dot_general(a, b, (((1,), (1,)), ((), ())), preferred_element_type=F32)


def silu(v):
    return v / (1.0 + jnp.exp(-v))


def rms_scale(values, gain):
    mean_sq = jnp.mean(values * values, axis=-1, keepdims=True)
    return values * lax.rsqrt(mean_sq + EPS) * gain


def column(shape):
    return lax.broadcasted_iota(jnp.int32, shape, 1)


def line(shape):
    return lax.broadcasted_iota(jnp.int32, shape, 0)


def ones_where(condition):
    return condition.astype(F32).astype(BF16)


def grid_place():
    at = lax.axis_index("space")
    return lax.div(at, TILE_COLS), lax.rem(at, TILE_COLS)


def pack_kernel(records, payload, lookup):
    count, readings = records.shape[0], records.shape[1] // 2
    pairs = payload.shape[0]
    obs = records[:, :readings]
    earlier = ones_where(line((count, count)) < column((count, count)))
    sort, lane = line((16, readings)), column((16, readings))
    weights = jnp.where((sort == 1) & (lane == 1), 16.0, 0.0)
    weights = jnp.where((sort == 0) & (lane == 0) | (sort == 1) & (lane == 2), 1.0, weights)
    ids = dot_rows(weights.astype(BF16), records[:, readings:]).astype(jnp.int32)
    dest, pixel = ids[0:1], ids[1:2]
    lane = column((pairs, readings))
    hot = (line((pairs // 2, count)) == dest).astype(F32)
    prior = dot(hot.astype(BF16), earlier)
    position = jnp.sum(prior * hot, axis=0, keepdims=True).astype(jnp.int32)
    key = dest * 2 + (position & 1) + pairs * (position >> 1)
    coarse = dest * 2 + ((pixel & (TILE_W - 1)) >> 4)
    sort = line((16, count))
    found = jnp.where(sort == 0, key >> 4, jnp.where(sort == 1, key & 15, 0))
    found = jnp.where(sort == 2, coarse >> 4, jnp.where(sort == 3, coarse & 15, found))
    lookup[...] = found.astype(F32).astype(BF16)
    places = jnp.zeros((pairs, readings), jnp.int32)
    for half in range(2):
        match = line((pairs, count)) + half * pairs == key
        sent = dot(ones_where(match), obs)
        payload[:, half * readings : (half + 1) * readings] = sent.astype(BF16)
        at = jnp.sum(jnp.where(match, pixel, 0), axis=1, keepdims=True)
        places = jnp.where(lane == 2 * half, at >> 4, places)
        places = jnp.where(lane == 2 * half + 1, at & 15, places)
    payload[:, 2 * readings :] = places.astype(F32).astype(BF16)


def inject_kernel(
    steps, arrived, embed, tiles, film_table,
    own, first_rows, last_rows, film,
):
    pairs = arrived.shape[0]
    readings = embed.shape[0]
    weight = embed[...]
    sort, lane = line((8, readings)), column((8, readings))
    weights = jnp.where(lane == 2 * sort, 16.0, jnp.where(lane == 2 * sort + 1, 1.0, 0.0))
    weights = jnp.where(sort < 2, weights, 0.0).astype(BF16)
    pixels = dot_rows(weights, arrived[:, 2 * readings :]).astype(jnp.int32)
    fine = 0.0
    for half in range(2):
        embedded = dot(arrived[:, half * readings : (half + 1) * readings], weight)
        hot = ones_where(line((CELLS, pairs)) == pixels[half : half + 1])
        fine += dot(hot, embedded.astype(BF16))
    fine = (fine + tiles[...].astype(F32)).reshape(TILE_H, TILE_W, DEPTH)
    own[...] = fine
    table_rows = film_table.shape[0]
    offset = lax.axis_index("lead") * table_rows
    sort = line((8, table_rows))
    at = jnp.full((8, table_rows), -1, jnp.int32)
    for i in range(4):
        at = jnp.where((sort & 3) == i, steps[0:1, i : i + 1] - offset, at)
    hot = ones_where(column((8, table_rows)) == at)
    both = dot(hot, film_table[...])
    rows = jnp.where(line((8, DEPTH)) < 4, both[:, :DEPTH], both[:, DEPTH:])
    film[...] = rows
    for target, start in ((first_rows, 0), (last_rows, TILE_H - HALO)):
        edge = fine[start : start + HALO].reshape(HALO * TILE_W, DEPTH)
        target[...] = jnp.concatenate([edge, rows], axis=0).astype(BF16)


def brought_film(north, south, col_at):
    above, below = (rows[HALO * TILE_W :].astype(F32) for rows in (north, south))
    return above + jnp.where(lax.rem(col_at, 2) == 0, below, 0.0)


def widen_kernel(image_rows, north, south, own, first_cols, last_cols):
    row_at, col_at = grid_place()
    film = brought_film(north, south, col_at)
    at = line((SIDE, DEPTH))
    for y in range(FRAME_H):
        for target, cols in (
            (first_cols, slice(0, SIDE)),
            (last_cols, slice(TILE_W - SIDE, TILE_W)),
        ):
            start = y % (HALO + TILE_H) * TILE_W + cols.start
            if y < HALO:
                rows = north[start : start + SIDE].astype(F32)
                rows = jnp.where(row_at > 0, rows, 0.0)
            elif y < HALO + TILE_H:
                rows = own[y - HALO, cols]
            else:
                rows = south[start : start + SIDE].astype(F32)
                rows = jnp.where(row_at < image_rows - 1, rows, 0.0)
            if y < 8 and target is last_cols:
                rows = jnp.where(at == 0, film[y : y + 1], rows)
            target[y] = rows.astype(BF16)


def trunk_kernel(
    image_rows,
    north, south, west, east, own, film, conv_fine, conv_mid, gains, arrived,
    partial_ref, parcel, film_ref,
    frame, taps, enc, mid_in, mid_taps,
):
    row_at, col_at = grid_place()
    left = west[...].astype(F32)
    at = line((8, DEPTH))
    rows = film[...] + brought_film(north, south, col_at)
    for y in range(8):
        rows += jnp.where(at == y, left[y, 0:1], 0.0)
    film_ref[...] = rows
    above, below = (
        rows[: HALO * TILE_W].astype(F32).reshape(HALO, TILE_W, DEPTH) for rows in (north, south)
    )
    inner = slice(SIDE, SIDE + TILE_W)
    frame[:HALO, inner] = jnp.where(row_at > 0, above, 0.0)
    frame[HALO : HALO + TILE_H, inner] = own[...]
    frame[HALO + TILE_H :, inner] = jnp.where(row_at < image_rows - 1, below, 0.0)
    frame[:, :SIDE] = jnp.where(col_at > 0, left, 0.0)
    frame[:, SIDE + TILE_W :] = jnp.where(col_at < TILE_COLS - 1, east[...].astype(F32), 0.0)
    gain = gains[0:1].astype(F32)
    for y in range(FRAME_H):
        normed = rms_scale(frame[y], gain)
        rows = slice(y * FRAME_W, (y + 1) * FRAME_W)
        taps[rows, :DEPTH] = pltpu.roll(normed, 1, 0).astype(BF16)
        taps[rows, DEPTH : 2 * DEPTH] = normed.astype(BF16)
        taps[rows, 2 * DEPTH :] = pltpu.roll(normed, FRAME_W - 1, 0).astype(BF16)
    size = ENC_H * FRAME_W
    conv = 0.0
    for dy in range(3):
        conv += dot(taps[dy * FRAME_W : dy * FRAME_W + size], conv_fine[dy])
    done = (frame[1 : 1 + ENC_H].reshape(size, DEPTH) + silu(conv)).astype(BF16)
    enc[...] = done.astype(F32).reshape(ENC_H, FRAME_W, DEPTH)
    group = 4 * FRAME_W
    at = column((MID_W, group))
    x = at - FRAME_W * sum((at >= FRAME_W * i).astype(jnp.int32) for i in range(1, 4))
    pool = ((x >> 2) - 1 == line((MID_W, group))) & (line((MID_W, group)) < 10)
    pool = jnp.where(pool, 1.0 / 16, 0.0).astype(BF16)
    for i in range(ENC_H // 4):
        mid_in[i * MID_W : (i + 1) * MID_W] = dot(pool, done[i * group : (i + 1) * group])

    mid = mid_in[...]
    normed = rms_scale(mid, gains[1:2].astype(F32))
    at = line(mid.shape)
    row = row_at * (TILE_H // 4) - 1 + at // MID_W
    col = col_at * (TILE_W // 4) - 1 + at % MID_W
    inside = (row >= 0) & (row < image_rows * (TILE_H // 4))
    inside = inside & (col >= 0) & (col < TILE_COLS * (TILE_W // 4))
    normed = jnp.where(inside, normed, 0.0)
    mid_taps[:, :DEPTH] = pltpu.roll(normed, 1, 0).astype(BF16)
    mid_taps[:, DEPTH : 2 * DEPTH] = normed.astype(BF16)
    mid_taps[:, 2 * DEPTH :] = pltpu.roll(normed, mid.shape[0] - 1, 0).astype(BF16)
    conv = 0.0
    for dy in range(3):
        conv += dot(mid_taps[dy * MID_W : (dy + 4) * MID_W], conv_mid[dy])
    enc_mid = mid[MID_W : 5 * MID_W] + silu(conv)
    high = enc_mid.astype(BF16)
    low = (enc_mid - high.astype(F32)).astype(BF16)

    shape = (CELLS, 4 * MID_W)
    cell = line(shape)
    spread = (cell >> 7) * MID_W + ((cell & (TILE_W - 1)) >> 2) + 1
    spread = ones_where(column(shape) == spread)
    centre = enc[HALO - 1 : HALO - 1 + TILE_H, SIDE : SIDE + TILE_W]
    partial = centre.reshape(CELLS, DEPTH) + (dot(spread, high) + dot(spread, low))
    partial_ref[...] = partial

    x = column((16, 4 * MID_W)) % MID_W - 1
    pool = (x >= 0) & (x < 8) & ((x >> 2) == line((16, 4 * MID_W)))
    pool = jnp.where(pool, 1.0 / 16, 0.0).astype(BF16)
    coarse = dot(pool, high) + dot(pool, low)
    pairs, readings = arrived.shape[0], arrived.shape[1] // 3
    partial = partial.astype(BF16)
    for half in range(2):
        at = 2 * readings + 2 * half
        pixel = arrived[:, at : at + 1].astype(F32) * 16 + arrived[:, at + 1 : at + 2].astype(F32)
        hot = ones_where(column((pairs, CELLS)) == pixel.astype(jnp.int32))
        parcel[:, half * DEPTH : (half + 1) * DEPTH] = dot(hot, partial).astype(BF16)
    even = line((pairs, DEPTH)) % 2 == 0
    parcel[:, 2 * DEPTH :] = jnp.where(even, coarse[0:1], coarse[1:2]).astype(BF16)


def tail_kernel(
    returned, conv_coarse, gains, partial, film, lookup, out_proj, projector,
    maps_ref, scores_ref,
    taps, maps, scores, sems,
):
    cells, wide = returned.shape[0], TILE_COLS * 2
    coarse = returned[:, 2 * DEPTH :].astype(F32)
    normed = rms_scale(coarse, gains[2:3].astype(F32))
    col = line(coarse.shape) % wide
    taps[:wide] = jnp.zeros((wide, 3 * DEPTH), BF16)
    taps[wide + cells :] = jnp.zeros((wide, 3 * DEPTH), BF16)
    inner = slice(wide, wide + cells)
    left, right = pltpu.roll(normed, 1, 0), pltpu.roll(normed, cells - 1, 0)
    taps[inner, :DEPTH] = jnp.where(col == 0, 0.0, left).astype(BF16)
    taps[inner, DEPTH : 2 * DEPTH] = normed.astype(BF16)
    taps[inner, 2 * DEPTH :] = jnp.where(col == wide - 1, 0.0, right).astype(BF16)
    conv = 0.0
    for dy in range(3):
        conv += dot(taps[dy * wide : dy * wide + cells], conv_coarse[dy])
    context = coarse + silu(conv)
    high = context.astype(BF16)
    low = (context - high.astype(F32)).astype(BF16)

    gain = gains[3:4].astype(F32)
    lead, at = lax.axis_index("lead"), line((8, DEPTH))
    scale = 1.0 + jnp.sum(jnp.where(at == lead, film[...], 0.0), axis=0, keepdims=True)
    shift = jnp.sum(jnp.where(at == lead + 4, film[...], 0.0), axis=0, keepdims=True)

    def decode(values):
        hidden = rms_scale(values, gain) * scale + shift
        return (values + dot(silu(hidden).astype(BF16), out_proj[...])).astype(BF16)

    row_at, col_at = grid_place()
    here = row_at * wide + col_at * 2 + ((line((CELLS, cells)) & (TILE_W - 1)) >> 4)
    mine = ones_where(column((CELLS, cells)) == here)
    spread = dot(mine, high) + dot(mine, low)
    maps[...] = decode(partial[...] + spread)
    put_maps = pltpu.make_async_copy(maps, maps_ref, sems.at[0])
    put_maps.start()

    count = lookup.shape[1]
    same = ones_where(line((count, count)) == column((count, count)))
    where = dot_rows(same, lookup[...])
    key = (where[:, 0:1] * 16 + where[:, 1:2]).astype(jnp.int32)
    area = (where[:, 2:3] * 16 + where[:, 3:4]).astype(jnp.int32)
    slot = column((count, cells))
    pick = ones_where(slot == area)
    at_stations = dot(pick, high) + dot(pick, low)
    for half in range(2):
        found = returned[:, half * DEPTH : (half + 1) * DEPTH]
        at_stations += dot(ones_where(slot + half * cells == key), found)
    scores[...] = dot(decode(at_stations), projector[...]).astype(BF16)
    put_scores = pltpu.make_async_copy(scores, scores_ref, sems.at[1])
    put_scores.start()
    put_maps.wait()
    put_scores.wait()


def call(kernel, outs, scratch, operands, hbm_outs=(), megabytes=4):
    vmem = pl.BlockSpec(memory_space=pltpu.VMEM)
    hbm = pl.BlockSpec(memory_space=pltpu.HBM)
    return pl.pallas_call(
        kernel,
        out_shape=[jax.ShapeDtypeStruct(shape, dtype) for shape, dtype in outs],
        in_specs=[vmem] * len(operands),
        out_specs=[hbm if i in hbm_outs else vmem for i in range(len(outs))],
        scratch_shapes=scratch,
        compiler_params=pltpu.CompilerParams(vmem_limit_bytes=megabytes * 2**20),
    )(*operands)


def pack(records, space_count):
    count, width = records.shape
    outs = [((2 * space_count, width // 2 * 3), BF16), ((16, count), BF16)]
    return call(pack_kernel, outs, [], [records], megabytes=8)


def inject(steps, arrived, embed, tiles, film_table):
    return call(
        inject_kernel,
        [
            ((TILE_H, TILE_W, DEPTH), F32),
            ((HALO * TILE_W + 8, DEPTH), BF16),
            ((HALO * TILE_W + 8, DEPTH), BF16),
            ((8, DEPTH), F32),
        ],
        [],
        [steps, arrived, embed, tiles, film_table],
        megabytes=8,
    )


def widen(image_rows, north, south, own):
    shape = (FRAME_H, SIDE, DEPTH)
    return call(
        functools.partial(widen_kernel, image_rows),
        [(shape, BF16), (shape, BF16)],
        [],
        [north, south, own],
    )


def trunk(image_rows, north, south, west, east, own, film, conv_fine, conv_mid, gains, arrived):
    return call(
        functools.partial(trunk_kernel, image_rows),
        [((CELLS, DEPTH), F32), ((arrived.shape[0], 3 * DEPTH), BF16), ((8, DEPTH), F32)],
        [
            pltpu.VMEM((FRAME_H, FRAME_W, DEPTH), F32),
            pltpu.VMEM((FRAME_H * FRAME_W, 3 * DEPTH), BF16),
            pltpu.VMEM((ENC_H, FRAME_W, DEPTH), F32),
            pltpu.VMEM((ENC_H // 4 * MID_W, DEPTH), F32),
            pltpu.VMEM((ENC_H // 4 * MID_W, 3 * DEPTH), BF16),
        ],
        [
            north, south, west, east, own, film,
            conv_fine.reshape(3, 3 * DEPTH, DEPTH),
            conv_mid.reshape(3, 3 * DEPTH, DEPTH),
            gains, arrived,
        ],
        megabytes=16,
    )


def tail(returned, conv_coarse, gains, partial, film, lookup, out_proj, projector):
    cells = returned.shape[0]
    outs = [((CELLS, DEPTH), BF16), ((lookup.shape[1], projector.shape[1]), BF16)]
    return call(
        tail_kernel,
        outs,
        [
            pltpu.VMEM((cells + 4 * TILE_COLS, 3 * DEPTH), BF16),
            *[pltpu.VMEM(shape, dtype) for shape, dtype in outs],
            pltpu.SemaphoreType.DMA((2,)),
        ],
        [
            returned, conv_coarse.reshape(3, 3 * DEPTH, DEPTH), gains,
            partial, film, lookup, out_proj, projector,
        ],
        hbm_outs=(0, 1),
        megabytes=16,
    )


def shifted(value, row_step, col_step, lead_steps=(0, 0)):
    rows, leads = lax.axis_size("space") // TILE_COLS, lax.axis_size("lead")
    pairs = []
    for row in range(rows):
        for col in range(TILE_COLS):
            for lead in range(leads):
                source = (row * TILE_COLS + col) * leads + lead
                there = (row + row_step) % rows * TILE_COLS + (col + col_step) % TILE_COLS
                pairs.append((source, there * leads + (lead - lead_steps[col % 2]) % leads))
    return lax.ppermute(value, ("space", "lead"), pairs)


def body(
    tiles,
    station_obs,
    station_tile,
    station_pixel,
    station_embed,
    conv_fine,
    conv_mid,
    conv_coarse,
    norm_gains,
    film_table,
    horizon_step_list,
    out_proj,
    gauge_bin_projector,
):
    space_count = lax.axis_size("space")
    count, readings = station_obs.shape
    col = column((count, readings))
    ids = jnp.where(col == 2, station_pixel[:, None] & 15, 0)
    ids = jnp.where(col == 1, station_pixel[:, None] >> 4, ids)
    ids = jnp.where(col == 0, station_tile, ids)
    records = jnp.concatenate([station_obs, ids.astype(BF16)], axis=1)
    payload, lookup = pack(records, space_count)
    arrived = lax.all_to_all(
        payload.reshape(space_count, 2, 3 * readings), "space", 0, 0, tiled=True
    ).reshape(2 * space_count, 3 * readings)
    own, first_rows, last_rows, film = inject(
        horizon_step_list.reshape(1, -1), arrived, station_embed, tiles.reshape(CELLS, DEPTH), film_table
    )

    image_rows = space_count // TILE_COLS
    north = shifted(last_rows, 1, 0, (1, 2))
    south = shifted(first_rows, -1, 0, (-1, 0))
    first_cols, last_cols = widen(image_rows, north, south, own)
    west = shifted(last_cols, 0, 1)
    east = shifted(first_cols, 0, -1)

    partial, parcel, film = trunk(
        image_rows,
        north, south, west, east, own, film, conv_fine, conv_mid, norm_gains, arrived,
    )
    returned = lax.all_to_all(
        parcel.reshape(space_count, 2, 3 * DEPTH), "space", 0, 0, tiled=True
    ).reshape(2 * space_count, 3 * DEPTH)

    maps, scores = tail(
        returned, conv_coarse, norm_gains, partial, film, lookup, out_proj, gauge_bin_projector
    )
    return maps.reshape(1, 1, TILE_H, TILE_W, DEPTH), scores.reshape(1, count, -1)


def solution(mesh):
    in_specs = (
        P("space", None, None, None),
        P("space", None),
        P("space", None),
        P("space"),
        P(),
        P(),
        P(),
        P(),
        P(),
        P("lead", None),
        P(),
        P(),
        P(),
    )
    out_specs = (P("lead", "space", None, None, None), P("lead", "space", None))
    return jax.shard_map(body, mesh=mesh, in_specs=in_specs, out_specs=out_specs, check_vma=False)
```

```python
import functools

import jax
import jax.numpy as jnp
from jax import lax
from jax.experimental import pallas as pl
from jax.experimental.pallas import tpu as pltpu
from jax.sharding import PartitionSpec as P

TILE_COLS = 8
TILE_H, TILE_W, DEPTH = 16, 32, 256
CELLS = TILE_H * TILE_W
EPS = 1e-06
HALO = 5
SIDE = 8
FRAME_H, FRAME_W = TILE_H + 2 * HALO, TILE_W + 2 * SIDE
ENC_H = FRAME_H - 2
MID_W = 16
F32 = jnp.float32
BF16 = jnp.bfloat16


def dot(a, b):
    return jnp.dot(a, b, preferred_element_type=F32)


def dot_rows(a, b):
    return lax.dot_general(a, b, (((1,), (1,)), ((), ())), preferred_element_type=F32)


def silu(v):
    return v / (1.0 + jnp.exp(-v))


def rms_scale(values, gain):
    mean_sq = jnp.mean(values * values, axis=-1, keepdims=True)
    return values * lax.rsqrt(mean_sq + EPS) * gain


def column(shape):
    return lax.broadcasted_iota(jnp.int32, shape, 1)


def line(shape):
    return lax.broadcasted_iota(jnp.int32, shape, 0)


def ones_where(condition):
    return condition.astype(F32).astype(BF16)


def grid_place():
    at = lax.axis_index("space")
    return lax.div(at, TILE_COLS), lax.rem(at, TILE_COLS)


def pack_kernel(records, payload, lookup):
    count, readings = records.shape[0], records.shape[1] // 2
    pairs = payload.shape[0]
    obs = records[:, :readings]
    earlier = ones_where(line((count, count)) < column((count, count)))
    sort, lane = line((16, readings)), column((16, readings))
    weights = jnp.where((sort == 1) & (lane == 1), 16.0, 0.0)
    weights = jnp.where((sort == 0) & (lane == 0) | (sort == 1) & (lane == 2), 1.0, weights)
    ids = dot_rows(weights.astype(BF16), records[:, readings:]).astype(jnp.int32)
    dest, pixel = ids[0:1], ids[1:2]
    lane = column((pairs, readings))
    hot = (line((pairs // 2, count)) == dest).astype(F32)
    prior = dot(hot.astype(BF16), earlier)
    position = jnp.sum(prior * hot, axis=0, keepdims=True).astype(jnp.int32)
    key = dest * 2 + (position & 1) + pairs * (position >> 1)
    coarse = dest * 2 + ((pixel & (TILE_W - 1)) >> 4)
    sort = line((16, count))
    found = jnp.where(sort == 0, key >> 4, jnp.where(sort == 1, key & 15, 0))
    found = jnp.where(sort == 2, coarse >> 4, jnp.where(sort == 3, coarse & 15, found))
    lookup[...] = found.astype(F32).astype(BF16)
    places = jnp.zeros((pairs, readings), jnp.int32)
    for half in range(2):
        match = line((pairs, count)) + half * pairs == key
        sent = dot(ones_where(match), obs)
        payload[:, half * readings : (half + 1) * readings] = sent.astype(BF16)
        at = jnp.sum(jnp.where(match, pixel, 0), axis=1, keepdims=True)
        places = jnp.where(lane == 2 * half, at >> 4, places)
        places = jnp.where(lane == 2 * half + 1, at & 15, places)
    payload[:, 2 * readings :] = places.astype(F32).astype(BF16)


def inject_kernel(
    steps, arrived, embed, tiles, film_table,
    own, first_rows, last_rows, film,
):
    pairs = arrived.shape[0]
    readings = embed.shape[0]
    weight = embed[...]
    sort, lane = line((8, readings)), column((8, readings))
    weights = jnp.where(lane == 2 * sort, 16.0, jnp.where(lane == 2 * sort + 1, 1.0, 0.0))
    weights = jnp.where(sort < 2, weights, 0.0).astype(BF16)
    pixels = dot_rows(weights, arrived[:, 2 * readings :]).astype(jnp.int32)
    fine = 0.0
    for half in range(2):
        embedded = dot(arrived[:, half * readings : (half + 1) * readings], weight)
        hot = ones_where(line((CELLS, pairs)) == pixels[half : half + 1])
        fine += dot(hot, embedded.astype(BF16))
    fine = (fine + tiles[...].astype(F32)).reshape(TILE_H, TILE_W, DEPTH)
    own[...] = fine
    table_rows = film_table.shape[0]
    offset = lax.axis_index("lead") * table_rows
    sort = line((8, table_rows))
    at = jnp.full((8, table_rows), -1, jnp.int32)
    for i in range(4):
        at = jnp.where((sort & 3) == i, steps[0:1, i : i + 1] - offset, at)
    hot = ones_where(column((8, table_rows)) == at)
    both = dot(hot, film_table[...])
    rows = jnp.where(line((8, DEPTH)) < 4, both[:, :DEPTH], both[:, DEPTH:])
    film[...] = rows
    for target, start in ((first_rows, 0), (last_rows, TILE_H - HALO)):
        edge = fine[start : start + HALO].reshape(HALO * TILE_W, DEPTH)
        target[...] = jnp.concatenate([edge, rows], axis=0).astype(BF16)


def brought_film(north, south, row_at, col_at):
    above, below = (rows[HALO * TILE_W :].astype(F32) for rows in (north, south))
    return above + jnp.where((lax.rem(col_at, 2) == 0) | (row_at == 0), below, 0.0)


def widen_kernel(image_rows, north, south, own, film_ref, first_cols, last_cols):
    row_at, col_at = grid_place()
    edge = (row_at == 0) | (row_at == image_rows - 1)
    film = brought_film(north, south, row_at, col_at) + jnp.where(edge, film_ref[...], 0.0)
    at = line((SIDE, DEPTH))
    for y in range(FRAME_H):
        for target, cols in (
            (first_cols, slice(0, SIDE)),
            (last_cols, slice(TILE_W - SIDE, TILE_W)),
        ):
            start = y % (HALO + TILE_H) * TILE_W + cols.start
            if y < HALO:
                rows = north[start : start + SIDE].astype(F32)
            elif y < HALO + TILE_H:
                rows = own[y - HALO, cols]
            else:
                rows = south[start : start + SIDE].astype(F32)
            if y < 8 and target is last_cols:
                rows = jnp.where(at == 0, film[y : y + 1], rows)
            target[y] = rows.astype(BF16)


def trunk_kernel(
    image_rows,
    north, south, west, east, own, film, conv_fine, conv_mid, gains, arrived,
    partial_ref, parcel, film_ref,
    frame, taps, enc, mid_in, mid_taps,
):
    row_at, col_at = grid_place()
    left = west[...].astype(F32)
    at = line((8, DEPTH))
    rows = film[...] + brought_film(north, south, row_at, col_at)
    for y in range(8):
        rows += jnp.where(at == y, left[y, 0:1], 0.0)
    film_ref[...] = rows
    above, below = (
        rows[: HALO * TILE_W].astype(F32).reshape(HALO, TILE_W, DEPTH) for rows in (north, south)
    )
    inner = slice(SIDE, SIDE + TILE_W)
    frame[:HALO, inner] = above
    frame[HALO : HALO + TILE_H, inner] = own[...]
    frame[HALO + TILE_H :, inner] = below
    frame[:, :SIDE] = jnp.where(col_at > 0, left, 0.0)
    frame[:, SIDE + TILE_W :] = jnp.where(col_at < TILE_COLS - 1, east[...].astype(F32), 0.0)
    gain = gains[0:1].astype(F32)
    for y in range(FRAME_H):
        normed = rms_scale(frame[y], gain)
        rows = slice(y * FRAME_W, (y + 1) * FRAME_W)
        taps[rows, :DEPTH] = pltpu.roll(normed, 1, 0).astype(BF16)
        taps[rows, DEPTH : 2 * DEPTH] = normed.astype(BF16)
        taps[rows, 2 * DEPTH :] = pltpu.roll(normed, FRAME_W - 1, 0).astype(BF16)
    size = ENC_H * FRAME_W
    conv = 0.0
    for dy in range(3):
        conv += dot(taps[dy * FRAME_W : dy * FRAME_W + size], conv_fine[dy])
    done = (frame[1 : 1 + ENC_H].reshape(size, DEPTH) + silu(conv)).astype(BF16)
    enc[...] = done.astype(F32).reshape(ENC_H, FRAME_W, DEPTH)
    group = 4 * FRAME_W
    at = column((MID_W, group))
    x = at - FRAME_W * sum((at >= FRAME_W * i).astype(jnp.int32) for i in range(1, 4))
    pool = ((x >> 2) - 1 == line((MID_W, group))) & (line((MID_W, group)) < 10)
    pool = jnp.where(pool, 1.0 / 16, 0.0).astype(BF16)
    for i in range(ENC_H // 4):
        mid_in[i * MID_W : (i + 1) * MID_W] = dot(pool, done[i * group : (i + 1) * group])

    mid = mid_in[...]
    normed = rms_scale(mid, gains[1:2].astype(F32))
    at = line(mid.shape)
    row = row_at * (TILE_H // 4) - 1 + at // MID_W
    col = col_at * (TILE_W // 4) - 1 + at % MID_W
    inside = (row >= 0) & (row < image_rows * (TILE_H // 4))
    inside = inside & (col >= 0) & (col < TILE_COLS * (TILE_W // 4))
    normed = jnp.where(inside, normed, 0.0)
    mid_taps[:, :DEPTH] = pltpu.roll(normed, 1, 0).astype(BF16)
    mid_taps[:, DEPTH : 2 * DEPTH] = normed.astype(BF16)
    mid_taps[:, 2 * DEPTH :] = pltpu.roll(normed, mid.shape[0] - 1, 0).astype(BF16)
    conv = 0.0
    for dy in range(3):
        conv += dot(mid_taps[dy * MID_W : (dy + 4) * MID_W], conv_mid[dy])
    enc_mid = mid[MID_W : 5 * MID_W] + silu(conv)
    high = enc_mid.astype(BF16)
    low = (enc_mid - high.astype(F32)).astype(BF16)

    shape = (CELLS, 4 * MID_W)
    cell = line(shape)
    spread = (cell >> 7) * MID_W + ((cell & (TILE_W - 1)) >> 2) + 1
    spread = ones_where(column(shape) == spread)
    centre = enc[HALO - 1 : HALO - 1 + TILE_H, SIDE : SIDE + TILE_W]
    partial = centre.reshape(CELLS, DEPTH) + (dot(spread, high) + dot(spread, low))
    partial_ref[...] = partial

    x = column((16, 4 * MID_W)) % MID_W - 1
    pool = (x >= 0) & (x < 8) & ((x >> 2) == line((16, 4 * MID_W)))
    pool = jnp.where(pool, 1.0 / 16, 0.0).astype(BF16)
    coarse = dot(pool, high) + dot(pool, low)
    pairs, readings = arrived.shape[0], arrived.shape[1] // 3
    partial = partial.astype(BF16)
    for half in range(2):
        at = 2 * readings + 2 * half
        pixel = arrived[:, at : at + 1].astype(F32) * 16 + arrived[:, at + 1 : at + 2].astype(F32)
        hot = ones_where(column((pairs, CELLS)) == pixel.astype(jnp.int32))
        parcel[:, half * DEPTH : (half + 1) * DEPTH] = dot(hot, partial).astype(BF16)
    even = line((pairs, DEPTH)) % 2 == 0
    parcel[:, 2 * DEPTH :] = jnp.where(even, coarse[0:1], coarse[1:2]).astype(BF16)


def tail_kernel(
    returned, conv_coarse, gains, partial, film, lookup, out_proj, projector,
    maps_ref, scores_ref,
    taps, maps, scores, sems,
):
    cells, wide = returned.shape[0], TILE_COLS * 2
    coarse = returned[:, 2 * DEPTH :].astype(F32)
    normed = rms_scale(coarse, gains[2:3].astype(F32))
    col = line(coarse.shape) % wide
    taps[:wide] = jnp.zeros((wide, 3 * DEPTH), BF16)
    taps[wide + cells :] = jnp.zeros((wide, 3 * DEPTH), BF16)
    inner = slice(wide, wide + cells)
    left, right = pltpu.roll(normed, 1, 0), pltpu.roll(normed, cells - 1, 0)
    taps[inner, :DEPTH] = jnp.where(col == 0, 0.0, left).astype(BF16)
    taps[inner, DEPTH : 2 * DEPTH] = normed.astype(BF16)
    taps[inner, 2 * DEPTH :] = jnp.where(col == wide - 1, 0.0, right).astype(BF16)
    conv = 0.0
    for dy in range(3):
        conv += dot(taps[dy * wide : dy * wide + cells], conv_coarse[dy])
    context = coarse + silu(conv)
    high = context.astype(BF16)
    low = (context - high.astype(F32)).astype(BF16)

    gain = gains[3:4].astype(F32)
    lead, at = lax.axis_index("lead"), line((8, DEPTH))
    scale = 1.0 + jnp.sum(jnp.where(at == lead, film[...], 0.0), axis=0, keepdims=True)
    shift = jnp.sum(jnp.where(at == lead + 4, film[...], 0.0), axis=0, keepdims=True)

    def decode(values):
        hidden = rms_scale(values, gain) * scale + shift
        return (values + dot(silu(hidden).astype(BF16), out_proj[...])).astype(BF16)

    row_at, col_at = grid_place()
    here = row_at * wide + col_at * 2 + ((line((CELLS, cells)) & (TILE_W - 1)) >> 4)
    mine = ones_where(column((CELLS, cells)) == here)
    spread = dot(mine, high) + dot(mine, low)
    maps[...] = decode(partial[...] + spread)
    put_maps = pltpu.make_async_copy(maps, maps_ref, sems.at[0])
    put_maps.start()

    count = lookup.shape[1]
    same = ones_where(line((count, count)) == column((count, count)))
    where = dot_rows(same, lookup[...])
    key = (where[:, 0:1] * 16 + where[:, 1:2]).astype(jnp.int32)
    area = (where[:, 2:3] * 16 + where[:, 3:4]).astype(jnp.int32)
    slot = column((count, cells))
    pick = ones_where(slot == area)
    at_stations = dot(pick, high) + dot(pick, low)
    for half in range(2):
        found = returned[:, half * DEPTH : (half + 1) * DEPTH]
        at_stations += dot(ones_where(slot + half * cells == key), found)
    scores[...] = dot(decode(at_stations), projector[...]).astype(BF16)
    put_scores = pltpu.make_async_copy(scores, scores_ref, sems.at[1])
    put_scores.start()
    put_maps.wait()
    put_scores.wait()


def call(kernel, outs, scratch, operands, hbm_outs=(), megabytes=4):
    vmem = pl.BlockSpec(memory_space=pltpu.VMEM)
    hbm = pl.BlockSpec(memory_space=pltpu.HBM)
    return pl.pallas_call(
        kernel,
        out_shape=[jax.ShapeDtypeStruct(shape, dtype) for shape, dtype in outs],
        in_specs=[vmem] * len(operands),
        out_specs=[hbm if i in hbm_outs else vmem for i in range(len(outs))],
        scratch_shapes=scratch,
        compiler_params=pltpu.CompilerParams(vmem_limit_bytes=megabytes * 2**20),
    )(*operands)


def pack(records, space_count):
    count, width = records.shape
    outs = [((2 * space_count, width // 2 * 3), BF16), ((16, count), BF16)]
    return call(pack_kernel, outs, [], [records], megabytes=8)


def inject(steps, arrived, embed, tiles, film_table):
    return call(
        inject_kernel,
        [
            ((TILE_H, TILE_W, DEPTH), F32),
            ((HALO * TILE_W + 8, DEPTH), BF16),
            ((HALO * TILE_W + 8, DEPTH), BF16),
            ((8, DEPTH), F32),
        ],
        [],
        [steps, arrived, embed, tiles, film_table],
        megabytes=8,
    )


def widen(image_rows, north, south, own, film):
    shape = (FRAME_H, SIDE, DEPTH)
    return call(
        functools.partial(widen_kernel, image_rows),
        [(shape, BF16), (shape, BF16)],
        [],
        [north, south, own, film],
    )


def trunk(image_rows, north, south, west, east, own, film, conv_fine, conv_mid, gains, arrived):
    return call(
        functools.partial(trunk_kernel, image_rows),
        [((CELLS, DEPTH), F32), ((arrived.shape[0], 3 * DEPTH), BF16), ((8, DEPTH), F32)],
        [
            pltpu.VMEM((FRAME_H, FRAME_W, DEPTH), F32),
            pltpu.VMEM((FRAME_H * FRAME_W, 3 * DEPTH), BF16),
            pltpu.VMEM((ENC_H, FRAME_W, DEPTH), F32),
            pltpu.VMEM((ENC_H // 4 * MID_W, DEPTH), F32),
            pltpu.VMEM((ENC_H // 4 * MID_W, 3 * DEPTH), BF16),
        ],
        [
            north, south, west, east, own, film,
            conv_fine.reshape(3, 3 * DEPTH, DEPTH),
            conv_mid.reshape(3, 3 * DEPTH, DEPTH),
            gains, arrived,
        ],
        megabytes=16,
    )


def tail(returned, conv_coarse, gains, partial, film, lookup, out_proj, projector):
    cells = returned.shape[0]
    outs = [((CELLS, DEPTH), BF16), ((lookup.shape[1], projector.shape[1]), BF16)]
    return call(
        tail_kernel,
        outs,
        [
            pltpu.VMEM((cells + 4 * TILE_COLS, 3 * DEPTH), BF16),
            *[pltpu.VMEM(shape, dtype) for shape, dtype in outs],
            pltpu.SemaphoreType.DMA((2,)),
        ],
        [
            returned, conv_coarse.reshape(3, 3 * DEPTH, DEPTH), gains,
            partial, film, lookup, out_proj, projector,
        ],
        hbm_outs=(0, 1),
        megabytes=16,
    )


def shifted(value, row_step, col_step, lead_step):
    rows, leads = lax.axis_size("space") // TILE_COLS, lax.axis_size("lead")
    pairs = []
    for row in range(max(0, row_step), min(rows, rows + row_step)):
        for col in range(TILE_COLS):
            source = (row - row_step) * TILE_COLS + (col - col_step) % TILE_COLS
            for lead in range(leads):
                other = (lead + lead_step(row, col)) % leads
                pairs.append((source * leads + other, (row * TILE_COLS + col) * leads + lead))
    return lax.ppermute(value, ("space", "lead"), pairs)


def body(
    tiles,
    station_obs,
    station_tile,
    station_pixel,
    station_embed,
    conv_fine,
    conv_mid,
    conv_coarse,
    norm_gains,
    film_table,
    horizon_step_list,
    out_proj,
    gauge_bin_projector,
):
    space_count = lax.axis_size("space")
    count, readings = station_obs.shape
    col = column((count, readings))
    ids = jnp.where(col == 2, station_pixel[:, None] & 15, 0)
    ids = jnp.where(col == 1, station_pixel[:, None] >> 4, ids)
    ids = jnp.where(col == 0, station_tile, ids)
    records = jnp.concatenate([station_obs, ids.astype(BF16)], axis=1)
    payload, lookup = pack(records, space_count)
    arrived = lax.all_to_all(
        payload.reshape(space_count, 2, 3 * readings), "space", 0, 0, tiled=True
    ).reshape(2 * space_count, 3 * readings)
    own, first_rows, last_rows, film = inject(
        horizon_step_list.reshape(1, -1), arrived, station_embed, tiles.reshape(CELLS, DEPTH), film_table
    )

    image_rows = space_count // TILE_COLS
    last = image_rows - 1

    def from_above(row, col):
        return 1 if row == last else 1 + col % 2

    def from_below(row, col):
        return 1 if row == 0 else col % 2 - 1

    north = shifted(last_rows, 1, 0, from_above)
    south = shifted(first_rows, -1, 0, from_below)
    first_cols, last_cols = widen(image_rows, north, south, own, film)
    west = shifted(last_cols, 0, 1, lambda row, col: 2 if row in (0, last) else 0)
    east = shifted(first_cols, 0, -1, lambda row, col: 0)

    partial, parcel, film = trunk(
        image_rows,
        north, south, west, east, own, film, conv_fine, conv_mid, norm_gains, arrived,
    )
    returned = lax.all_to_all(
        parcel.reshape(space_count, 2, 3 * DEPTH), "space", 0, 0, tiled=True
    ).reshape(2 * space_count, 3 * DEPTH)

    maps, scores = tail(
        returned, conv_coarse, norm_gains, partial, film, lookup, out_proj, gauge_bin_projector
    )
    return maps.reshape(1, 1, TILE_H, TILE_W, DEPTH), scores.reshape(1, count, -1)


def solution(mesh):
    in_specs = (
        P("space", None, None, None),
        P("space", None),
        P("space", None),
        P("space"),
        P(),
        P(),
        P(),
        P(),
        P(),
        P("lead", None),
        P(),
        P(),
        P(),
    )
    out_specs = (P("lead", "space", None, None, None), P("lead", "space", None))
    return jax.shard_map(body, mesh=mesh, in_specs=in_specs, out_specs=out_specs, check_vma=False)
```

```python
import functools

import jax
import jax.numpy as jnp
from jax import lax
from jax.experimental import pallas as pl
from jax.experimental.pallas import tpu as pltpu
from jax.sharding import PartitionSpec as P

TILE_COLS = 8
TILE_H, TILE_W, DEPTH = 16, 32, 256
CELLS = TILE_H * TILE_W
EPS = 1e-06
FILM_ROWS = 256
HALO = 5
SIDE = 8
FRAME_H, FRAME_W = TILE_H + 2 * HALO, TILE_W + 2 * SIDE
ENC_H = FRAME_H - 2
MID_W = 16
F32 = jnp.float32
BF16 = jnp.bfloat16


def dot(a, b):
    return jnp.dot(a, b, preferred_element_type=F32)


def dot_rows(a, b):
    return lax.dot_general(a, b, (((1,), (1,)), ((), ())), preferred_element_type=F32)


def silu(v):
    return v / (1.0 + jnp.exp(-v))


def rms_scale(values, gain):
    mean_sq = jnp.mean(values * values, axis=-1, keepdims=True)
    return values * lax.rsqrt(mean_sq + EPS) * gain


def column(shape):
    return lax.broadcasted_iota(jnp.int32, shape, 1)


def line(shape):
    return lax.broadcasted_iota(jnp.int32, shape, 0)


def ones_where(condition):
    return condition.astype(F32).astype(BF16)


def grid_place():
    at = lax.axis_index("space")
    return lax.div(at, TILE_COLS), lax.rem(at, TILE_COLS)


def pack_kernel(records, payload, lookup):
    count, readings = records.shape[0], records.shape[1] // 2
    pairs = payload.shape[0]
    obs = records[:, :readings]
    earlier = ones_where(line((count, count)) < column((count, count)))
    sort, lane = line((16, readings)), column((16, readings))
    weights = jnp.where((sort == 1) & (lane == 1), 16.0, 0.0)
    weights = jnp.where((sort == 0) & (lane == 0) | (sort == 1) & (lane == 2), 1.0, weights)
    ids = dot_rows(weights.astype(BF16), records[:, readings:]).astype(jnp.int32)
    dest, pixel = ids[0:1], ids[1:2]
    lane = column((pairs, readings))
    hot = (line((pairs // 2, count)) == dest).astype(F32)
    prior = dot(hot.astype(BF16), earlier)
    position = jnp.sum(prior * hot, axis=0, keepdims=True).astype(jnp.int32)
    key = dest * 2 + (position & 1) + pairs * (position >> 1)
    coarse = dest * 2 + ((pixel & (TILE_W - 1)) >> 4)
    sort = line((16, count))
    found = jnp.where(sort == 0, key >> 4, jnp.where(sort == 1, key & 15, 0))
    found = jnp.where(sort == 2, coarse >> 4, jnp.where(sort == 3, coarse & 15, found))
    lookup[...] = found.astype(F32).astype(BF16)
    places = jnp.zeros((pairs, readings), jnp.int32)
    for half in range(2):
        match = line((pairs, count)) + half * pairs == key
        sent = dot(ones_where(match), obs)
        payload[:, half * readings : (half + 1) * readings] = sent.astype(BF16)
        at = jnp.sum(jnp.where(match, pixel, 0), axis=1, keepdims=True)
        places = jnp.where(lane == 2 * half, at >> 4, places)
        places = jnp.where(lane == 2 * half + 1, at & 15, places)
    payload[:, 2 * readings :] = places.astype(F32).astype(BF16)


def inject_kernel(
    arrived, embed, tiles, own, first_rows, last_rows
):
    pairs = arrived.shape[0]
    readings = embed.shape[0]
    weight = embed[...]
    sort, lane = line((8, readings)), column((8, readings))
    weights = jnp.where(lane == 2 * sort, 16.0, jnp.where(lane == 2 * sort + 1, 1.0, 0.0))
    weights = jnp.where(sort < 2, weights, 0.0).astype(BF16)
    pixels = dot_rows(weights, arrived[:, 2 * readings :]).astype(jnp.int32)
    fine = 0.0
    for half in range(2):
        embedded = dot(arrived[:, half * readings : (half + 1) * readings], weight)
        hot = ones_where(line((CELLS, pairs)) == pixels[half : half + 1])
        fine += dot(hot, embedded.astype(BF16))
    fine = (fine + tiles[...].astype(F32)).reshape(TILE_H, TILE_W, DEPTH)
    own[...] = fine
    first_rows[...] = fine[:HALO].reshape(HALO * TILE_W, DEPTH).astype(BF16)
    last_rows[...] = fine[-HALO:].reshape(HALO * TILE_W, DEPTH).astype(BF16)


def film_kernel(steps, film_table, out):
    table_rows = film_table.shape[0]
    offset = lax.axis_index("lead") * table_rows
    sort = line((8, table_rows))
    at = jnp.full((8, table_rows), -1, jnp.int32)
    for i in range(4):
        at = jnp.where((sort & 3) == i, steps[0:1, i : i + 1] - offset, at)
    both = dot(ones_where(column((8, table_rows)) == at), film_table[...])
    rows = jnp.where(line((8, DEPTH)) < 4, both[:, :DEPTH], both[:, DEPTH:])
    out[...] = jnp.zeros(out.shape, BF16)
    out[:16] = jnp.concatenate([rows, jnp.zeros((8, DEPTH), F32)], axis=0).astype(BF16)


def widen_kernel(north, south, own, first_cols, last_cols):
    for y in range(FRAME_H):
        for target, cols in (
            (first_cols, slice(0, SIDE)),
            (last_cols, slice(TILE_W - SIDE, TILE_W)),
        ):
            start = y % (HALO + TILE_H) * TILE_W + cols.start
            if y < HALO:
                rows = north[start : start + SIDE].astype(F32)
            elif y < HALO + TILE_H:
                rows = own[y - HALO, cols]
            else:
                rows = south[start : start + SIDE].astype(F32)
            target[y] = rows.astype(BF16)


def trunk_kernel(
    image_rows,
    north, south, west, east, own, conv_fine, conv_mid, gains, arrived,
    partial_ref, parcel,
    frame, taps, enc, mid_in, mid_taps,
):
    row_at, col_at = grid_place()
    above, below = (
        rows[: HALO * TILE_W].astype(F32).reshape(HALO, TILE_W, DEPTH) for rows in (north, south)
    )
    inner = slice(SIDE, SIDE + TILE_W)
    frame[:HALO, inner] = above
    frame[HALO : HALO + TILE_H, inner] = own[...]
    frame[HALO + TILE_H :, inner] = below
    frame[:, :SIDE] = west[...].astype(F32)
    frame[:, SIDE + TILE_W :] = east[...].astype(F32)
    gain = gains[0:1].astype(F32)
    for y in range(FRAME_H):
        normed = rms_scale(frame[y], gain)
        rows = slice(y * FRAME_W, (y + 1) * FRAME_W)
        taps[rows, :DEPTH] = pltpu.roll(normed, 1, 0).astype(BF16)
        taps[rows, DEPTH : 2 * DEPTH] = normed.astype(BF16)
        taps[rows, 2 * DEPTH :] = pltpu.roll(normed, FRAME_W - 1, 0).astype(BF16)
    size = ENC_H * FRAME_W
    conv = 0.0
    for dy in range(3):
        conv += dot(taps[dy * FRAME_W : dy * FRAME_W + size], conv_fine[dy])
    done = (frame[1 : 1 + ENC_H].reshape(size, DEPTH) + silu(conv)).astype(BF16)
    enc[...] = done.astype(F32).reshape(ENC_H, FRAME_W, DEPTH)
    group = 4 * FRAME_W
    at = column((MID_W, group))
    x = at - FRAME_W * sum((at >= FRAME_W * i).astype(jnp.int32) for i in range(1, 4))
    pool = ((x >> 2) - 1 == line((MID_W, group))) & (line((MID_W, group)) < 10)
    pool = jnp.where(pool, 1.0 / 16, 0.0).astype(BF16)
    for i in range(ENC_H // 4):
        mid_in[i * MID_W : (i + 1) * MID_W] = dot(pool, done[i * group : (i + 1) * group])

    mid = mid_in[...]
    normed = rms_scale(mid, gains[1:2].astype(F32))
    at = line(mid.shape)
    row = row_at * (TILE_H // 4) - 1 + at // MID_W
    col = col_at * (TILE_W // 4) - 1 + at % MID_W
    inside = (row >= 0) & (row < image_rows * (TILE_H // 4))
    inside = inside & (col >= 0) & (col < TILE_COLS * (TILE_W // 4))
    normed = jnp.where(inside, normed, 0.0)
    mid_taps[:, :DEPTH] = pltpu.roll(normed, 1, 0).astype(BF16)
    mid_taps[:, DEPTH : 2 * DEPTH] = normed.astype(BF16)
    mid_taps[:, 2 * DEPTH :] = pltpu.roll(normed, mid.shape[0] - 1, 0).astype(BF16)
    conv = 0.0
    for dy in range(3):
        conv += dot(mid_taps[dy * MID_W : (dy + 4) * MID_W], conv_mid[dy])
    enc_mid = mid[MID_W : 5 * MID_W] + silu(conv)
    high = enc_mid.astype(BF16)
    low = (enc_mid - high.astype(F32)).astype(BF16)

    shape = (CELLS, 4 * MID_W)
    cell = line(shape)
    spread = (cell >> 7) * MID_W + ((cell & (TILE_W - 1)) >> 2) + 1
    spread = ones_where(column(shape) == spread)
    centre = enc[HALO - 1 : HALO - 1 + TILE_H, SIDE : SIDE + TILE_W]
    partial = centre.reshape(CELLS, DEPTH) + (dot(spread, high) + dot(spread, low))
    partial_ref[...] = partial

    x = column((16, 4 * MID_W)) % MID_W - 1
    pool = (x >= 0) & (x < 8) & ((x >> 2) == line((16, 4 * MID_W)))
    pool = jnp.where(pool, 1.0 / 16, 0.0).astype(BF16)
    coarse = dot(pool, high) + dot(pool, low)
    pairs, readings = arrived.shape[0], arrived.shape[1] // 3
    partial = partial.astype(BF16)
    for half in range(2):
        at = 2 * readings + 2 * half
        pixel = arrived[:, at : at + 1].astype(F32) * 16 + arrived[:, at + 1 : at + 2].astype(F32)
        hot = ones_where(column((pairs, CELLS)) == pixel.astype(jnp.int32))
        parcel[:, half * DEPTH : (half + 1) * DEPTH] = dot(hot, partial).astype(BF16)
    even = line((pairs, DEPTH)) % 2 == 0
    parcel[:, 2 * DEPTH :] = jnp.where(even, coarse[0:1], coarse[1:2]).astype(BF16)


def tail_kernel(
    returned, conv_coarse, gains, partial, film, lookup, out_proj, projector,
    maps_ref, scores_ref,
    taps, maps, scores, sems,
):
    cells, wide = returned.shape[0], TILE_COLS * 2
    coarse = returned[:, 2 * DEPTH :].astype(F32)
    normed = rms_scale(coarse, gains[2:3].astype(F32))
    col = line(coarse.shape) % wide
    taps[:wide] = jnp.zeros((wide, 3 * DEPTH), BF16)
    taps[wide + cells :] = jnp.zeros((wide, 3 * DEPTH), BF16)
    inner = slice(wide, wide + cells)
    left, right = pltpu.roll(normed, 1, 0), pltpu.roll(normed, cells - 1, 0)
    taps[inner, :DEPTH] = jnp.where(col == 0, 0.0, left).astype(BF16)
    taps[inner, DEPTH : 2 * DEPTH] = normed.astype(BF16)
    taps[inner, 2 * DEPTH :] = jnp.where(col == wide - 1, 0.0, right).astype(BF16)
    conv = 0.0
    for dy in range(3):
        conv += dot(taps[dy * wide : dy * wide + cells], conv_coarse[dy])
    context = coarse + silu(conv)
    high = context.astype(BF16)
    low = (context - high.astype(F32)).astype(BF16)

    gain = gains[3:4].astype(F32)
    lead, at = lax.axis_index("lead"), line((16, DEPTH))
    rows = film[:16].astype(F32)
    scale = 1.0 + jnp.sum(jnp.where(at == lead, rows, 0.0), axis=0, keepdims=True)
    shift = jnp.sum(jnp.where(at == lead + 4, rows, 0.0), axis=0, keepdims=True)

    def decode(values):
        hidden = rms_scale(values, gain) * scale + shift
        return (values + dot(silu(hidden).astype(BF16), out_proj[...])).astype(BF16)

    row_at, col_at = grid_place()
    here = row_at * wide + col_at * 2 + ((line((CELLS, cells)) & (TILE_W - 1)) >> 4)
    mine = ones_where(column((CELLS, cells)) == here)
    spread = dot(mine, high) + dot(mine, low)
    maps[...] = decode(partial[...] + spread)
    put_maps = pltpu.make_async_copy(maps, maps_ref, sems.at[0])
    put_maps.start()

    count = lookup.shape[1]
    same = ones_where(line((count, count)) == column((count, count)))
    where = dot_rows(same, lookup[...])
    key = (where[:, 0:1] * 16 + where[:, 1:2]).astype(jnp.int32)
    area = (where[:, 2:3] * 16 + where[:, 3:4]).astype(jnp.int32)
    slot = column((count, cells))
    pick = ones_where(slot == area)
    at_stations = dot(pick, high) + dot(pick, low)
    for half in range(2):
        found = returned[:, half * DEPTH : (half + 1) * DEPTH]
        at_stations += dot(ones_where(slot + half * cells == key), found)
    scores[...] = dot(decode(at_stations), projector[...]).astype(BF16)
    put_scores = pltpu.make_async_copy(scores, scores_ref, sems.at[1])
    put_scores.start()
    put_maps.wait()
    put_scores.wait()


def call(kernel, outs, scratch, operands, hbm_outs=(), megabytes=4):
    vmem = pl.BlockSpec(memory_space=pltpu.VMEM)
    hbm = pl.BlockSpec(memory_space=pltpu.HBM)
    return pl.pallas_call(
        kernel,
        out_shape=[jax.ShapeDtypeStruct(shape, dtype) for shape, dtype in outs],
        in_specs=[vmem] * len(operands),
        out_specs=[hbm if i in hbm_outs else vmem for i in range(len(outs))],
        scratch_shapes=scratch,
        compiler_params=pltpu.CompilerParams(vmem_limit_bytes=megabytes * 2**20),
    )(*operands)


def pack(records, space_count):
    count, width = records.shape
    outs = [((2 * space_count, width // 2 * 3), BF16), ((16, count), BF16)]
    return call(pack_kernel, outs, [], [records], megabytes=8)


def film_rows(steps, film_table):
    return call(film_kernel, [((FILM_ROWS, DEPTH), BF16)], [], [steps, film_table])[0]


def inject(arrived, embed, tiles):
    return call(
        inject_kernel,
        [
            ((TILE_H, TILE_W, DEPTH), F32),
            ((HALO * TILE_W, DEPTH), BF16),
            ((HALO * TILE_W, DEPTH), BF16),
        ],
        [],
        [arrived, embed, tiles],
        megabytes=8,
    )


def widen(north, south, own):
    shape = (FRAME_H, SIDE, DEPTH)
    return call(widen_kernel, [(shape, BF16), (shape, BF16)], [], [north, south, own])


def trunk(image_rows, north, south, west, east, own, conv_fine, conv_mid, gains, arrived):
    return call(
        functools.partial(trunk_kernel, image_rows),
        [((CELLS, DEPTH), F32), ((arrived.shape[0], 3 * DEPTH), BF16)],
        [
            pltpu.VMEM((FRAME_H, FRAME_W, DEPTH), F32),
            pltpu.VMEM((FRAME_H * FRAME_W, 3 * DEPTH), BF16),
            pltpu.VMEM((ENC_H, FRAME_W, DEPTH), F32),
            pltpu.VMEM((ENC_H // 4 * MID_W, DEPTH), F32),
            pltpu.VMEM((ENC_H // 4 * MID_W, 3 * DEPTH), BF16),
        ],
        [
            north, south, west, east, own,
            conv_fine.reshape(3, 3 * DEPTH, DEPTH),
            conv_mid.reshape(3, 3 * DEPTH, DEPTH),
            gains, arrived,
        ],
        megabytes=16,
    )


def tail(returned, conv_coarse, gains, partial, film, lookup, out_proj, projector):
    cells = returned.shape[0]
    outs = [((CELLS, DEPTH), BF16), ((lookup.shape[1], projector.shape[1]), BF16)]
    return call(
        tail_kernel,
        outs,
        [
            pltpu.VMEM((cells + 4 * TILE_COLS, 3 * DEPTH), BF16),
            *[pltpu.VMEM(shape, dtype) for shape, dtype in outs],
            pltpu.SemaphoreType.DMA((2,)),
        ],
        [
            returned, conv_coarse.reshape(3, 3 * DEPTH, DEPTH), gains,
            partial, film, lookup, out_proj, projector,
        ],
        hbm_outs=(0, 1),
        megabytes=16,
    )


def shifted(value, row_step, col_step):
    count = lax.axis_size("space")
    pairs = []
    for source in range(count):
        row, col = source // TILE_COLS + row_step, source % TILE_COLS + col_step
        if 0 <= row < count // TILE_COLS and 0 <= col < TILE_COLS:
            pairs.append((source, row * TILE_COLS + col))
    return lax.ppermute(value, "space", pairs)


def body(
    tiles,
    station_obs,
    station_tile,
    station_pixel,
    station_embed,
    conv_fine,
    conv_mid,
    conv_coarse,
    norm_gains,
    film_table,
    horizon_step_list,
    out_proj,
    gauge_bin_projector,
):
    space_count = lax.axis_size("space")
    count, readings = station_obs.shape
    col = column((count, readings))
    ids = jnp.where(col == 2, station_pixel[:, None] & 15, 0)
    ids = jnp.where(col == 1, station_pixel[:, None] >> 4, ids)
    ids = jnp.where(col == 0, station_tile, ids)
    records = jnp.concatenate([station_obs, ids.astype(BF16)], axis=1)
    payload, lookup = pack(records, space_count)
    arrived = lax.all_to_all(
        payload.reshape(space_count, 2, 3 * readings), "space", 0, 0, tiled=True
    ).reshape(2 * space_count, 3 * readings)
    own, first_rows, last_rows = inject(arrived, station_embed, tiles.reshape(CELLS, DEPTH))

    north = shifted(last_rows, 1, 0)
    south = shifted(first_rows, -1, 0)
    steps, last_rows = lax.optimization_barrier((horizon_step_list.reshape(1, -1), last_rows))
    film = lax.psum(film_rows(steps, film_table), "lead")
    first_cols, last_cols = widen(north, south, own)
    west = shifted(last_cols, 0, 1)
    east = shifted(first_cols, 0, -1)

    partial, parcel = trunk(
        space_count // TILE_COLS,
        north, south, west, east, own, conv_fine, conv_mid, norm_gains, arrived,
    )
    returned = lax.all_to_all(
        parcel.reshape(space_count, 2, 3 * DEPTH), "space", 0, 0, tiled=True
    ).reshape(2 * space_count, 3 * DEPTH)

    maps, scores = tail(
        returned, conv_coarse, norm_gains, partial, film, lookup, out_proj, gauge_bin_projector
    )
    return maps.reshape(1, 1, TILE_H, TILE_W, DEPTH), scores.reshape(1, count, -1)


def solution(mesh):
    in_specs = (
        P("space", None, None, None),
        P("space", None),
        P("space", None),
        P("space"),
        P(),
        P(),
        P(),
        P(),
        P(),
        P("lead", None),
        P(),
        P(),
        P(),
    )
    out_specs = (P("lead", "space", None, None, None), P("lead", "space", None))
    return jax.shard_map(body, mesh=mesh, in_specs=in_specs, out_specs=out_specs, check_vma=False)
```

```python
import functools

import jax
import jax.numpy as jnp
from jax import lax
from jax.experimental import pallas as pl
from jax.experimental.pallas import tpu as pltpu
from jax.sharding import PartitionSpec as P

TILE_COLS = 8
TILE_H, TILE_W, DEPTH = 16, 32, 256
CELLS = TILE_H * TILE_W
EPS = 1e-06
FILM_ROWS = 16
HALO = 5
SIDE = 8
FRAME_H, FRAME_W = TILE_H + 2 * HALO, TILE_W + 2 * SIDE
ENC_H = FRAME_H - 2
MID_W = 16
F32 = jnp.float32
BF16 = jnp.bfloat16


def dot(a, b):
    return jnp.dot(a, b, preferred_element_type=F32)


def dot_rows(a, b):
    return lax.dot_general(a, b, (((1,), (1,)), ((), ())), preferred_element_type=F32)


def silu(v):
    return v / (1.0 + jnp.exp(-v))


def rms_scale(values, gain):
    mean_sq = jnp.mean(values * values, axis=-1, keepdims=True)
    return values * lax.rsqrt(mean_sq + EPS) * gain


def column(shape):
    return lax.broadcasted_iota(jnp.int32, shape, 1)


def line(shape):
    return lax.broadcasted_iota(jnp.int32, shape, 0)


def ones_where(condition):
    return condition.astype(F32).astype(BF16)


def grid_place():
    at = lax.axis_index("space")
    return lax.div(at, TILE_COLS), lax.rem(at, TILE_COLS)


def pack_kernel(records, payload, lookup):
    count, readings = records.shape[0], records.shape[1] // 2
    pairs = payload.shape[0]
    obs = records[:, :readings]
    earlier = ones_where(line((count, count)) < column((count, count)))
    sort, lane = line((16, readings)), column((16, readings))
    weights = jnp.where((sort == 1) & (lane == 1), 16.0, 0.0)
    weights = jnp.where((sort == 0) & (lane == 0) | (sort == 1) & (lane == 2), 1.0, weights)
    ids = dot_rows(weights.astype(BF16), records[:, readings:]).astype(jnp.int32)
    dest, pixel = ids[0:1], ids[1:2]
    lane = column((pairs, readings))
    hot = (line((pairs // 2, count)) == dest).astype(F32)
    prior = dot(hot.astype(BF16), earlier)
    position = jnp.sum(prior * hot, axis=0, keepdims=True).astype(jnp.int32)
    key = dest * 2 + (position & 1) + pairs * (position >> 1)
    coarse = dest * 2 + ((pixel & (TILE_W - 1)) >> 4)
    sort = line((16, count))
    found = jnp.where(sort == 0, key >> 4, jnp.where(sort == 1, key & 15, 0))
    found = jnp.where(sort == 2, coarse >> 4, jnp.where(sort == 3, coarse & 15, found))
    lookup[...] = found.astype(F32).astype(BF16)
    places = jnp.zeros((pairs, readings), jnp.int32)
    for half in range(2):
        match = line((pairs, count)) + half * pairs == key
        sent = dot(ones_where(match), obs)
        payload[:, half * readings : (half + 1) * readings] = sent.astype(BF16)
        at = jnp.sum(jnp.where(match, pixel, 0), axis=1, keepdims=True)
        places = jnp.where(lane == 2 * half, at >> 4, places)
        places = jnp.where(lane == 2 * half + 1, at & 15, places)
    payload[:, 2 * readings :] = places.astype(F32).astype(BF16)


def inject_kernel(
    arrived, embed, tiles, own, first_rows, last_rows
):
    pairs = arrived.shape[0]
    readings = embed.shape[0]
    weight = embed[...]
    sort, lane = line((8, readings)), column((8, readings))
    weights = jnp.where(lane == 2 * sort, 16.0, jnp.where(lane == 2 * sort + 1, 1.0, 0.0))
    weights = jnp.where(sort < 2, weights, 0.0).astype(BF16)
    pixels = dot_rows(weights, arrived[:, 2 * readings :]).astype(jnp.int32)
    fine = 0.0
    for half in range(2):
        embedded = dot(arrived[:, half * readings : (half + 1) * readings], weight)
        hot = ones_where(line((CELLS, pairs)) == pixels[half : half + 1])
        fine += dot(hot, embedded.astype(BF16))
    fine = (fine + tiles[...].astype(F32)).reshape(TILE_H, TILE_W, DEPTH)
    own[...] = fine
    first_rows[...] = fine[:HALO].reshape(HALO * TILE_W, DEPTH).astype(BF16)
    last_rows[...] = fine[-HALO:].reshape(HALO * TILE_W, DEPTH).astype(BF16)


def film_kernel(steps, film_table, out):
    table_rows = film_table.shape[0]
    offset = lax.axis_index("lead") * table_rows
    sort = line((8, table_rows))
    at = jnp.full((8, table_rows), -1, jnp.int32)
    for i in range(4):
        at = jnp.where((sort & 3) == i, steps[0:1, i : i + 1] - offset, at)
    both = dot(ones_where(column((8, table_rows)) == at), film_table[...])
    rows = jnp.where(line((8, DEPTH)) < 4, both[:, :DEPTH], both[:, DEPTH:])
    rest = jnp.zeros((FILM_ROWS - 8, DEPTH), F32)
    out[...] = jnp.concatenate([rows, rest], axis=0).astype(BF16)


def widen_kernel(north, south, own, first_cols, last_cols):
    for y in range(FRAME_H):
        for target, cols in (
            (first_cols, slice(0, SIDE)),
            (last_cols, slice(TILE_W - SIDE, TILE_W)),
        ):
            start = y % (HALO + TILE_H) * TILE_W + cols.start
            if y < HALO:
                rows = north[start : start + SIDE].astype(F32)
            elif y < HALO + TILE_H:
                rows = own[y - HALO, cols]
            else:
                rows = south[start : start + SIDE].astype(F32)
            target[y] = rows.astype(BF16)


def trunk_kernel(
    image_rows,
    north, south, west, east, own, conv_fine, conv_mid, gains, arrived,
    partial_ref, parcel,
    frame, taps, enc, mid_in, mid_taps,
):
    row_at, col_at = grid_place()
    above, below = (
        rows[: HALO * TILE_W].astype(F32).reshape(HALO, TILE_W, DEPTH) for rows in (north, south)
    )
    inner = slice(SIDE, SIDE + TILE_W)
    frame[:HALO, inner] = above
    frame[HALO : HALO + TILE_H, inner] = own[...]
    frame[HALO + TILE_H :, inner] = below
    frame[:, :SIDE] = west[...].astype(F32)
    frame[:, SIDE + TILE_W :] = east[...].astype(F32)
    gain = gains[0:1].astype(F32)
    for y in range(FRAME_H):
        normed = rms_scale(frame[y], gain)
        rows = slice(y * FRAME_W, (y + 1) * FRAME_W)
        taps[rows, :DEPTH] = pltpu.roll(normed, 1, 0).astype(BF16)
        taps[rows, DEPTH : 2 * DEPTH] = normed.astype(BF16)
        taps[rows, 2 * DEPTH :] = pltpu.roll(normed, FRAME_W - 1, 0).astype(BF16)
    size = ENC_H * FRAME_W
    conv = 0.0
    for dy in range(3):
        conv += dot(taps[dy * FRAME_W : dy * FRAME_W + size], conv_fine[dy])
    done = (frame[1 : 1 + ENC_H].reshape(size, DEPTH) + silu(conv)).astype(BF16)
    enc[...] = done.astype(F32).reshape(ENC_H, FRAME_W, DEPTH)
    group = 4 * FRAME_W
    at = column((MID_W, group))
    x = at - FRAME_W * sum((at >= FRAME_W * i).astype(jnp.int32) for i in range(1, 4))
    pool = ((x >> 2) - 1 == line((MID_W, group))) & (line((MID_W, group)) < 10)
    pool = jnp.where(pool, 1.0 / 16, 0.0).astype(BF16)
    for i in range(ENC_H // 4):
        mid_in[i * MID_W : (i + 1) * MID_W] = dot(pool, done[i * group : (i + 1) * group])

    mid = mid_in[...]
    normed = rms_scale(mid, gains[1:2].astype(F32))
    at = line(mid.shape)
    row = row_at * (TILE_H // 4) - 1 + at // MID_W
    col = col_at * (TILE_W // 4) - 1 + at % MID_W
    inside = (row >= 0) & (row < image_rows * (TILE_H // 4))
    inside = inside & (col >= 0) & (col < TILE_COLS * (TILE_W // 4))
    normed = jnp.where(inside, normed, 0.0)
    mid_taps[:, :DEPTH] = pltpu.roll(normed, 1, 0).astype(BF16)
    mid_taps[:, DEPTH : 2 * DEPTH] = normed.astype(BF16)
    mid_taps[:, 2 * DEPTH :] = pltpu.roll(normed, mid.shape[0] - 1, 0).astype(BF16)
    conv = 0.0
    for dy in range(3):
        conv += dot(mid_taps[dy * MID_W : (dy + 4) * MID_W], conv_mid[dy])
    enc_mid = mid[MID_W : 5 * MID_W] + silu(conv)
    high = enc_mid.astype(BF16)
    low = (enc_mid - high.astype(F32)).astype(BF16)

    shape = (CELLS, 4 * MID_W)
    cell = line(shape)
    spread = (cell >> 7) * MID_W + ((cell & (TILE_W - 1)) >> 2) + 1
    spread = ones_where(column(shape) == spread)
    centre = enc[HALO - 1 : HALO - 1 + TILE_H, SIDE : SIDE + TILE_W]
    partial = centre.reshape(CELLS, DEPTH) + (dot(spread, high) + dot(spread, low))
    partial_ref[...] = partial

    x = column((16, 4 * MID_W)) % MID_W - 1
    pool = (x >= 0) & (x < 8) & ((x >> 2) == line((16, 4 * MID_W)))
    pool = jnp.where(pool, 1.0 / 16, 0.0).astype(BF16)
    coarse = dot(pool, high) + dot(pool, low)
    pairs, readings = arrived.shape[0], arrived.shape[1] // 3
    partial = partial.astype(BF16)
    for half in range(2):
        at = 2 * readings + 2 * half
        pixel = arrived[:, at : at + 1].astype(F32) * 16 + arrived[:, at + 1 : at + 2].astype(F32)
        hot = ones_where(column((pairs, CELLS)) == pixel.astype(jnp.int32))
        parcel[:, half * DEPTH : (half + 1) * DEPTH] = dot(hot, partial).astype(BF16)
    even = line((pairs, DEPTH)) % 2 == 0
    parcel[:, 2 * DEPTH :] = jnp.where(even, coarse[0:1], coarse[1:2]).astype(BF16)


def tail_kernel(
    returned, conv_coarse, gains, partial, film, lookup, out_proj, projector,
    maps_ref, scores_ref,
    taps, maps, scores, sems,
):
    cells, wide = returned.shape[0], TILE_COLS * 2
    coarse = returned[:, 2 * DEPTH :].astype(F32)
    normed = rms_scale(coarse, gains[2:3].astype(F32))
    col = line(coarse.shape) % wide
    taps[:wide] = jnp.zeros((wide, 3 * DEPTH), BF16)
    taps[wide + cells :] = jnp.zeros((wide, 3 * DEPTH), BF16)
    inner = slice(wide, wide + cells)
    left, right = pltpu.roll(normed, 1, 0), pltpu.roll(normed, cells - 1, 0)
    taps[inner, :DEPTH] = jnp.where(col == 0, 0.0, left).astype(BF16)
    taps[inner, DEPTH : 2 * DEPTH] = normed.astype(BF16)
    taps[inner, 2 * DEPTH :] = jnp.where(col == wide - 1, 0.0, right).astype(BF16)
    conv = 0.0
    for dy in range(3):
        conv += dot(taps[dy * wide : dy * wide + cells], conv_coarse[dy])
    context = coarse + silu(conv)
    high = context.astype(BF16)
    low = (context - high.astype(F32)).astype(BF16)

    gain = gains[3:4].astype(F32)
    lead, at = lax.axis_index("lead"), line((FILM_ROWS, DEPTH))
    rows = film[...].astype(F32)
    scale = 1.0 + jnp.sum(jnp.where(at == lead, rows, 0.0), axis=0, keepdims=True)
    shift = jnp.sum(jnp.where(at == lead + 4, rows, 0.0), axis=0, keepdims=True)

    def decode(values):
        hidden = rms_scale(values, gain) * scale + shift
        return (values + dot(silu(hidden).astype(BF16), out_proj[...])).astype(BF16)

    row_at, col_at = grid_place()
    here = row_at * wide + col_at * 2 + ((line((CELLS, cells)) & (TILE_W - 1)) >> 4)
    mine = ones_where(column((CELLS, cells)) == here)
    spread = dot(mine, high) + dot(mine, low)
    maps[...] = decode(partial[...] + spread)
    put_maps = pltpu.make_async_copy(maps, maps_ref, sems.at[0])
    put_maps.start()

    count = lookup.shape[1]
    same = ones_where(line((count, count)) == column((count, count)))
    where = dot_rows(same, lookup[...])
    key = (where[:, 0:1] * 16 + where[:, 1:2]).astype(jnp.int32)
    area = (where[:, 2:3] * 16 + where[:, 3:4]).astype(jnp.int32)
    slot = column((count, cells))
    pick = ones_where(slot == area)
    at_stations = dot(pick, high) + dot(pick, low)
    for half in range(2):
        found = returned[:, half * DEPTH : (half + 1) * DEPTH]
        at_stations += dot(ones_where(slot + half * cells == key), found)
    scores[...] = dot(decode(at_stations), projector[...]).astype(BF16)
    put_scores = pltpu.make_async_copy(scores, scores_ref, sems.at[1])
    put_scores.start()
    put_maps.wait()
    put_scores.wait()


def call(kernel, outs, scratch, operands, hbm_outs=(), megabytes=4):
    vmem = pl.BlockSpec(memory_space=pltpu.VMEM)
    hbm = pl.BlockSpec(memory_space=pltpu.HBM)
    return pl.pallas_call(
        kernel,
        out_shape=[jax.ShapeDtypeStruct(shape, dtype) for shape, dtype in outs],
        in_specs=[vmem] * len(operands),
        out_specs=[hbm if i in hbm_outs else vmem for i in range(len(outs))],
        scratch_shapes=scratch,
        compiler_params=pltpu.CompilerParams(vmem_limit_bytes=megabytes * 2**20),
    )(*operands)


def pack(records, space_count):
    count, width = records.shape
    outs = [((2 * space_count, width // 2 * 3), BF16), ((16, count), BF16)]
    return call(pack_kernel, outs, [], [records], megabytes=8)


def film_rows(steps, film_table):
    return call(film_kernel, [((FILM_ROWS, DEPTH), BF16)], [], [steps, film_table])[0]


def inject(arrived, embed, tiles):
    return call(
        inject_kernel,
        [
            ((TILE_H, TILE_W, DEPTH), F32),
            ((HALO * TILE_W, DEPTH), BF16),
            ((HALO * TILE_W, DEPTH), BF16),
        ],
        [],
        [arrived, embed, tiles],
        megabytes=8,
    )


def widen(north, south, own):
    shape = (FRAME_H, SIDE, DEPTH)
    return call(widen_kernel, [(shape, BF16), (shape, BF16)], [], [north, south, own])


def trunk(image_rows, north, south, west, east, own, conv_fine, conv_mid, gains, arrived):
    return call(
        functools.partial(trunk_kernel, image_rows),
        [((CELLS, DEPTH), F32), ((arrived.shape[0], 3 * DEPTH), BF16)],
        [
            pltpu.VMEM((FRAME_H, FRAME_W, DEPTH), F32),
            pltpu.VMEM((FRAME_H * FRAME_W, 3 * DEPTH), BF16),
            pltpu.VMEM((ENC_H, FRAME_W, DEPTH), F32),
            pltpu.VMEM((ENC_H // 4 * MID_W, DEPTH), F32),
            pltpu.VMEM((ENC_H // 4 * MID_W, 3 * DEPTH), BF16),
        ],
        [
            north, south, west, east, own,
            conv_fine.reshape(3, 3 * DEPTH, DEPTH),
            conv_mid.reshape(3, 3 * DEPTH, DEPTH),
            gains, arrived,
        ],
        megabytes=16,
    )


def tail(returned, conv_coarse, gains, partial, film, lookup, out_proj, projector):
    cells = returned.shape[0]
    outs = [((CELLS, DEPTH), BF16), ((lookup.shape[1], projector.shape[1]), BF16)]
    return call(
        tail_kernel,
        outs,
        [
            pltpu.VMEM((cells + 4 * TILE_COLS, 3 * DEPTH), BF16),
            *[pltpu.VMEM(shape, dtype) for shape, dtype in outs],
            pltpu.SemaphoreType.DMA((2,)),
        ],
        [
            returned, conv_coarse.reshape(3, 3 * DEPTH, DEPTH), gains,
            partial, film, lookup, out_proj, projector,
        ],
        hbm_outs=(0, 1),
        megabytes=16,
    )


def shifted(value, row_step, col_step):
    count = lax.axis_size("space")
    pairs = []
    for source in range(count):
        row, col = source // TILE_COLS + row_step, source % TILE_COLS + col_step
        if 0 <= row < count // TILE_COLS and 0 <= col < TILE_COLS:
            pairs.append((source, row * TILE_COLS + col))
    return lax.ppermute(value, "space", pairs)


def body(
    tiles,
    station_obs,
    station_tile,
    station_pixel,
    station_embed,
    conv_fine,
    conv_mid,
    conv_coarse,
    norm_gains,
    film_table,
    horizon_step_list,
    out_proj,
    gauge_bin_projector,
):
    space_count = lax.axis_size("space")
    count, readings = station_obs.shape
    col = column((count, readings))
    ids = jnp.where(col == 2, station_pixel[:, None] & 15, 0)
    ids = jnp.where(col == 1, station_pixel[:, None] >> 4, ids)
    ids = jnp.where(col == 0, station_tile, ids)
    records = jnp.concatenate([station_obs, ids.astype(BF16)], axis=1)
    payload, lookup = pack(records, space_count)
    arrived = lax.all_to_all(
        payload.reshape(space_count, 2, 3 * readings), "space", 0, 0, tiled=True
    ).reshape(2 * space_count, 3 * readings)
    own, first_rows, last_rows = inject(arrived, station_embed, tiles.reshape(CELLS, DEPTH))

    north = shifted(last_rows, 1, 0)
    south = shifted(first_rows, -1, 0)
    first_cols, last_cols = widen(north, south, own)
    west = shifted(last_cols, 0, 1)
    east = shifted(first_cols, 0, -1)

    partial, parcel = trunk(
        space_count // TILE_COLS,
        north, south, west, east, own, conv_fine, conv_mid, norm_gains, arrived,
    )
    steps, parcel = lax.optimization_barrier((horizon_step_list.reshape(1, -1), parcel))
    film = lax.psum(film_rows(steps, film_table), "lead")
    returned = lax.all_to_all(
        parcel.reshape(space_count, 2, 3 * DEPTH), "space", 0, 0, tiled=True
    ).reshape(2 * space_count, 3 * DEPTH)

    maps, scores = tail(
        returned, conv_coarse, norm_gains, partial, film, lookup, out_proj, gauge_bin_projector
    )
    return maps.reshape(1, 1, TILE_H, TILE_W, DEPTH), scores.reshape(1, count, -1)


def solution(mesh):
    in_specs = (
        P("space", None, None, None),
        P("space", None),
        P("space", None),
        P("space"),
        P(),
        P(),
        P(),
        P(),
        P(),
        P("lead", None),
        P(),
        P(),
        P(),
    )
    out_specs = (P("lead", "space", None, None, None), P("lead", "space", None))
    return jax.shard_map(body, mesh=mesh, in_specs=in_specs, out_specs=out_specs, check_vma=False)
```

```python
import functools

import jax
import jax.numpy as jnp
from jax import lax
from jax.experimental import pallas as pl
from jax.experimental.pallas import tpu as pltpu
from jax.sharding import PartitionSpec as P

TILE_COLS = 8
TILE_H, TILE_W, DEPTH = 16, 32, 256
CELLS = TILE_H * TILE_W
EPS = 1e-06
FILM_ROWS = 16
HALO = 5
SIDE = 8
FRAME_H, FRAME_W = TILE_H + 2 * HALO, TILE_W + 2 * SIDE
ENC_H = FRAME_H - 2
MID_W = 16
F32 = jnp.float32
BF16 = jnp.bfloat16


def dot(a, b):
    return jnp.dot(a, b, preferred_element_type=F32)


def dot_rows(a, b):
    return lax.dot_general(a, b, (((1,), (1,)), ((), ())), preferred_element_type=F32)


def silu(v):
    return v / (1.0 + jnp.exp(-v))


def rms_scale(values, gain):
    mean_sq = jnp.mean(values * values, axis=-1, keepdims=True)
    return values * lax.rsqrt(mean_sq + EPS) * gain


def column(shape):
    return lax.broadcasted_iota(jnp.int32, shape, 1)


def line(shape):
    return lax.broadcasted_iota(jnp.int32, shape, 0)


def ones_where(condition):
    return condition.astype(F32).astype(BF16)


def grid_place():
    at = lax.axis_index("space")
    return lax.div(at, TILE_COLS), lax.rem(at, TILE_COLS)


def pack_kernel(records, payload, lookup):
    count, readings = records.shape[0], records.shape[1] // 2
    pairs = payload.shape[0]
    obs = records[:, :readings]
    earlier = ones_where(line((count, count)) < column((count, count)))
    sort, lane = line((16, readings)), column((16, readings))
    weights = jnp.where((sort == 1) & (lane == 1), 16.0, 0.0)
    weights = jnp.where((sort == 0) & (lane == 0) | (sort == 1) & (lane == 2), 1.0, weights)
    ids = dot_rows(weights.astype(BF16), records[:, readings:]).astype(jnp.int32)
    dest, pixel = ids[0:1], ids[1:2]
    lane = column((pairs, readings))
    hot = (line((pairs // 2, count)) == dest).astype(F32)
    prior = dot(hot.astype(BF16), earlier)
    position = jnp.sum(prior * hot, axis=0, keepdims=True).astype(jnp.int32)
    key = dest * 2 + (position & 1) + pairs * (position >> 1)
    coarse = dest * 2 + ((pixel & (TILE_W - 1)) >> 4)
    sort = line((16, count))
    found = jnp.where(sort == 0, key >> 4, jnp.where(sort == 1, key & 15, 0))
    found = jnp.where(sort == 2, coarse >> 4, jnp.where(sort == 3, coarse & 15, found))
    lookup[...] = found.astype(F32).astype(BF16)
    places = jnp.zeros((pairs, readings), jnp.int32)
    for half in range(2):
        match = line((pairs, count)) + half * pairs == key
        sent = dot(ones_where(match), obs)
        payload[:, half * readings : (half + 1) * readings] = sent.astype(BF16)
        at = jnp.sum(jnp.where(match, pixel, 0), axis=1, keepdims=True)
        places = jnp.where(lane == 2 * half, at >> 4, places)
        places = jnp.where(lane == 2 * half + 1, at & 15, places)
    payload[:, 2 * readings :] = places.astype(F32).astype(BF16)


def inject_kernel(
    arrived, embed, tiles, own, first_rows, last_rows
):
    pairs = arrived.shape[0]
    readings = embed.shape[0]
    weight = embed[...]
    sort, lane = line((8, readings)), column((8, readings))
    weights = jnp.where(lane == 2 * sort, 16.0, jnp.where(lane == 2 * sort + 1, 1.0, 0.0))
    weights = jnp.where(sort < 2, weights, 0.0).astype(BF16)
    pixels = dot_rows(weights, arrived[:, 2 * readings :]).astype(jnp.int32)
    fine = 0.0
    for half in range(2):
        embedded = dot(arrived[:, half * readings : (half + 1) * readings], weight)
        hot = ones_where(line((CELLS, pairs)) == pixels[half : half + 1])
        fine += dot(hot, embedded.astype(BF16))
    fine = (fine + tiles[...].astype(F32)).reshape(TILE_H, TILE_W, DEPTH)
    own[...] = fine
    first_rows[...] = fine[:HALO].reshape(HALO * TILE_W, DEPTH).astype(BF16)
    last_rows[...] = fine[-HALO:].reshape(HALO * TILE_W, DEPTH).astype(BF16)


def film_kernel(steps, film_table, out):
    table_rows = film_table.shape[0]
    offset = lax.axis_index("lead") * table_rows
    sort = line((8, table_rows))
    at = jnp.full((8, table_rows), -1, jnp.int32)
    for i in range(4):
        at = jnp.where((sort & 3) == i, steps[0:1, i : i + 1] - offset, at)
    both = dot(ones_where(column((8, table_rows)) == at), film_table[...])
    rows = jnp.where(line((8, DEPTH)) < 4, both[:, :DEPTH], both[:, DEPTH:])
    rest = jnp.zeros((FILM_ROWS - 8, DEPTH), F32)
    out[...] = jnp.concatenate([rows, rest], axis=0).astype(BF16)


def widen_kernel(north, south, own, first_cols, last_cols):
    for y in range(FRAME_H):
        for target, cols in (
            (first_cols, slice(0, SIDE)),
            (last_cols, slice(TILE_W - SIDE, TILE_W)),
        ):
            start = y % (HALO + TILE_H) * TILE_W + cols.start
            if y < HALO:
                rows = north[start : start + SIDE].astype(F32)
            elif y < HALO + TILE_H:
                rows = own[y - HALO, cols]
            else:
                rows = south[start : start + SIDE].astype(F32)
            target[y] = rows.astype(BF16)


def trunk_kernel(
    image_rows,
    north, south, west, east, own, conv_fine, conv_mid, gains, arrived,
    partial_ref, parcel,
    frame, taps, enc, mid_in, mid_taps,
):
    row_at, col_at = grid_place()
    above, below = (
        rows[: HALO * TILE_W].astype(F32).reshape(HALO, TILE_W, DEPTH) for rows in (north, south)
    )
    inner = slice(SIDE, SIDE + TILE_W)
    frame[:HALO, inner] = above
    frame[HALO : HALO + TILE_H, inner] = own[...]
    frame[HALO + TILE_H :, inner] = below
    frame[:, :SIDE] = jnp.where(col_at > 0, west[...].astype(F32), 0.0)
    frame[:, SIDE + TILE_W :] = jnp.where(col_at < TILE_COLS - 1, east[...].astype(F32), 0.0)
    gain = gains[0:1].astype(F32)
    for y in range(FRAME_H):
        normed = rms_scale(frame[y], gain)
        rows = slice(y * FRAME_W, (y + 1) * FRAME_W)
        taps[rows, :DEPTH] = pltpu.roll(normed, 1, 0).astype(BF16)
        taps[rows, DEPTH : 2 * DEPTH] = normed.astype(BF16)
        taps[rows, 2 * DEPTH :] = pltpu.roll(normed, FRAME_W - 1, 0).astype(BF16)
    size = ENC_H * FRAME_W
    conv = 0.0
    for dy in range(3):
        conv += dot(taps[dy * FRAME_W : dy * FRAME_W + size], conv_fine[dy])
    done = (frame[1 : 1 + ENC_H].reshape(size, DEPTH) + silu(conv)).astype(BF16)
    enc[...] = done.astype(F32).reshape(ENC_H, FRAME_W, DEPTH)
    group = 4 * FRAME_W
    at = column((MID_W, group))
    x = at - FRAME_W * sum((at >= FRAME_W * i).astype(jnp.int32) for i in range(1, 4))
    pool = ((x >> 2) - 1 == line((MID_W, group))) & (line((MID_W, group)) < 10)
    pool = jnp.where(pool, 1.0 / 16, 0.0).astype(BF16)
    for i in range(ENC_H // 4):
        mid_in[i * MID_W : (i + 1) * MID_W] = dot(pool, done[i * group : (i + 1) * group])

    mid = mid_in[...]
    normed = rms_scale(mid, gains[1:2].astype(F32))
    at = line(mid.shape)
    row = row_at * (TILE_H // 4) - 1 + at // MID_W
    col = col_at * (TILE_W // 4) - 1 + at % MID_W
    inside = (row >= 0) & (row < image_rows * (TILE_H // 4))
    inside = inside & (col >= 0) & (col < TILE_COLS * (TILE_W // 4))
    normed = jnp.where(inside, normed, 0.0)
    mid_taps[:, :DEPTH] = pltpu.roll(normed, 1, 0).astype(BF16)
    mid_taps[:, DEPTH : 2 * DEPTH] = normed.astype(BF16)
    mid_taps[:, 2 * DEPTH :] = pltpu.roll(normed, mid.shape[0] - 1, 0).astype(BF16)
    conv = 0.0
    for dy in range(3):
        conv += dot(mid_taps[dy * MID_W : (dy + 4) * MID_W], conv_mid[dy])
    enc_mid = mid[MID_W : 5 * MID_W] + silu(conv)
    high = enc_mid.astype(BF16)
    low = (enc_mid - high.astype(F32)).astype(BF16)

    shape = (CELLS, 4 * MID_W)
    cell = line(shape)
    spread = (cell >> 7) * MID_W + ((cell & (TILE_W - 1)) >> 2) + 1
    spread = ones_where(column(shape) == spread)
    centre = enc[HALO - 1 : HALO - 1 + TILE_H, SIDE : SIDE + TILE_W]
    partial = centre.reshape(CELLS, DEPTH) + (dot(spread, high) + dot(spread, low))
    partial_ref[...] = partial

    x = column((16, 4 * MID_W)) % MID_W - 1
    pool = (x >= 0) & (x < 8) & ((x >> 2) == line((16, 4 * MID_W)))
    pool = jnp.where(pool, 1.0 / 16, 0.0).astype(BF16)
    coarse = dot(pool, high) + dot(pool, low)
    pairs, readings = arrived.shape[0], arrived.shape[1] // 3
    partial = partial.astype(BF16)
    for half in range(2):
        at = 2 * readings + 2 * half
        pixel = arrived[:, at : at + 1].astype(F32) * 16 + arrived[:, at + 1 : at + 2].astype(F32)
        hot = ones_where(column((pairs, CELLS)) == pixel.astype(jnp.int32))
        parcel[:, half * DEPTH : (half + 1) * DEPTH] = dot(hot, partial).astype(BF16)
    even = line((pairs, DEPTH)) % 2 == 0
    parcel[:, 2 * DEPTH :] = jnp.where(even, coarse[0:1], coarse[1:2]).astype(BF16)


def tail_kernel(
    returned, conv_coarse, gains, partial, film, lookup, out_proj, projector,
    maps_ref, scores_ref,
    taps, maps, scores, sems,
):
    cells, wide = returned.shape[0], TILE_COLS * 2
    coarse = returned[:, 2 * DEPTH :].astype(F32)
    normed = rms_scale(coarse, gains[2:3].astype(F32))
    col = line(coarse.shape) % wide
    taps[:wide] = jnp.zeros((wide, 3 * DEPTH), BF16)
    taps[wide + cells :] = jnp.zeros((wide, 3 * DEPTH), BF16)
    inner = slice(wide, wide + cells)
    left, right = pltpu.roll(normed, 1, 0), pltpu.roll(normed, cells - 1, 0)
    taps[inner, :DEPTH] = jnp.where(col == 0, 0.0, left).astype(BF16)
    taps[inner, DEPTH : 2 * DEPTH] = normed.astype(BF16)
    taps[inner, 2 * DEPTH :] = jnp.where(col == wide - 1, 0.0, right).astype(BF16)
    conv = 0.0
    for dy in range(3):
        conv += dot(taps[dy * wide : dy * wide + cells], conv_coarse[dy])
    context = coarse + silu(conv)
    high = context.astype(BF16)
    low = (context - high.astype(F32)).astype(BF16)

    gain = gains[3:4].astype(F32)
    lead, at = lax.axis_index("lead"), line((FILM_ROWS, DEPTH))
    rows = film[...].astype(F32)
    scale = 1.0 + jnp.sum(jnp.where(at == lead, rows, 0.0), axis=0, keepdims=True)
    shift = jnp.sum(jnp.where(at == lead + 4, rows, 0.0), axis=0, keepdims=True)

    def decode(values):
        hidden = rms_scale(values, gain) * scale + shift
        return (values + dot(silu(hidden).astype(BF16), out_proj[...])).astype(BF16)

    row_at, col_at = grid_place()
    here = row_at * wide + col_at * 2 + ((line((CELLS, cells)) & (TILE_W - 1)) >> 4)
    mine = ones_where(column((CELLS, cells)) == here)
    spread = dot(mine, high) + dot(mine, low)
    maps[...] = decode(partial[...] + spread)
    put_maps = pltpu.make_async_copy(maps, maps_ref, sems.at[0])
    put_maps.start()

    count = lookup.shape[1]
    same = ones_where(line((count, count)) == column((count, count)))
    where = dot_rows(same, lookup[...])
    key = (where[:, 0:1] * 16 + where[:, 1:2]).astype(jnp.int32)
    area = (where[:, 2:3] * 16 + where[:, 3:4]).astype(jnp.int32)
    slot = column((count, cells))
    pick = ones_where(slot == area)
    at_stations = dot(pick, high) + dot(pick, low)
    for half in range(2):
        found = returned[:, half * DEPTH : (half + 1) * DEPTH]
        at_stations += dot(ones_where(slot + half * cells == key), found)
    scores[...] = dot(decode(at_stations), projector[...]).astype(BF16)
    put_scores = pltpu.make_async_copy(scores, scores_ref, sems.at[1])
    put_scores.start()
    put_maps.wait()
    put_scores.wait()


def call(kernel, outs, scratch, operands, hbm_outs=(), megabytes=4):
    vmem = pl.BlockSpec(memory_space=pltpu.VMEM)
    hbm = pl.BlockSpec(memory_space=pltpu.HBM)
    return pl.pallas_call(
        kernel,
        out_shape=[jax.ShapeDtypeStruct(shape, dtype) for shape, dtype in outs],
        in_specs=[vmem] * len(operands),
        out_specs=[hbm if i in hbm_outs else vmem for i in range(len(outs))],
        scratch_shapes=scratch,
        compiler_params=pltpu.CompilerParams(vmem_limit_bytes=megabytes * 2**20),
    )(*operands)


def pack(records, space_count):
    count, width = records.shape
    outs = [((2 * space_count, width // 2 * 3), BF16), ((16, count), BF16)]
    return call(pack_kernel, outs, [], [records], megabytes=8)


def film_rows(steps, film_table):
    return call(film_kernel, [((FILM_ROWS, DEPTH), BF16)], [], [steps, film_table])[0]


def inject(arrived, embed, tiles):
    return call(
        inject_kernel,
        [
            ((TILE_H, TILE_W, DEPTH), F32),
            ((HALO * TILE_W, DEPTH), BF16),
            ((HALO * TILE_W, DEPTH), BF16),
        ],
        [],
        [arrived, embed, tiles],
        megabytes=8,
    )


def widen(north, south, own):
    shape = (FRAME_H, SIDE, DEPTH)
    return call(widen_kernel, [(shape, BF16), (shape, BF16)], [], [north, south, own])


def trunk(image_rows, north, south, west, east, own, conv_fine, conv_mid, gains, arrived):
    return call(
        functools.partial(trunk_kernel, image_rows),
        [((CELLS, DEPTH), F32), ((arrived.shape[0], 3 * DEPTH), BF16)],
        [
            pltpu.VMEM((FRAME_H, FRAME_W, DEPTH), F32),
            pltpu.VMEM((FRAME_H * FRAME_W, 3 * DEPTH), BF16),
            pltpu.VMEM((ENC_H, FRAME_W, DEPTH), F32),
            pltpu.VMEM((ENC_H // 4 * MID_W, DEPTH), F32),
            pltpu.VMEM((ENC_H // 4 * MID_W, 3 * DEPTH), BF16),
        ],
        [
            north, south, west, east, own,
            conv_fine.reshape(3, 3 * DEPTH, DEPTH),
            conv_mid.reshape(3, 3 * DEPTH, DEPTH),
            gains, arrived,
        ],
        megabytes=16,
    )


def tail(returned, conv_coarse, gains, partial, film, lookup, out_proj, projector):
    cells = returned.shape[0]
    outs = [((CELLS, DEPTH), BF16), ((lookup.shape[1], projector.shape[1]), BF16)]
    return call(
        tail_kernel,
        outs,
        [
            pltpu.VMEM((cells + 4 * TILE_COLS, 3 * DEPTH), BF16),
            *[pltpu.VMEM(shape, dtype) for shape, dtype in outs],
            pltpu.SemaphoreType.DMA((2,)),
        ],
        [
            returned, conv_coarse.reshape(3, 3 * DEPTH, DEPTH), gains,
            partial, film, lookup, out_proj, projector,
        ],
        hbm_outs=(0, 1),
        megabytes=16,
    )


def shifted(value, row_step, col_step):
    count = lax.axis_size("space")
    pairs = []
    for source in range(count):
        row, col = source // TILE_COLS + row_step, (source + col_step) % TILE_COLS
        if 0 <= row < count // TILE_COLS:
            pairs.append((source, row * TILE_COLS + col))
    return lax.ppermute(value, "space", pairs)


def body(
    tiles,
    station_obs,
    station_tile,
    station_pixel,
    station_embed,
    conv_fine,
    conv_mid,
    conv_coarse,
    norm_gains,
    film_table,
    horizon_step_list,
    out_proj,
    gauge_bin_projector,
):
    space_count = lax.axis_size("space")
    count, readings = station_obs.shape
    col = column((count, readings))
    ids = jnp.where(col == 2, station_pixel[:, None] & 15, 0)
    ids = jnp.where(col == 1, station_pixel[:, None] >> 4, ids)
    ids = jnp.where(col == 0, station_tile, ids)
    records = jnp.concatenate([station_obs, ids.astype(BF16)], axis=1)
    payload, lookup = pack(records, space_count)
    arrived = lax.all_to_all(
        payload.reshape(space_count, 2, 3 * readings), "space", 0, 0, tiled=True
    ).reshape(2 * space_count, 3 * readings)
    own, first_rows, last_rows = inject(arrived, station_embed, tiles.reshape(CELLS, DEPTH))

    north = shifted(last_rows, 1, 0)
    south = shifted(first_rows, -1, 0)
    first_cols, last_cols = widen(north, south, own)
    west = shifted(last_cols, 0, 1)
    east = shifted(first_cols, 0, -1)

    partial, parcel = trunk(
        space_count // TILE_COLS,
        north, south, west, east, own, conv_fine, conv_mid, norm_gains, arrived,
    )
    steps, parcel = lax.optimization_barrier((horizon_step_list.reshape(1, -1), parcel))
    film = lax.psum(film_rows(steps, film_table), "lead")
    returned = lax.all_to_all(
        parcel.reshape(space_count, 2, 3 * DEPTH), "space", 0, 0, tiled=True
    ).reshape(2 * space_count, 3 * DEPTH)

    maps, scores = tail(
        returned, conv_coarse, norm_gains, partial, film, lookup, out_proj, gauge_bin_projector
    )
    return maps.reshape(1, 1, TILE_H, TILE_W, DEPTH), scores.reshape(1, count, -1)


def solution(mesh):
    in_specs = (
        P("space", None, None, None),
        P("space", None),
        P("space", None),
        P("space"),
        P(),
        P(),
        P(),
        P(),
        P(),
        P("lead", None),
        P(),
        P(),
        P(),
    )
    out_specs = (P("lead", "space", None, None, None), P("lead", "space", None))
    return jax.shard_map(body, mesh=mesh, in_specs=in_specs, out_specs=out_specs, check_vma=False)
```

```python
import functools

import jax
import jax.numpy as jnp
from jax import lax
from jax.experimental import pallas as pl
from jax.experimental.pallas import tpu as pltpu
from jax.sharding import PartitionSpec as P

TILE_COLS = 8
TILE_H, TILE_W, DEPTH = 16, 32, 256
CELLS = TILE_H * TILE_W
EPS = 1e-06
FILM_ROWS = 16
HALO = 5
SIDE = 8
FRAME_H, FRAME_W = TILE_H + 2 * HALO, TILE_W + 2 * SIDE
ENC_H = FRAME_H - 2
MID_W = 16
F32 = jnp.float32
BF16 = jnp.bfloat16


def dot(a, b):
    return jnp.dot(a, b, preferred_element_type=F32)


def dot_rows(a, b):
    return lax.dot_general(a, b, (((1,), (1,)), ((), ())), preferred_element_type=F32)


def silu(v):
    return v / (1.0 + jnp.exp(-v))


def rms_scale(values, gain):
    mean_sq = jnp.mean(values * values, axis=-1, keepdims=True)
    return values * lax.rsqrt(mean_sq + EPS) * gain


def column(shape):
    return lax.broadcasted_iota(jnp.int32, shape, 1)


def line(shape):
    return lax.broadcasted_iota(jnp.int32, shape, 0)


def ones_where(condition):
    return condition.astype(F32).astype(BF16)


def grid_place():
    at = lax.axis_index("space")
    return lax.div(at, TILE_COLS), lax.rem(at, TILE_COLS)


def pack_kernel(records, payload, lookup):
    count, readings = records.shape[0], records.shape[1] // 2
    pairs = payload.shape[0]
    obs = records[:, :readings]
    earlier = ones_where(line((count, count)) < column((count, count)))
    sort, lane = line((16, readings)), column((16, readings))
    weights = jnp.where((sort == 1) & (lane == 1), 16.0, 0.0)
    weights = jnp.where((sort == 0) & (lane == 0) | (sort == 1) & (lane == 2), 1.0, weights)
    ids = dot_rows(weights.astype(BF16), records[:, readings:]).astype(jnp.int32)
    dest, pixel = ids[0:1], ids[1:2]
    lane = column((pairs, readings))
    hot = (line((pairs // 2, count)) == dest).astype(F32)
    prior = dot(hot.astype(BF16), earlier)
    position = jnp.sum(prior * hot, axis=0, keepdims=True).astype(jnp.int32)
    key = dest * 2 + (position & 1) + pairs * (position >> 1)
    coarse = dest * 2 + ((pixel & (TILE_W - 1)) >> 4)
    sort = line((16, count))
    found = jnp.where(sort == 0, key >> 4, jnp.where(sort == 1, key & 15, 0))
    found = jnp.where(sort == 2, coarse >> 4, jnp.where(sort == 3, coarse & 15, found))
    lookup[...] = found.astype(F32).astype(BF16)
    places = jnp.zeros((pairs, readings), jnp.int32)
    for half in range(2):
        match = line((pairs, count)) + half * pairs == key
        sent = dot(ones_where(match), obs)
        payload[:, half * readings : (half + 1) * readings] = sent.astype(BF16)
        at = jnp.sum(jnp.where(match, pixel, 0), axis=1, keepdims=True)
        places = jnp.where(lane == 2 * half, at >> 4, places)
        places = jnp.where(lane == 2 * half + 1, at & 15, places)
    payload[:, 2 * readings :] = places.astype(F32).astype(BF16)


def inject_kernel(
    arrived, embed, tiles, own, first_rows, last_rows
):
    pairs = arrived.shape[0]
    readings = embed.shape[0]
    weight = embed[...]
    sort, lane = line((8, readings)), column((8, readings))
    weights = jnp.where(lane == 2 * sort, 16.0, jnp.where(lane == 2 * sort + 1, 1.0, 0.0))
    weights = jnp.where(sort < 2, weights, 0.0).astype(BF16)
    pixels = dot_rows(weights, arrived[:, 2 * readings :]).astype(jnp.int32)
    fine = 0.0
    for half in range(2):
        embedded = dot(arrived[:, half * readings : (half + 1) * readings], weight)
        hot = ones_where(line((CELLS, pairs)) == pixels[half : half + 1])
        fine += dot(hot, embedded.astype(BF16))
    fine = (fine + tiles[...].astype(F32)).reshape(TILE_H, TILE_W, DEPTH)
    own[...] = fine
    first_rows[...] = fine[:HALO].reshape(HALO * TILE_W, DEPTH).astype(BF16)
    last_rows[...] = fine[-HALO:].reshape(HALO * TILE_W, DEPTH).astype(BF16)


def film_kernel(steps, film_table, out):
    table_rows = film_table.shape[0]
    offset = lax.axis_index("lead") * table_rows
    sort = line((8, table_rows))
    at = jnp.full((8, table_rows), -1, jnp.int32)
    for i in range(4):
        at = jnp.where((sort & 3) == i, steps[0:1, i : i + 1] - offset, at)
    both = dot(ones_where(column((8, table_rows)) == at), film_table[...])
    rows = jnp.where(line((8, DEPTH)) < 4, both[:, :DEPTH], both[:, DEPTH:])
    rest = jnp.zeros((FILM_ROWS - 8, DEPTH), F32)
    out[...] = jnp.concatenate([rows, rest], axis=0).astype(BF16)


def widen_kernel(image_rows, north, south, own, first_cols, last_cols):
    row_at, _ = grid_place()
    for y in range(FRAME_H):
        for target, cols in (
            (first_cols, slice(0, SIDE)),
            (last_cols, slice(TILE_W - SIDE, TILE_W)),
        ):
            start = y % (HALO + TILE_H) * TILE_W + cols.start
            if y < HALO:
                rows = jnp.where(row_at > 0, north[start : start + SIDE].astype(F32), 0.0)
            elif y < HALO + TILE_H:
                rows = own[y - HALO, cols]
            else:
                rows = south[start : start + SIDE].astype(F32)
                rows = jnp.where(row_at < image_rows - 1, rows, 0.0)
            target[y] = rows.astype(BF16)


def trunk_kernel(
    image_rows,
    north, south, west, east, own, conv_fine, conv_mid, gains, arrived,
    partial_ref, parcel,
    frame, taps, enc, mid_in, mid_taps,
):
    row_at, col_at = grid_place()
    above, below = (
        rows[: HALO * TILE_W].astype(F32).reshape(HALO, TILE_W, DEPTH) for rows in (north, south)
    )
    inner = slice(SIDE, SIDE + TILE_W)
    frame[:HALO, inner] = jnp.where(row_at > 0, above, 0.0)
    frame[HALO : HALO + TILE_H, inner] = own[...]
    frame[HALO + TILE_H :, inner] = jnp.where(row_at < image_rows - 1, below, 0.0)
    frame[:, :SIDE] = jnp.where(col_at > 0, west[...].astype(F32), 0.0)
    frame[:, SIDE + TILE_W :] = jnp.where(col_at < TILE_COLS - 1, east[...].astype(F32), 0.0)
    gain = gains[0:1].astype(F32)
    for y in range(FRAME_H):
        normed = rms_scale(frame[y], gain)
        rows = slice(y * FRAME_W, (y + 1) * FRAME_W)
        taps[rows, :DEPTH] = pltpu.roll(normed, 1, 0).astype(BF16)
        taps[rows, DEPTH : 2 * DEPTH] = normed.astype(BF16)
        taps[rows, 2 * DEPTH :] = pltpu.roll(normed, FRAME_W - 1, 0).astype(BF16)
    size = ENC_H * FRAME_W
    conv = 0.0
    for dy in range(3):
        conv += dot(taps[dy * FRAME_W : dy * FRAME_W + size], conv_fine[dy])
    done = (frame[1 : 1 + ENC_H].reshape(size, DEPTH) + silu(conv)).astype(BF16)
    enc[...] = done.astype(F32).reshape(ENC_H, FRAME_W, DEPTH)
    group = 4 * FRAME_W
    at = column((MID_W, group))
    x = at - FRAME_W * sum((at >= FRAME_W * i).astype(jnp.int32) for i in range(1, 4))
    pool = ((x >> 2) - 1 == line((MID_W, group))) & (line((MID_W, group)) < 10)
    pool = jnp.where(pool, 1.0 / 16, 0.0).astype(BF16)
    for i in range(ENC_H // 4):
        mid_in[i * MID_W : (i + 1) * MID_W] = dot(pool, done[i * group : (i + 1) * group])

    mid = mid_in[...]
    normed = rms_scale(mid, gains[1:2].astype(F32))
    at = line(mid.shape)
    row = row_at * (TILE_H // 4) - 1 + at // MID_W
    col = col_at * (TILE_W // 4) - 1 + at % MID_W
    inside = (row >= 0) & (row < image_rows * (TILE_H // 4))
    inside = inside & (col >= 0) & (col < TILE_COLS * (TILE_W // 4))
    normed = jnp.where(inside, normed, 0.0)
    mid_taps[:, :DEPTH] = pltpu.roll(normed, 1, 0).astype(BF16)
    mid_taps[:, DEPTH : 2 * DEPTH] = normed.astype(BF16)
    mid_taps[:, 2 * DEPTH :] = pltpu.roll(normed, mid.shape[0] - 1, 0).astype(BF16)
    conv = 0.0
    for dy in range(3):
        conv += dot(mid_taps[dy * MID_W : (dy + 4) * MID_W], conv_mid[dy])
    enc_mid = mid[MID_W : 5 * MID_W] + silu(conv)
    high = enc_mid.astype(BF16)
    low = (enc_mid - high.astype(F32)).astype(BF16)

    shape = (CELLS, 4 * MID_W)
    cell = line(shape)
    spread = (cell >> 7) * MID_W + ((cell & (TILE_W - 1)) >> 2) + 1
    spread = ones_where(column(shape) == spread)
    centre = enc[HALO - 1 : HALO - 1 + TILE_H, SIDE : SIDE + TILE_W]
    partial = centre.reshape(CELLS, DEPTH) + (dot(spread, high) + dot(spread, low))
    partial_ref[...] = partial

    x = column((16, 4 * MID_W)) % MID_W - 1
    pool = (x >= 0) & (x < 8) & ((x >> 2) == line((16, 4 * MID_W)))
    pool = jnp.where(pool, 1.0 / 16, 0.0).astype(BF16)
    coarse = dot(pool, high) + dot(pool, low)
    pairs, readings = arrived.shape[0], arrived.shape[1] // 3
    partial = partial.astype(BF16)
    for half in range(2):
        at = 2 * readings + 2 * half
        pixel = arrived[:, at : at + 1].astype(F32) * 16 + arrived[:, at + 1 : at + 2].astype(F32)
        hot = ones_where(column((pairs, CELLS)) == pixel.astype(jnp.int32))
        parcel[:, half * DEPTH : (half + 1) * DEPTH] = dot(hot, partial).astype(BF16)
    even = line((pairs, DEPTH)) % 2 == 0
    parcel[:, 2 * DEPTH :] = jnp.where(even, coarse[0:1], coarse[1:2]).astype(BF16)


def tail_kernel(
    returned, conv_coarse, gains, partial, film, lookup, out_proj, projector,
    maps_ref, scores_ref,
    taps, maps, scores, sems,
):
    cells, wide = returned.shape[0], TILE_COLS * 2
    coarse = returned[:, 2 * DEPTH :].astype(F32)
    normed = rms_scale(coarse, gains[2:3].astype(F32))
    col = line(coarse.shape) % wide
    taps[:wide] = jnp.zeros((wide, 3 * DEPTH), BF16)
    taps[wide + cells :] = jnp.zeros((wide, 3 * DEPTH), BF16)
    inner = slice(wide, wide + cells)
    left, right = pltpu.roll(normed, 1, 0), pltpu.roll(normed, cells - 1, 0)
    taps[inner, :DEPTH] = jnp.where(col == 0, 0.0, left).astype(BF16)
    taps[inner, DEPTH : 2 * DEPTH] = normed.astype(BF16)
    taps[inner, 2 * DEPTH :] = jnp.where(col == wide - 1, 0.0, right).astype(BF16)
    conv = 0.0
    for dy in range(3):
        conv += dot(taps[dy * wide : dy * wide + cells], conv_coarse[dy])
    context = coarse + silu(conv)
    high = context.astype(BF16)
    low = (context - high.astype(F32)).astype(BF16)

    gain = gains[3:4].astype(F32)
    lead, at = lax.axis_index("lead"), line((FILM_ROWS, DEPTH))
    rows = film[...].astype(F32)
    scale = 1.0 + jnp.sum(jnp.where(at == lead, rows, 0.0), axis=0, keepdims=True)
    shift = jnp.sum(jnp.where(at == lead + 4, rows, 0.0), axis=0, keepdims=True)

    def decode(values):
        hidden = rms_scale(values, gain) * scale + shift
        return (values + dot(silu(hidden).astype(BF16), out_proj[...])).astype(BF16)

    row_at, col_at = grid_place()
    here = row_at * wide + col_at * 2 + ((line((CELLS, cells)) & (TILE_W - 1)) >> 4)
    mine = ones_where(column((CELLS, cells)) == here)
    spread = dot(mine, high) + dot(mine, low)
    maps[...] = decode(partial[...] + spread)
    put_maps = pltpu.make_async_copy(maps, maps_ref, sems.at[0])
    put_maps.start()

    count = lookup.shape[1]
    same = ones_where(line((count, count)) == column((count, count)))
    where = dot_rows(same, lookup[...])
    key = (where[:, 0:1] * 16 + where[:, 1:2]).astype(jnp.int32)
    area = (where[:, 2:3] * 16 + where[:, 3:4]).astype(jnp.int32)
    slot = column((count, cells))
    pick = ones_where(slot == area)
    at_stations = dot(pick, high) + dot(pick, low)
    for half in range(2):
        found = returned[:, half * DEPTH : (half + 1) * DEPTH]
        at_stations += dot(ones_where(slot + half * cells == key), found)
    scores[...] = dot(decode(at_stations), projector[...]).astype(BF16)
    put_scores = pltpu.make_async_copy(scores, scores_ref, sems.at[1])
    put_scores.start()
    put_maps.wait()
    put_scores.wait()


def call(kernel, outs, scratch, operands, hbm_outs=(), megabytes=4):
    vmem = pl.BlockSpec(memory_space=pltpu.VMEM)
    hbm = pl.BlockSpec(memory_space=pltpu.HBM)
    return pl.pallas_call(
        kernel,
        out_shape=[jax.ShapeDtypeStruct(shape, dtype) for shape, dtype in outs],
        in_specs=[vmem] * len(operands),
        out_specs=[hbm if i in hbm_outs else vmem for i in range(len(outs))],
        scratch_shapes=scratch,
        compiler_params=pltpu.CompilerParams(vmem_limit_bytes=megabytes * 2**20),
    )(*operands)


def pack(records, space_count):
    count, width = records.shape
    outs = [((2 * space_count, width // 2 * 3), BF16), ((16, count), BF16)]
    return call(pack_kernel, outs, [], [records], megabytes=8)


def film_rows(steps, film_table):
    return call(film_kernel, [((FILM_ROWS, DEPTH), BF16)], [], [steps, film_table])[0]


def inject(arrived, embed, tiles):
    return call(
        inject_kernel,
        [
            ((TILE_H, TILE_W, DEPTH), F32),
            ((HALO * TILE_W, DEPTH), BF16),
            ((HALO * TILE_W, DEPTH), BF16),
        ],
        [],
        [arrived, embed, tiles],
        megabytes=8,
    )


def widen(image_rows, north, south, own):
    shape = (FRAME_H, SIDE, DEPTH)
    return call(functools.partial(widen_kernel, image_rows), [(shape, BF16), (shape, BF16)], [], [north, south, own])


def trunk(image_rows, north, south, west, east, own, conv_fine, conv_mid, gains, arrived):
    return call(
        functools.partial(trunk_kernel, image_rows),
        [((CELLS, DEPTH), F32), ((arrived.shape[0], 3 * DEPTH), BF16)],
        [
            pltpu.VMEM((FRAME_H, FRAME_W, DEPTH), F32),
            pltpu.VMEM((FRAME_H * FRAME_W, 3 * DEPTH), BF16),
            pltpu.VMEM((ENC_H, FRAME_W, DEPTH), F32),
            pltpu.VMEM((ENC_H // 4 * MID_W, DEPTH), F32),
            pltpu.VMEM((ENC_H // 4 * MID_W, 3 * DEPTH), BF16),
        ],
        [
            north, south, west, east, own,
            conv_fine.reshape(3, 3 * DEPTH, DEPTH),
            conv_mid.reshape(3, 3 * DEPTH, DEPTH),
            gains, arrived,
        ],
        megabytes=16,
    )


def tail(returned, conv_coarse, gains, partial, film, lookup, out_proj, projector):
    cells = returned.shape[0]
    outs = [((CELLS, DEPTH), BF16), ((lookup.shape[1], projector.shape[1]), BF16)]
    return call(
        tail_kernel,
        outs,
        [
            pltpu.VMEM((cells + 4 * TILE_COLS, 3 * DEPTH), BF16),
            *[pltpu.VMEM(shape, dtype) for shape, dtype in outs],
            pltpu.SemaphoreType.DMA((2,)),
        ],
        [
            returned, conv_coarse.reshape(3, 3 * DEPTH, DEPTH), gains,
            partial, film, lookup, out_proj, projector,
        ],
        hbm_outs=(0, 1),
        megabytes=16,
    )


def shifted(value, row_step, col_step):
    count = lax.axis_size("space")
    pairs = []
    for source in range(count):
        row = (source // TILE_COLS + row_step) % (count // TILE_COLS)
        pairs.append((source, row * TILE_COLS + (source + col_step) % TILE_COLS))
    return lax.ppermute(value, "space", pairs)


def body(
    tiles,
    station_obs,
    station_tile,
    station_pixel,
    station_embed,
    conv_fine,
    conv_mid,
    conv_coarse,
    norm_gains,
    film_table,
    horizon_step_list,
    out_proj,
    gauge_bin_projector,
):
    space_count = lax.axis_size("space")
    count, readings = station_obs.shape
    col = column((count, readings))
    ids = jnp.where(col == 2, station_pixel[:, None] & 15, 0)
    ids = jnp.where(col == 1, station_pixel[:, None] >> 4, ids)
    ids = jnp.where(col == 0, station_tile, ids)
    records = jnp.concatenate([station_obs, ids.astype(BF16)], axis=1)
    payload, lookup = pack(records, space_count)
    arrived = lax.all_to_all(
        payload.reshape(space_count, 2, 3 * readings), "space", 0, 0, tiled=True
    ).reshape(2 * space_count, 3 * readings)
    own, first_rows, last_rows = inject(arrived, station_embed, tiles.reshape(CELLS, DEPTH))

    north = shifted(last_rows, 1, 0)
    south = shifted(first_rows, -1, 0)
    first_cols, last_cols = widen(space_count // TILE_COLS, north, south, own)
    west = shifted(last_cols, 0, 1)
    east = shifted(first_cols, 0, -1)

    partial, parcel = trunk(
        space_count // TILE_COLS,
        north, south, west, east, own, conv_fine, conv_mid, norm_gains, arrived,
    )
    steps, parcel = lax.optimization_barrier((horizon_step_list.reshape(1, -1), parcel))
    film = lax.psum(film_rows(steps, film_table), "lead")
    returned = lax.all_to_all(
        parcel.reshape(space_count, 2, 3 * DEPTH), "space", 0, 0, tiled=True
    ).reshape(2 * space_count, 3 * DEPTH)

    maps, scores = tail(
        returned, conv_coarse, norm_gains, partial, film, lookup, out_proj, gauge_bin_projector
    )
    return maps.reshape(1, 1, TILE_H, TILE_W, DEPTH), scores.reshape(1, count, -1)


def solution(mesh):
    in_specs = (
        P("space", None, None, None),
        P("space", None),
        P("space", None),
        P("space"),
        P(),
        P(),
        P(),
        P(),
        P(),
        P("lead", None),
        P(),
        P(),
        P(),
    )
    out_specs = (P("lead", "space", None, None, None), P("lead", "space", None))
    return jax.shard_map(body, mesh=mesh, in_specs=in_specs, out_specs=out_specs, check_vma=False)
```
